512 devices in a mesh: seq: 32 (over x, z_lo, core), head: 16 (over y, z_hi).
Axes of the slice: x: 4, y: 4, z: 16 (z_hi: 4, z_lo: 4; z = z_hi * 4 + z_lo), core: 2. Of those that a mesh axis runs over, the one named last changes fastest.
Arguments:
- features: bfloat16 [65536, 4096], P(('seq', 'head')), may hold values from -6 to 6
- dt_raw: bfloat16 [65536, 64], P(('seq', 'head')), may hold values from -3 to 3
- b_proj: bfloat16 [65536, 512], P(('seq', 'head')), may hold values from -2 to 2
- c_proj: bfloat16 [65536, 512], P(('seq', 'head')), may hold values from -2 to 2
- cotangent: bfloat16 [65536, 4096], P(('seq', 'head')), may hold values from -6 to 6
- starts: int32 [65536], P('seq'), may hold values from 0 to 1, as said below
- a_log: float32 [64], P('head'), may hold values from -14 to 0
- dt_bias: float32 [64], P('head'), may hold values from -6 to -1
- d_skip: float32 [64], P('head'), may hold values from 0.5 to 1.5
Outputs:
- mixed_out: bfloat16 [65536, 4096], P(('seq', 'head'))
- grad_features: bfloat16 [65536, 4096], P(('seq', 'head'))
- grad_dt: bfloat16 [65536, 64], P(('seq', 'head'))
- grad_b: bfloat16 [65536, 512], P(('seq', 'head'))
- grad_c: bfloat16 [65536, 512], P(('seq', 'head'))
The draws below stay inside these ranges and needn't reach their ends.
Inputs may be any that keep to these rules, and one draw needn't show every extreme that they name: `starts`: 1 marks the first token of a document, 0 any other token; the window's first token is always 1.
All inputs are finite; a program needn't handle non-finite values.
Results may differ from the reference program's by a relative error of at most 0.0022.
Values may be sent and summed in bfloat16 or wider, within the bound.
No kernel may reach another device: no remote copies, remote signals or barrier semaphores. Data moves between devices by JAX's collectives and lax.ppermute only.
A program may use at most 128 MiB of HBM per device.

```python
import jax
import jax.numpy as jnp
from jax import lax

HEADS = 64
GROUPS = 4
HEADDIM = 64
STATE = 128
SPAN = 256
TOKENS = 65536


def head_speeds(key, slow_share):
    first, second, third = jax.random.split(key, 3)
    picked = jax.random.uniform(first, (HEADS,))
    spread = jax.random.uniform(second, (HEADS,))
    wobble = jax.random.uniform(third, (HEADS,), minval=-0.5, maxval=0.5)
    slow_heads = picked < slow_share
    fast_rate = jnp.exp(jnp.log(1.0 / 50.0) + spread * (jnp.log(1.0 / 30.0) - jnp.log(1.0 / 50.0)))
    slow_rate = (0.2 + 0.8 * spread) * 2.3 / TOKENS
    rate = jnp.where(slow_heads, slow_rate, fast_rate)
    slow_base = jnp.maximum(0.01 * jnp.exp(wobble), 2.0 * slow_rate)
    step_base = jnp.where(slow_heads, slow_base, 0.1 * jnp.exp(wobble))
    return (rate, step_base)


def draw_a_log(key, part):
    share = 0.5
    rate, step_base = head_speeds(key, share)
    return jnp.log(rate / step_base).astype(jnp.float32)


def draw_dt_bias(key, part):
    share = 0.5
    rate, step_base = head_speeds(key, share)
    return jnp.log(jnp.expm1(step_base)).astype(jnp.float32)


def draw_starts(key, part):
    key = jax.random.fold_in(key, 7)
    places = jax.random.randint(key, (3,), 1, TOKENS)
    spots = jnp.arange(TOKENS)
    marked = jnp.any(spots[:, None] == places[None, :], axis=1) | (spots == 0)
    return marked.astype(jnp.int32)


def level_of(rng, shape, cuts, smallest, top_value):
    loudness, own = 1.0, jax.random.fold_in(rng, 6)
    for position, blocks in cuts:
        heights = jnp.exp(jax.random.uniform(jax.random.fold_in(own, position), (blocks,), jnp.float32, smallest / len(cuts), top_value / len(cuts)))
        loudness = loudness * jnp.repeat(heights, shape[position] // blocks).reshape([-1 if axis == position else 1 for axis in range(len(shape))])
    return loudness


def noise(rng, shape, scale, most, cuts=(), held_as=jnp.bfloat16):
    result = scale * jax.random.normal(rng, shape, jnp.float32)
    if cuts:
        result = result * level_of(rng, shape, cuts, -0.22, 0.18)
    return jnp.clip(result, -most, most).astype(held_as)


def setup_inputs(seed: int = 0) -> dict:
    streams_of = jax.random.split(jax.random.key(seed), 10)
    features = noise(streams_of[0], (TOKENS, HEADS * HEADDIM), 1.0, 6.0, ((0, 512),))
    dt_raw = noise(streams_of[1], (TOKENS, HEADS), 0.5, 3.0, ((0, 512),))
    b_proj = noise(streams_of[2], (TOKENS, GROUPS * STATE), 0.3, 2.0, ((0, 512),))
    c_proj = noise(streams_of[3], (TOKENS, GROUPS * STATE), 0.3, 2.0, ((0, 512),))
    cotangent = noise(streams_of[4], (TOKENS, HEADS * HEADDIM), 1.0, 6.0, ((0, 512),))
    starts = draw_starts(jax.random.fold_in(streams_of[9], 71), 0)
    a_log = draw_a_log(jax.random.fold_in(streams_of[9], 71), 0)
    dt_bias = draw_dt_bias(jax.random.fold_in(streams_of[9], 71), 0)
    d_skip = jnp.clip(0.5 + 1.0 * jax.random.uniform(streams_of[8], (HEADS,), jnp.float32) ** level_of(streams_of[8], (HEADS,), ((0, 16),), -0.2, 0.2), 0.5, 1.5)
    return dict(features=features, dt_raw=dt_raw, b_proj=b_proj, c_proj=c_proj, cotangent=cotangent, starts=starts, a_log=a_log, dt_bias=dt_bias, d_skip=d_skip)


PRECISE = lax.Precision.HIGHEST

def span_step(state, pieces):
    scaled, running, b_vals, c_vals, doc_count = pieces
    length = doc_count.shape[0]
    places = jnp.arange(length)
    same_doc = (doc_count[:, None] == doc_count[None, :]) & (places[:, None] >= places[None, :])
    scores = jnp.einsum('tgn,sgn->gts', c_vals, b_vals, precision=PRECISE)
    run_heads = jnp.transpose(running, (1, 2, 0))
    spread = run_heads[:, :, :, None] - run_heads[:, :, None, :]
    decay = jnp.exp(jnp.where(same_doc[None, None], spread, -1e+30))
    weights = scores[:, None] * decay
    inner = jnp.einsum('gkts,sgkp->tgkp', weights, scaled, precision=PRECISE)
    reach = jnp.exp(running) * (doc_count == 0)[:, None, None]
    carried = jnp.einsum('tgn,gkpn->tgkp', c_vals, state, precision=PRECISE) * reach[..., None]
    last_doc = doc_count[-1]
    tail = jnp.exp(running[-1][None] - running) * (doc_count == last_doc)[:, None, None]
    keep = jnp.exp(running[-1]) * (last_doc == 0)
    added = jnp.einsum('sgkp,sgn->gkpn', scaled * tail[..., None], b_vals, precision=PRECISE)
    return (keep[..., None, None] * state + added, inner + carried)

def reference(features, dt_raw, b_proj, c_proj, cotangent, starts, a_log, dt_bias, d_skip):
    total = features.shape[0]
    blocks = total // SPAN
    per_group = HEADS // GROUPS
    doc_count = jnp.cumsum(starts.reshape(blocks, SPAN), axis=1).astype(jnp.int32)
    decay_head = -jnp.exp(a_log)

    def forward(feat, rates, b_vals, c_vals):
        sizes = jax.nn.softplus(rates + dt_bias)
        log_rate = sizes * decay_head
        feat_four = feat.reshape(total, GROUPS, per_group, HEADDIM)
        scaled = feat_four * sizes.reshape(total, GROUPS, per_group)[..., None]
        running = jnp.cumsum(log_rate.reshape(blocks, SPAN, GROUPS, per_group), axis=1)
        start_state = jnp.zeros((GROUPS, per_group, HEADDIM, STATE), jnp.float32)
        pieces = (scaled.reshape(blocks, SPAN, GROUPS, per_group, HEADDIM), running, b_vals.reshape(blocks, SPAN, GROUPS, STATE), c_vals.reshape(blocks, SPAN, GROUPS, STATE), doc_count)
        _, outputs = lax.scan(jax.checkpoint(span_step), start_state, pieces)
        skipped = feat_four * d_skip.reshape(GROUPS, per_group)[..., None]
        return (outputs.reshape(total, GROUPS, per_group, HEADDIM) + skipped).reshape(total, HEADS * HEADDIM)
    mixed, pull_back = jax.vjp(forward, features.astype(jnp.float32), dt_raw.astype(jnp.float32), b_proj.astype(jnp.float32), c_proj.astype(jnp.float32))
    grads = pull_back(cotangent.astype(jnp.float32))
    return (mixed.astype(jnp.bfloat16), grads[0].astype(jnp.bfloat16), grads[1].astype(jnp.bfloat16), grads[2].astype(jnp.bfloat16), grads[3].astype(jnp.bfloat16))
```

```python
import functools

import jax
import jax.numpy as jnp
from jax import lax
from jax.experimental import pallas as pl
from jax.experimental.pallas import tpu as pltpu
from jax.sharding import PartitionSpec as P

GROUPS = 4
HEADDIM = 64
STATE = 128
ROWS = STATE + 8
TOP = 13.0
CUT = -65000.0
F32 = jnp.float32
BF16 = jnp.bfloat16
PRECISE = lax.Precision.HIGHEST
PARAMS = pltpu.CompilerParams(vmem_limit_bytes=40 * 1024 * 1024)


def iota(shape, axis):
    return lax.broadcasted_iota(jnp.int32, shape, axis)


def split(value):
    high = value.astype(BF16)
    return high, (value - high.astype(F32)).astype(BF16)


def dot(a, b, dims=((1,), (0,)), precision=None):
    return lax.dot_general(a, b, (dims, ((), ())), precision=precision, preferred_element_type=F32)


def spread_map(heads, dtype):
    shape = (heads, heads * HEADDIM)
    return (iota(shape, 0) == iota(shape, 1) // HEADDIM).astype(dtype)


def widen(value):
    both = jnp.concatenate(split(value), axis=1)
    spread = spread_map(value.shape[1], BF16)
    return dot(both, jnp.concatenate([spread, spread], axis=0))


def head_sums(value):
    heads = value.shape[1] // HEADDIM
    shape = (heads * HEADDIM, heads)
    fold = (iota(shape, 0) // HEADDIM == iota(shape, 1)).astype(BF16)
    high, low = split(value)
    return dot(high, fold) + dot(low, fold)


def exponent_of(block):
    top = jnp.max(jnp.max(jnp.abs(block), axis=0, keepdims=True), axis=1, keepdims=True)
    return jnp.clip(jnp.floor(jnp.log(jnp.maximum(top, 1e-30)) * 1.4426950408889634), -90.0, 40.0)


def prep_kernel(dt_ref, par_ref, st_ref, size_ref, sig_ref, run_ref, runt_ref, reach_ref, tail_ref, bias_ref, edge_ref):
    tokens, heads = dt_ref.shape
    per = heads // GROUPS
    par = par_ref[...]
    a_log, dt_bias = par[0:1], par[1:2]
    decay = -jnp.exp(a_log)
    value = dt_ref[...].astype(F32) + dt_bias
    sizes = jnp.maximum(value, 0.0) + jnp.log1p(jnp.exp(-jnp.abs(value)))
    sigmoid = 1.0 / (1.0 + jnp.exp(-value))
    shape = (tokens, tokens)
    lower = (iota(shape, 0) >= iota(shape, 1)).astype(F32)
    upper = (iota(shape, 0) <= iota(shape, 1)).astype(F32)
    running = dot(lower, sizes * decay, precision=PRECISE)
    marks = st_ref[...]
    doc_row = dot(marks, upper)[0:1]
    doc_col = dot(lower, marks, ((1,), (1,)))[:, 0:1]
    doc_last = doc_row[:, tokens - 1 :]
    last = running[tokens - 1 :]
    reach = jnp.where(doc_col == 0.0, jnp.exp(running), 0.0)
    tail = jnp.where(doc_col == doc_last, jnp.exp(last - running), 0.0) * sizes
    linked = (doc_col == doc_row) & (iota(shape, 0) >= iota(shape, 1))
    bias_ref[...] = jnp.where(linked, 0.0, -1e30)
    turned = (running - jnp.log(sizes)).T
    through = jnp.where(doc_last == 0.0, last * 128.0, CUT)
    high = through.astype(BF16).astype(F32)
    mid = (through - high).astype(BF16).astype(F32)
    low = (through - high - mid).astype(BF16).astype(F32)
    keep = jnp.exp((high + mid + low) * (1.0 / 128.0))
    edge = jnp.concatenate([high, mid, low, jnp.zeros_like(keep), keep, decay, decay, decay], axis=0)
    for g in range(GROUPS):
        mine = slice(g * per, (g + 1) * per)
        size_ref[g] = sizes[:, mine]
        sig_ref[g] = sigmoid[:, mine]
        run_ref[g] = running[:, mine]
        runt_ref[g] = turned[mine]
        reach_ref[g] = reach[:, mine]
        tail_ref[g] = tail[:, mine]
        edge_ref[g] = edge[:, mine]


def prep(dt_raw, params, marks):
    tokens, heads = dt_raw.shape
    per = heads // GROUPS
    token_head = jax.ShapeDtypeStruct((GROUPS, tokens, per), F32)
    return pl.pallas_call(
        prep_kernel,
        out_shape=[
            token_head,
            token_head,
            token_head,
            jax.ShapeDtypeStruct((GROUPS, per, tokens), F32),
            token_head,
            token_head,
            jax.ShapeDtypeStruct((tokens, tokens), F32),
            jax.ShapeDtypeStruct((GROUPS, 8, per), F32),
        ],
        compiler_params=PARAMS,
        name="prep",
    )(dt_raw, params, marks)


def state_kernel(val_ref, proj_ref, scale_ref, edge_ref, out_ref):
    wide = widen(scale_ref[0])
    high, low = split(val_ref[...].astype(F32) * wide)
    proj = proj_ref[...]
    state = dot(jnp.concatenate([proj, proj], axis=0), jnp.concatenate([high, low], axis=0), ((0,), (0,)))
    pieces = dot(edge_ref[0].astype(BF16), spread_map(scale_ref.shape[2], BF16))
    chunks, _, width = out_ref.shape
    row = iota((8, width), 0)
    for j in range(chunks):
        mine = slice(j * width, (j + 1) * width)
        block = state[:, mine]
        power = exponent_of(block)
        out_ref[j, 0:STATE] = block * jnp.exp2(TOP - power)
        aux = jnp.where(row == 3, jnp.broadcast_to(power, row.shape), pieces[:, mine])
        out_ref[j, STATE:ROWS] = jnp.where(row < 4, aux, 0.0)


def states(values, proj, scale, edge, parts):
    tokens, channels = values.shape
    chunks = parts // GROUPS
    wide = channels // GROUPS
    per = scale.shape[2]
    return pl.pallas_call(
        state_kernel,
        grid=(GROUPS,),
        in_specs=[
            pl.BlockSpec((tokens, wide), lambda g: (0, g)),
            pl.BlockSpec((tokens, STATE), lambda g: (0, g)),
            pl.BlockSpec((1, tokens, per), lambda g: (g, 0, 0)),
            pl.BlockSpec((1, 8, per), lambda g: (g, 0, 0)),
        ],
        out_specs=pl.BlockSpec((chunks, ROWS, wide // chunks), lambda g: (g, 0, 0)),
        out_shape=jax.ShapeDtypeStruct((parts, ROWS, channels // parts), F32),
        compiler_params=PARAMS,
        cost_estimate=pl.CostEstimate(flops=2 * 2 * tokens * STATE * channels, bytes_accessed=3500000, transcendentals=0),
        name="states",
    )(values, proj, scale, edge)


def keep_row(block):
    return jnp.exp((block[STATE : STATE + 1] + block[STATE + 1 : STATE + 2] + block[STATE + 2 : STATE + 3]) * (1.0 / 128.0))


def unscaled(block):
    return block[0:STATE] * jnp.exp2(block[STATE + 3 : STATE + 4] - TOP)


def total_kernel(reverse, pay_ref, out_ref):
    parts, _, width = pay_ref.shape
    total = jnp.zeros((STATE, width), F32)
    through = jnp.ones((1, width), F32)
    for i in reversed(range(parts)) if reverse else range(parts):
        block = pay_ref[i]
        keep = keep_row(block)
        total = keep * total + unscaled(block)
        through = through * keep
    out_ref[0:STATE] = total
    out_ref[STATE:ROWS] = jnp.broadcast_to(through, (8, width))


def totals(pay, reverse):
    _, _, width = pay.shape
    return pl.pallas_call(
        functools.partial(total_kernel, reverse),
        out_shape=jax.ShapeDtypeStruct((ROWS, width), F32),
        compiler_params=PARAMS,
        cost_estimate=pl.CostEstimate(flops=2 * pay.size, bytes_accessed=4 * pay.size, transcendentals=0),
        name="totals",
    )(pay)


def enter_kernel(reverse, pay_ref, carry_ref, out_ref):
    parts, _, width = pay_ref.shape
    state = carry_ref[0:STATE]
    row = iota((8, width), 0)
    for i in reversed(range(parts)) if reverse else range(parts):
        power = exponent_of(state)
        out_ref[i, 0:STATE] = state * jnp.exp2(TOP - power)
        out_ref[i, STATE:ROWS] = jnp.where(row == 3, jnp.broadcast_to(power, row.shape), 0.0)
        block = pay_ref[i]
        state = keep_row(block) * state + unscaled(block)


def entering(pay, carry, reverse):
    return pl.pallas_call(
        functools.partial(enter_kernel, reverse),
        out_shape=jax.ShapeDtypeStruct(pay.shape, F32),
        compiler_params=PARAMS,
        cost_estimate=pl.CostEstimate(flops=4 * pay.size, bytes_accessed=8 * pay.size, transcendentals=0),
        name="entering",
    )(pay, carry)


def carried_in(total, reverse):
    count = lax.axis_size("far")

    def moved(value, by):
        if reverse:
            pairs = [(s, s - by) for s in range(by, count)]
        else:
            pairs = [(s, s + by) for s in range(count - by)]
        return lax.ppermute(value, "far", pairs)

    def joined(near, far):
        state = near[0:STATE] + near[STATE : STATE + 1] * far[0:STATE]
        return jnp.concatenate([state, near[STATE:] * far[STATE:]], axis=0)

    near = functools.reduce(joined, [moved(total, by) for by in (1, 2, 3, 4)])
    reach = 4
    while reach < count:
        steps = [by for by in (reach, 2 * reach, 3 * reach) if by < count]
        near = functools.reduce(joined, [near] + [moved(near, by) for by in steps])
        reach *= 4
    return near


def inner_kernel(x_ref, w_ref, b_ref, c_ref, run_ref, runt_ref, bias_ref, skip_ref, y_ref, gx_ref, gb_ref, gc_ref, col_ref, diff_ref):
    tokens, wide = x_ref.shape
    heads = wide // HEADDIM
    pair = 2 * HEADDIM
    b_vals, c_vals = b_ref[...], c_ref[...]
    scores = dot(c_vals, b_vals, ((1,), (1,)))
    bias = bias_ref[...]
    run, runt = run_ref[0], runt_ref[0]
    first = iota((tokens, pair), 1) < HEADDIM
    grad_scores = jnp.zeros((tokens, tokens), F32)
    y_all, u_all = [], []
    for k in range(0, heads, 2):
        mine = slice(k * HEADDIM, (k + 2) * HEADDIM)
        x_pair, w_pair = x_ref[:, mine], w_ref[:, mine]
        x_two = jnp.concatenate([x_pair, x_pair], axis=0)
        w_two = jnp.concatenate([w_pair, w_pair], axis=0)
        ys, us = [], []
        for which in range(2):
            h = k + which
            keep = first if which == 0 else ~first
            weight = jnp.exp(run[:, h : h + 1] - runt[h : h + 1, :] + bias)
            cross = dot(jnp.where(keep, w_pair, jnp.zeros_like(w_pair)), x_pair, ((1,), (1,)))
            grad_scores = grad_scores + weight * cross
            high, low = split(weight * scores)
            ys.append(dot(jnp.concatenate([high, low], axis=1), x_two))
            us.append(dot(jnp.concatenate([high, low], axis=0), w_two, ((0,), (0,))))
        y_all.append(jnp.where(first, ys[0], ys[1]))
        u_all.append(jnp.where(first, us[0], us[1]))
    y_in = jnp.concatenate(y_all, axis=1)
    u_in = jnp.concatenate(u_all, axis=1)
    x_vals, w_vals = x_ref[...].astype(F32), w_ref[...].astype(F32)
    skip = skip_ref[0:1]
    y_ref[...] = y_in + skip * x_vals
    gx_ref[...] = u_in + skip * w_vals
    high, low = split(grad_scores)
    gc_ref[...] = dot(jnp.concatenate([high, low], axis=1), jnp.concatenate([b_vals, b_vals], axis=0))
    gb_ref[...] = dot(jnp.concatenate([high, low], axis=0), jnp.concatenate([c_vals, c_vals], axis=0), ((0,), (0,)))
    col = head_sums(x_vals * u_in)
    col_ref[0] = col
    diff_ref[0] = head_sums(w_vals * y_in) - col


def inner(x, w, b, c, run, runt, bias, skip):
    tokens, channels = x.shape
    wide = channels // GROUPS
    per = run.shape[2]
    values = pl.BlockSpec((tokens, wide), lambda g: (0, g))
    proj = pl.BlockSpec((tokens, STATE), lambda g: (0, g))
    small = pl.BlockSpec((1, tokens, per), lambda g: (g, 0, 0))
    return pl.pallas_call(
        inner_kernel,
        grid=(GROUPS,),
        in_specs=[
            values,
            values,
            proj,
            proj,
            small,
            pl.BlockSpec((1, per, tokens), lambda g: (g, 0, 0)),
            pl.BlockSpec((tokens, tokens), lambda g: (0, 0)),
            pl.BlockSpec((8, wide), lambda g: (0, g)),
        ],
        out_specs=[values, values, proj, proj, small, small],
        out_shape=[
            jax.ShapeDtypeStruct((tokens, channels), F32),
            jax.ShapeDtypeStruct((tokens, channels), F32),
            jax.ShapeDtypeStruct((tokens, GROUPS * STATE), F32),
            jax.ShapeDtypeStruct((tokens, GROUPS * STATE), F32),
            jax.ShapeDtypeStruct((GROUPS, tokens, per), F32),
            jax.ShapeDtypeStruct((GROUPS, tokens, per), F32),
        ],
        compiler_params=PARAMS,
        cost_estimate=pl.CostEstimate(flops=20_000_000_000, bytes_accessed=8_000_000, transcendentals=tokens * tokens * 64),
        name="inner",
    )(x, w, b, c, run, runt, bias, skip)


def carried_terms(pay_ref, val_ref, other_ref, scale_ref, proj_ref):
    chunks = pay_ref.shape[0]
    wide = widen(scale_ref[0])
    proj = proj_ref[...]
    blocks = [pay_ref[j] for j in range(chunks)]
    state = jnp.concatenate([block[0:STATE] for block in blocks], axis=1)
    factor = jnp.exp2(jnp.concatenate([block[STATE + 3 : STATE + 4] for block in blocks], axis=1) - TOP)
    high, low = split(state)
    wide = wide * factor
    terms = dot(jnp.concatenate([proj, proj], axis=1), jnp.concatenate([high, low], axis=0)) * wide
    left_high, left_low = split(val_ref[...].astype(F32) * wide)
    last = ((1,), (1,))
    grad = dot(left_high, high, last) + (dot(left_high, low, last) + dot(left_low, high, last))
    return terms, grad, head_sums(terms * other_ref[...].astype(F32))


def forward_kernel(pay_ref, w_ref, c_ref, reach_ref, y_ref, gc_ref, mixed_ref, grad_ref, row_ref):
    terms, grad, rows = carried_terms(pay_ref, w_ref, w_ref, reach_ref, c_ref)
    mixed_ref[...] = (y_ref[...] + terms).astype(BF16)
    grad_ref[...] = (gc_ref[...] + grad).astype(BF16)
    row_ref[0] = rows


def forward(pay, w, c, reach, y, gc):
    tokens, channels = w.shape
    parts, _, width = pay.shape
    wide = channels // GROUPS
    per = reach.shape[2]
    values = pl.BlockSpec((tokens, wide), lambda g: (0, g))
    proj = pl.BlockSpec((tokens, STATE), lambda g: (0, g))
    small = pl.BlockSpec((1, tokens, per), lambda g: (g, 0, 0))
    return pl.pallas_call(
        forward_kernel,
        grid=(GROUPS,),
        in_specs=[
            pl.BlockSpec((parts // GROUPS, ROWS, width), lambda g: (g, 0, 0)),
            values,
            proj,
            small,
            values,
            proj,
        ],
        out_specs=[values, proj, small],
        out_shape=[
            jax.ShapeDtypeStruct((tokens, channels), BF16),
            jax.ShapeDtypeStruct((tokens, GROUPS * STATE), BF16),
            jax.ShapeDtypeStruct((GROUPS, tokens, per), F32),
        ],
        compiler_params=PARAMS,
        cost_estimate=pl.CostEstimate(flops=5 * 2 * tokens * STATE * channels, bytes_accessed=7_000_000, transcendentals=0),
        name="forward",
    )(pay, w, c, reach, y, gc)


def backward_kernel(
    pay_ref, enter_ref, x_ref, b_ref, tail_ref, gx_ref, gb_ref, col_ref, diff_ref, row_ref, size_ref, sig_ref, edge_ref,
    gradx_ref, grad_ref, dt_ref, all_ref,
):
    g = pl.program_id(0)
    tokens, _ = x_ref.shape
    chunks, _, width = pay_ref.shape
    per = tail_ref.shape[2]
    terms, grad, cols = carried_terms(pay_ref, x_ref, x_ref, tail_ref, b_ref)
    gradx_ref[...] = (gx_ref[...] + terms).astype(BF16)
    grad_ref[...] = (gb_ref[...] + grad).astype(BF16)
    met = []
    for j in range(chunks):
        leave, enter = pay_ref[j], enter_ref[j]
        factor = jnp.exp2(leave[STATE + 3 : STATE + 4] - TOP) * jnp.exp2(enter[STATE + 3 : STATE + 4] - TOP)
        met.append(jnp.sum(leave[0:STATE] * enter[0:STATE], axis=0, keepdims=True) * factor)
    met = head_sums(jnp.broadcast_to(jnp.concatenate(met, axis=1), (8, chunks * width)))[0:1]
    edge = edge_ref[0]
    keep, decay = edge[4:5], edge[5:6]
    shape = (tokens, tokens)
    from_here = (iota(shape, 0) <= iota(shape, 1)).astype(F32)
    before = (iota(shape, 0) > iota(shape, 1)).astype(F32)
    grad_rate = (
        dot(from_here, diff_ref[0] + row_ref[0], precision=PRECISE)
        + dot(before, cols, precision=PRECISE)
        + keep * met
    )
    grad_size = (col_ref[0] + cols) / size_ref[0] + decay * grad_rate
    place = (iota((per, GROUPS * per), 0) + g * per == iota((per, GROUPS * per), 1)).astype(F32)
    placed = dot(grad_size * sig_ref[0], place, precision=PRECISE)

    @pl.when(g == 0)
    def _():
        all_ref[...] = placed

    @pl.when(g > 0)
    def _():
        all_ref[...] += placed

    dt_ref[...] = all_ref[...].astype(BF16)


def backward(pay, enter, x, b, tail, gx, gb, col, diff, row, size, sig, edge):
    tokens, channels = x.shape
    parts, _, width = pay.shape
    wide = channels // GROUPS
    per = tail.shape[2]
    chunk = pl.BlockSpec((parts // GROUPS, ROWS, width), lambda g: (g, 0, 0))
    values = pl.BlockSpec((tokens, wide), lambda g: (0, g))
    proj = pl.BlockSpec((tokens, STATE), lambda g: (0, g))
    small = pl.BlockSpec((1, tokens, per), lambda g: (g, 0, 0))
    return pl.pallas_call(
        backward_kernel,
        grid=(GROUPS,),
        in_specs=[
            chunk, chunk, values, proj, small, values, proj, small, small, small, small, small,
            pl.BlockSpec((1, 8, per), lambda g: (g, 0, 0)),
        ],
        out_specs=[values, proj, pl.BlockSpec((tokens, GROUPS * per), lambda g: (0, 0))],
        out_shape=[
            jax.ShapeDtypeStruct((tokens, channels), BF16),
            jax.ShapeDtypeStruct((tokens, GROUPS * STATE), BF16),
            jax.ShapeDtypeStruct((tokens, GROUPS * per), BF16),
        ],
        scratch_shapes=[pltpu.VMEM((tokens, GROUPS * per), F32)],
        compiler_params=PARAMS,
        cost_estimate=pl.CostEstimate(flops=5 * 2 * tokens * STATE * channels, bytes_accessed=9_000_000, transcendentals=0),
        name="backward",
    )(pay, enter, x, b, tail, gx, gb, col, diff, row, size, sig, edge)


GROUP = ("near", "head")


def exchanged(*values):
    sent = jnp.concatenate([value.astype(jnp.float16) for value in values], axis=1)
    sent = lax.all_to_all(sent, GROUP, split_axis=0, concat_axis=0, tiled=True)
    return [sent[:, k * ROWS : (k + 1) * ROWS].astype(F32) for k in range(len(values))]


def gathered(own, heads):
    parts = lax.axis_size("head")
    per_dev = own.shape[1]
    mine = lax.axis_index("head")
    whole = jnp.where(iota((8, 128), 1) // per_dev == mine, jnp.tile(own, (1, 128 // per_dev)), 0.0)
    whole = jnp.broadcast_to(whole[None], (parts, 8, 128))
    return lax.all_to_all(whole, "head", split_axis=0, concat_axis=0, tiled=True).sum(axis=0)[:, :heads]


def per_device(features, dt_raw, b_proj, c_proj, cotangent, starts, a_log, dt_bias, d_skip):
    parts = lax.axis_size(GROUP)
    tokens, heads = dt_raw.shape
    params = gathered(jnp.stack([a_log, dt_bias, d_skip] + [d_skip] * 5), heads)
    marks = lax.dynamic_slice(starts, (lax.axis_index("head") * tokens,), (tokens,)).astype(F32)
    marks = jnp.broadcast_to(marks[None], (8, tokens))
    skip = jnp.broadcast_to(jnp.repeat(params[2], HEADDIM)[None], (8, heads * HEADDIM))
    size, sig, run, runt, reach, tail, bias, edge = prep(dt_raw, params, marks)
    leave, back = exchanged(
        states(features, b_proj, tail, edge, parts), states(cotangent, c_proj, reach, edge, parts)
    )
    y, gx, gb, gc, col, diff = inner(features, cotangent, b_proj, c_proj, run, runt, bias, skip)
    enter, after = exchanged(
        entering(leave, carried_in(totals(leave, False), False), False),
        entering(back, carried_in(totals(back, True), True), True),
    )
    mixed, grad_c, row = forward(enter, cotangent, c_proj, reach, y, gc)
    grad_x, grad_b, grad_dt = backward(
        after, enter, features, b_proj, tail, gx, gb, col, diff, row, size, sig, edge
    )
    return mixed, grad_x, grad_dt, grad_b, grad_c


def solution(mesh):
    devices = mesh.devices
    seq, parts = devices.shape
    fine = jax.sharding.Mesh(devices.reshape(seq // 2, 2, parts), ("far",) + GROUP)
    token = P(("far",) + GROUP, None)
    return jax.shard_map(
        per_device,
        mesh=fine,
        in_specs=(token, token, token, token, token, P(("far", "near")), P("head"), P("head"), P("head")),
        out_specs=(token, token, token, token, token),
        check_vma=False,
    )
```

```python
import functools

import jax
import jax.numpy as jnp
from jax import lax
from jax.experimental import pallas as pl
from jax.experimental.pallas import tpu as pltpu
from jax.sharding import PartitionSpec as P

GROUPS = 4
HEADDIM = 64
STATE = 128
LANES = 128
TOP = 13.0
CUT = -65000.0
F32 = jnp.float32
BF16 = jnp.bfloat16
PRECISE = lax.Precision.HIGHEST
PARAMS = pltpu.CompilerParams(vmem_limit_bytes=40 * 1024 * 1024)


def iota(shape, axis):
    return lax.broadcasted_iota(jnp.int32, shape, axis)


def split(value):
    high = value.astype(BF16)
    return high, (value - high.astype(F32)).astype(BF16)


def dot(a, b, dims=((1,), (0,)), precision=None):
    return lax.dot_general(a, b, (dims, ((), ())), precision=precision, preferred_element_type=F32)


def spread_map(heads, dtype):
    shape = (heads, heads * HEADDIM)
    return (iota(shape, 0) == iota(shape, 1) // HEADDIM).astype(dtype)


def widen(value):
    both = jnp.concatenate(split(value), axis=1)
    spread = spread_map(value.shape[1], BF16)
    return dot(both, jnp.concatenate([spread, spread], axis=0))


def head_sums(value):
    heads = value.shape[1] // HEADDIM
    shape = (heads * HEADDIM, heads)
    fold = (iota(shape, 0) // HEADDIM == iota(shape, 1)).astype(BF16)
    high, low = split(value)
    return dot(high, fold) + dot(low, fold)


def exponent_of(block):
    top = jnp.max(jnp.abs(block), axis=0, keepdims=True)
    return jnp.clip(jnp.floor(jnp.log(jnp.maximum(top, 1e-30)) * 1.4426950408889634), -90.0, 40.0)


def prep_kernel(dt_ref, par_ref, st_ref, size_ref, sig_ref, run_ref, runt_ref, reach_ref, tail_ref, bias_ref, edge_ref):
    tokens, heads = dt_ref.shape
    per = heads // GROUPS
    par = par_ref[...]
    a_log, dt_bias = par[0:1], par[1:2]
    decay = -jnp.exp(a_log)
    value = dt_ref[...].astype(F32) + dt_bias
    sizes = jnp.maximum(value, 0.0) + jnp.log1p(jnp.exp(-jnp.abs(value)))
    sigmoid = 1.0 / (1.0 + jnp.exp(-value))
    shape = (tokens, tokens)
    lower = (iota(shape, 0) >= iota(shape, 1)).astype(F32)
    upper = (iota(shape, 0) <= iota(shape, 1)).astype(F32)
    running = dot(lower, sizes * decay, precision=PRECISE)
    marks = st_ref[...]
    doc_row = dot(marks, upper)[0:1]
    doc_col = dot(lower, marks, ((1,), (1,)))[:, 0:1]
    doc_last = doc_row[:, tokens - 1 :]
    last = running[tokens - 1 :]
    reach = jnp.where(doc_col == 0.0, jnp.exp(running), 0.0)
    tail = jnp.where(doc_col == doc_last, jnp.exp(last - running), 0.0) * sizes
    linked = (doc_col == doc_row) & (iota(shape, 0) >= iota(shape, 1))
    bias_ref[...] = jnp.where(linked, 0.0, -1e30)
    turned = (running - jnp.log(sizes)).T
    through = jnp.where(doc_last == 0.0, last * 128.0, CUT)
    high = through.astype(BF16).astype(F32)
    mid = (through - high).astype(BF16).astype(F32)
    low = (through - high - mid).astype(BF16).astype(F32)
    keep = jnp.exp((high + mid + low) * (1.0 / 128.0))
    edge = jnp.concatenate([high, mid, low, jnp.zeros_like(keep), keep, decay, decay, decay], axis=0)
    for g in range(GROUPS):
        mine = slice(g * per, (g + 1) * per)
        size_ref[g] = sizes[:, mine]
        sig_ref[g] = sigmoid[:, mine]
        run_ref[g] = running[:, mine]
        runt_ref[g] = turned[mine]
        reach_ref[g] = reach[:, mine]
        tail_ref[g] = tail[:, mine]
        edge_ref[g] = edge[:, mine]


def prep(dt_raw, params, marks):
    tokens, heads = dt_raw.shape
    per = heads // GROUPS
    token_head = jax.ShapeDtypeStruct((GROUPS, tokens, per), F32)
    return pl.pallas_call(
        prep_kernel,
        out_shape=[
            token_head,
            token_head,
            token_head,
            jax.ShapeDtypeStruct((GROUPS, per, tokens), F32),
            token_head,
            token_head,
            jax.ShapeDtypeStruct((tokens, tokens), F32),
            jax.ShapeDtypeStruct((GROUPS, 8, per), F32),
        ],
        compiler_params=PARAMS,
        name="prep",
    )(dt_raw, params, marks)


def state_of(val_ref, proj_ref, scale_ref):
    high, low = split(val_ref[...].astype(F32) * widen(scale_ref[0]))
    proj = proj_ref[...]
    return dot(jnp.concatenate([proj, proj], axis=0), jnp.concatenate([high, low], axis=0), ((0,), (0,)))


def state_kernel(x_ref, w_ref, b_ref, c_ref, tail_ref, reach_ref, edge_ref, out_ref):
    forth = state_of(x_ref, b_ref, tail_ref)
    back = state_of(w_ref, c_ref, reach_ref)
    pieces = dot(edge_ref[0].astype(BF16), spread_map(tail_ref.shape[2], BF16))
    messages, rows, _ = out_ref.shape
    part = (rows - 8) // 2
    fold = STATE // part
    row = iota((8, LANES), 0)
    for k in range(messages):
        lanes = slice(k // fold * LANES, (k // fold + 1) * LANES)
        here = slice(k % fold * part, (k % fold + 1) * part)
        aux = jnp.where(row < 3, pieces[:, lanes], 0.0)
        for which, state in enumerate((forth, back)):
            block = state[here, lanes]
            power = exponent_of(block)
            out_ref[k, which * part : (which + 1) * part] = block * jnp.exp2(TOP - power)
            aux = jnp.where(row == 3 + which, power, aux)
        out_ref[k, 2 * part :] = aux


def states(x, w, b, c, tail, reach, edge, parts):
    tokens, channels = x.shape
    wide = channels // GROUPS
    per = tail.shape[2]
    rows = 2 * STATE * channels // (parts * LANES) + 8
    values = pl.BlockSpec((tokens, wide), lambda g: (0, g))
    proj = pl.BlockSpec((tokens, STATE), lambda g: (0, g))
    small = pl.BlockSpec((1, tokens, per), lambda g: (g, 0, 0))
    return pl.pallas_call(
        state_kernel,
        grid=(GROUPS,),
        in_specs=[values, values, proj, proj, small, small, pl.BlockSpec((1, 8, per), lambda g: (g, 0, 0))],
        out_specs=pl.BlockSpec((parts // GROUPS, rows, LANES), lambda g: (g, 0, 0)),
        out_shape=jax.ShapeDtypeStruct((parts, rows, LANES), F32),
        compiler_params=PARAMS,
        cost_estimate=pl.CostEstimate(flops=8 * tokens * STATE * channels, bytes_accessed=7000000, transcendentals=0),
        name="states",
    )(x, w, b, c, tail, reach, edge)


def keep_row(pay_ref, i, part):
    side = pay_ref[i, 2 * part :]
    return jnp.exp((side[0:1] + side[1:2] + side[2:3]) * (1.0 / 128.0))


def unscaled(pay_ref, i, part, which):
    power = pay_ref[i, 2 * part :][3 + which : 4 + which]
    return pay_ref[i, which * part : (which + 1) * part] * jnp.exp2(power - TOP)


def total_kernel(pay_ref, out_ref):
    blocks, rows, _ = pay_ref.shape
    part = (rows - 8) // 2

    def step(k, carry):
        forth, back, through = carry
        forth = keep_row(pay_ref, k, part) * forth + unscaled(pay_ref, k, part, 0)
        late = blocks - 1 - k
        keep = keep_row(pay_ref, late, part)
        return forth, unscaled(pay_ref, late, part, 1) + keep * back, through * keep

    zero = jnp.zeros((part, LANES), F32)
    forth, back, through = lax.fori_loop(0, blocks, step, (zero, zero, jnp.ones((1, LANES), F32)), unroll=8)
    for which, state in enumerate((forth, back)):
        out_ref[which, 0:part] = state
        out_ref[which, part:] = jnp.broadcast_to(through, (8, LANES))


def totals(pay):
    _, rows, _ = pay.shape
    part = (rows - 8) // 2
    return pl.pallas_call(
        total_kernel,
        out_shape=jax.ShapeDtypeStruct((2, part + 8, LANES), F32),
        compiler_params=PARAMS,
        cost_estimate=pl.CostEstimate(flops=2 * pay.size, bytes_accessed=4 * pay.size, transcendentals=0),
        name="totals",
    )(pay)


def enter_kernel(pay_ref, forth_ref, back_ref, out_ref):
    blocks, rows, _ = pay_ref.shape
    part = (rows - 8) // 2
    row = iota((8, LANES), 0)

    def put(i, which, state):
        power = exponent_of(state)
        out_ref[i, which * part : (which + 1) * part] = state * jnp.exp2(TOP - power)
        return power

    def step(k, carry):
        forth, back = carry
        late = blocks - 1 - k
        out_ref[k, 2 * part :] = jnp.where(row == 3, put(k, 0, forth), out_ref[k, 2 * part :])
        out_ref[late, 2 * part :] = jnp.where(row == 4, put(late, 1, back), out_ref[late, 2 * part :])
        forth = keep_row(pay_ref, k, part) * forth + unscaled(pay_ref, k, part, 0)
        back = keep_row(pay_ref, late, part) * back + unscaled(pay_ref, late, part, 1)
        return forth, back

    out_ref[:, 2 * part :, :] = jnp.zeros((blocks, 8, LANES), F32)
    lax.fori_loop(0, blocks, step, (forth_ref[0:part], back_ref[0:part]), unroll=8)


def entering(pay, forth, back):
    return pl.pallas_call(
        enter_kernel,
        out_shape=jax.ShapeDtypeStruct(pay.shape, F32),
        compiler_params=PARAMS,
        cost_estimate=pl.CostEstimate(flops=4 * pay.size, bytes_accessed=8 * pay.size, transcendentals=0),
        name="entering",
    )(pay, forth, back)


def carried_in(total, reverse):
    count = lax.axis_size("far")

    def moved(by):
        if reverse:
            pairs = [(s, s - by) for s in range(by, count)]
        else:
            pairs = [(s, s + by) for s in range(count - by)]
        return lax.ppermute(total, "far", pairs)

    def joined(near, far):
        through = near[-8:]
        state = near[:-8] + through[0:1] * far[:-8]
        return jnp.concatenate([state, through * far[-8:]], axis=0)

    return functools.reduce(joined, [moved(by) for by in range(1, count)])


def inner_kernel(x_ref, w_ref, b_ref, c_ref, run_ref, runt_ref, bias_ref, skip_ref, y_ref, gx_ref, gb_ref, gc_ref, col_ref, diff_ref):
    tokens, wide = x_ref.shape
    heads = wide // HEADDIM
    pair = 2 * HEADDIM
    b_vals, c_vals = b_ref[...], c_ref[...]
    scores = dot(c_vals, b_vals, ((1,), (1,)))
    bias = bias_ref[...]
    run, runt = run_ref[0], runt_ref[0]
    first = iota((tokens, pair), 1) < HEADDIM
    grad_scores = jnp.zeros((tokens, tokens), F32)
    y_all, u_all = [], []
    for k in range(0, heads, 2):
        mine = slice(k * HEADDIM, (k + 2) * HEADDIM)
        x_pair, w_pair = x_ref[:, mine], w_ref[:, mine]
        x_two = jnp.concatenate([x_pair, x_pair], axis=0)
        w_two = jnp.concatenate([w_pair, w_pair], axis=0)
        ys, us = [], []
        for which in range(2):
            h = k + which
            keep = first if which == 0 else ~first
            weight = jnp.exp(run[:, h : h + 1] - runt[h : h + 1, :] + bias)
            cross = dot(jnp.where(keep, w_pair, jnp.zeros_like(w_pair)), x_pair, ((1,), (1,)))
            grad_scores = grad_scores + weight * cross
            high, low = split(weight * scores)
            ys.append(dot(jnp.concatenate([high, low], axis=1), x_two))
            us.append(dot(jnp.concatenate([high, low], axis=0), w_two, ((0,), (0,))))
        y_all.append(jnp.where(first, ys[0], ys[1]))
        u_all.append(jnp.where(first, us[0], us[1]))
    y_in = jnp.concatenate(y_all, axis=1)
    u_in = jnp.concatenate(u_all, axis=1)
    x_vals, w_vals = x_ref[...].astype(F32), w_ref[...].astype(F32)
    skip = skip_ref[0:1]
    y_ref[...] = y_in + skip * x_vals
    gx_ref[...] = u_in + skip * w_vals
    high, low = split(grad_scores)
    gc_ref[...] = dot(jnp.concatenate([high, low], axis=1), jnp.concatenate([b_vals, b_vals], axis=0))
    gb_ref[...] = dot(jnp.concatenate([high, low], axis=0), jnp.concatenate([c_vals, c_vals], axis=0), ((0,), (0,)))
    col = head_sums(x_vals * u_in)
    col_ref[0] = col
    diff_ref[0] = head_sums(w_vals * y_in) - col


def inner(x, w, b, c, run, runt, bias, skip):
    tokens, channels = x.shape
    wide = channels // GROUPS
    per = run.shape[2]
    values = pl.BlockSpec((tokens, wide), lambda g: (0, g))
    proj = pl.BlockSpec((tokens, STATE), lambda g: (0, g))
    small = pl.BlockSpec((1, tokens, per), lambda g: (g, 0, 0))
    return pl.pallas_call(
        inner_kernel,
        grid=(GROUPS,),
        in_specs=[
            values,
            values,
            proj,
            proj,
            small,
            pl.BlockSpec((1, per, tokens), lambda g: (g, 0, 0)),
            pl.BlockSpec((tokens, tokens), lambda g: (0, 0)),
            pl.BlockSpec((8, wide), lambda g: (0, g)),
        ],
        out_specs=[values, values, proj, proj, small, small],
        out_shape=[
            jax.ShapeDtypeStruct((tokens, channels), F32),
            jax.ShapeDtypeStruct((tokens, channels), F32),
            jax.ShapeDtypeStruct((tokens, GROUPS * STATE), F32),
            jax.ShapeDtypeStruct((tokens, GROUPS * STATE), F32),
            jax.ShapeDtypeStruct((GROUPS, tokens, per), F32),
            jax.ShapeDtypeStruct((GROUPS, tokens, per), F32),
        ],
        compiler_params=PARAMS,
        cost_estimate=pl.CostEstimate(flops=20_000_000_000, bytes_accessed=8_000_000, transcendentals=tokens * tokens * 64),
        name="inner",
    )(x, w, b, c, run, runt, bias, skip)


def state_from(pay_ref, which):
    messages, rows, _ = pay_ref.shape
    part = (rows - 8) // 2
    fold = STATE // part
    columns = []
    for first in range(0, messages, fold):
        columns.append(jnp.concatenate([unscaled(pay_ref, first + k, part, which) for k in range(fold)], axis=0))
    return jnp.concatenate(columns, axis=1)


def carried_terms(state, values, scale_ref, proj_ref):
    wide = widen(scale_ref[0])
    proj = proj_ref[...]
    high, low = split(state)
    terms = dot(jnp.concatenate([proj, proj], axis=1), jnp.concatenate([high, low], axis=0)) * wide
    left_high, left_low = split(values * wide)
    last = ((1,), (1,))
    grad = dot(left_high, high, last) + (dot(left_high, low, last) + dot(left_low, high, last))
    return terms, grad, head_sums(terms * values)


def finish_kernel(
    pay_ref, x_ref, w_ref, b_ref, c_ref, tail_ref, reach_ref, y_ref, gx_ref, gb_ref, gc_ref, col_ref, diff_ref, size_ref, sig_ref, edge_ref,
    mixed_ref, gradx_ref, dt_ref, gradb_ref, gradc_ref, all_ref,
):
    g = pl.program_id(0)
    tokens, _ = x_ref.shape
    per = tail_ref.shape[2]
    enter, leave = state_from(pay_ref, 0), state_from(pay_ref, 1)
    terms, grad, rows = carried_terms(enter, w_ref[...].astype(F32), reach_ref, c_ref)
    mixed_ref[...] = (y_ref[...] + terms).astype(BF16)
    gradc_ref[...] = (gc_ref[...] + grad).astype(BF16)
    terms, grad, cols = carried_terms(leave, x_ref[...].astype(F32), tail_ref, b_ref)
    gradx_ref[...] = (gx_ref[...] + terms).astype(BF16)
    gradb_ref[...] = (gb_ref[...] + grad).astype(BF16)
    met = jnp.sum(enter * leave, axis=0, keepdims=True)
    met = head_sums(jnp.broadcast_to(met, (8, met.shape[1])))[0:1]
    edge = edge_ref[0]
    keep, decay = edge[4:5], edge[5:6]
    shape = (tokens, tokens)
    from_here = (iota(shape, 0) <= iota(shape, 1)).astype(F32)
    before = (iota(shape, 0) > iota(shape, 1)).astype(F32)
    grad_rate = dot(from_here, diff_ref[0] + rows, precision=PRECISE) + dot(before, cols, precision=PRECISE) + keep * met
    grad_size = (col_ref[0] + cols) / size_ref[0] + decay * grad_rate
    place = (iota((per, GROUPS * per), 0) + g * per == iota((per, GROUPS * per), 1)).astype(F32)
    placed = dot(grad_size * sig_ref[0], place, precision=PRECISE)

    @pl.when(g == 0)
    def _():
        all_ref[...] = placed

    @pl.when(g > 0)
    def _():
        all_ref[...] += placed

    dt_ref[...] = all_ref[...].astype(BF16)


def finish(pay, x, w, b, c, tail, reach, y, gx, gb, gc, col, diff, size, sig, edge):
    tokens, channels = x.shape
    parts, rows, _ = pay.shape
    wide = channels // GROUPS
    per = tail.shape[2]
    values = pl.BlockSpec((tokens, wide), lambda g: (0, g))
    proj = pl.BlockSpec((tokens, STATE), lambda g: (0, g))
    small = pl.BlockSpec((1, tokens, per), lambda g: (g, 0, 0))
    return pl.pallas_call(
        finish_kernel,
        grid=(GROUPS,),
        in_specs=[
            pl.BlockSpec((parts // GROUPS, rows, LANES), lambda g: (g, 0, 0)),
            values, values, proj, proj, small, small, values, values, proj, proj, small, small, small, small,
            pl.BlockSpec((1, 8, per), lambda g: (g, 0, 0)),
        ],
        out_specs=[values, values, pl.BlockSpec((tokens, GROUPS * per), lambda g: (0, 0)), proj, proj],
        out_shape=[
            jax.ShapeDtypeStruct((tokens, channels), BF16),
            jax.ShapeDtypeStruct((tokens, channels), BF16),
            jax.ShapeDtypeStruct((tokens, GROUPS * per), BF16),
            jax.ShapeDtypeStruct((tokens, GROUPS * STATE), BF16),
            jax.ShapeDtypeStruct((tokens, GROUPS * STATE), BF16),
        ],
        scratch_shapes=[pltpu.VMEM((tokens, GROUPS * per), F32)],
        compiler_params=PARAMS,
        cost_estimate=pl.CostEstimate(flops=20 * tokens * STATE * channels, bytes_accessed=14_000_000, transcendentals=0),
        name="finish",
    )(pay, x, w, b, c, tail, reach, y, gx, gb, gc, col, diff, size, sig, edge)


GROUP = ("near", "head")


def exchanged(messages):
    sent = lax.all_to_all(messages.astype(jnp.float16), GROUP, split_axis=0, concat_axis=0, tiled=True)
    return sent.astype(F32)


def gathered(own, heads):
    parts = lax.axis_size("head")
    per_dev = own.shape[1]
    mine = lax.axis_index("head")
    whole = jnp.where(iota((8, 128), 1) // per_dev == mine, jnp.tile(own, (1, 128 // per_dev)), 0.0)
    whole = jnp.broadcast_to(whole[None], (parts, 8, 128))
    return lax.all_to_all(whole, "head", split_axis=0, concat_axis=0, tiled=True).sum(axis=0)[:, :heads]


def per_device(features, dt_raw, b_proj, c_proj, cotangent, starts, a_log, dt_bias, d_skip):
    parts = lax.axis_size(GROUP)
    tokens, heads = dt_raw.shape
    params = gathered(jnp.stack([a_log, dt_bias, d_skip] + [d_skip] * 5), heads)
    marks = lax.dynamic_slice(starts, (lax.axis_index("head") * tokens,), (tokens,)).astype(F32)
    marks = jnp.broadcast_to(marks[None], (8, tokens))
    skip = jnp.broadcast_to(jnp.repeat(params[2], HEADDIM)[None], (8, heads * HEADDIM))
    size, sig, run, runt, reach, tail, bias, edge = prep(dt_raw, params, marks)
    came = exchanged(states(features, cotangent, b_proj, c_proj, tail, reach, edge, parts))
    y, gx, gb, gc, col, diff = inner(features, cotangent, b_proj, c_proj, run, runt, bias, skip)
    total = totals(came)
    back = exchanged(entering(came, carried_in(total[0], False), carried_in(total[1], True)))
    return finish(
        back, features, cotangent, b_proj, c_proj, tail, reach, y, gx, gb, gc, col, diff, size, sig, edge
    )


def solution(mesh):
    near = 8
    devices = mesh.devices
    seq, parts = devices.shape
    fine = jax.sharding.Mesh(devices.reshape(seq // near, near, parts), ("far",) + GROUP)
    token = P(("far",) + GROUP, None)
    return jax.shard_map(
        per_device,
        mesh=fine,
        in_specs=(token, token, token, token, token, P(("far", "near")), P("head"), P("head"), P("head")),
        out_specs=(token, token, token, token, token),
        check_vma=False,
    )
```

```python
import functools

import jax
import jax.numpy as jnp
from jax import lax
from jax.experimental import pallas as pl
from jax.experimental.pallas import tpu as pltpu
from jax.sharding import PartitionSpec as P

GROUPS = 4
HEADDIM = 64
STATE = 128
LANES = 128
BITS = 10.0
TOP = 13.0
CUT = -1000.0
F32 = jnp.float32
BF16 = jnp.bfloat16
PRECISE = lax.Precision.HIGHEST
PARAMS = pltpu.CompilerParams(vmem_limit_bytes=40 * 1024 * 1024)


def iota(shape, axis):
    return lax.broadcasted_iota(jnp.int32, shape, axis)


def split(value):
    high = value.astype(BF16)
    return high, (value - high.astype(F32)).astype(BF16)


def dot(a, b, dims=((1,), (0,)), precision=None):
    return lax.dot_general(a, b, (dims, ((), ())), precision=precision, preferred_element_type=F32)


def spread_map(heads, dtype):
    shape = (heads, heads * HEADDIM)
    return (iota(shape, 0) == iota(shape, 1) // HEADDIM).astype(dtype)


def widen(value):
    both = jnp.concatenate(split(value), axis=1)
    spread = spread_map(value.shape[1], BF16)
    return dot(both, jnp.concatenate([spread, spread], axis=0))


def head_sums(value):
    heads = value.shape[1] // HEADDIM
    shape = (heads * HEADDIM, heads)
    fold = (iota(shape, 0) // HEADDIM == iota(shape, 1)).astype(BF16)
    high, low = split(value)
    return dot(high, fold) + dot(low, fold)


def exponent_of(block):
    top = jnp.max(jnp.max(jnp.abs(block), axis=0, keepdims=True), axis=1, keepdims=True)
    return jnp.clip(jnp.floor(jnp.log(jnp.maximum(top, 1e-30)) * 1.4426950408889634), -90.0, 40.0)


def prep_kernel(dt_ref, par_ref, st_ref, size_ref, sig_ref, run_ref, runt_ref, reach_ref, tail_ref, bias_ref, edge_ref):
    tokens, heads = dt_ref.shape
    per = heads // GROUPS
    par = par_ref[...]
    a_log, dt_bias = par[0:1], par[1:2]
    decay = -jnp.exp(a_log)
    value = dt_ref[...].astype(F32) + dt_bias
    sizes = jnp.maximum(value, 0.0) + jnp.log1p(jnp.exp(-jnp.abs(value)))
    sigmoid = 1.0 / (1.0 + jnp.exp(-value))
    shape = (tokens, tokens)
    lower = (iota(shape, 0) >= iota(shape, 1)).astype(F32)
    upper = (iota(shape, 0) <= iota(shape, 1)).astype(F32)
    running = dot(lower, sizes * decay, precision=PRECISE)
    marks = st_ref[...]
    doc_row = dot(marks, upper)[0:1]
    doc_col = dot(lower, marks, ((1,), (1,)))[:, 0:1]
    doc_last = doc_row[:, tokens - 1 :]
    last = running[tokens - 1 :]
    reach = jnp.where(doc_col == 0.0, jnp.exp(running), 0.0)
    tail = jnp.where(doc_col == doc_last, jnp.exp(last - running), 0.0) * sizes
    linked = (doc_col == doc_row) & (iota(shape, 0) >= iota(shape, 1))
    bias_ref[...] = jnp.where(linked, 0.0, -1e30)
    turned = (running - jnp.log(sizes)).T
    through = jnp.where(doc_last == 0.0, last, CUT)
    keep = jnp.exp(through)
    edge = jnp.concatenate([through, keep, decay] + [decay] * 5, axis=0)
    for g in range(GROUPS):
        mine = slice(g * per, (g + 1) * per)
        size_ref[g] = sizes[:, mine]
        sig_ref[g] = sigmoid[:, mine]
        run_ref[g] = running[:, mine]
        runt_ref[g] = turned[mine]
        reach_ref[g] = reach[:, mine]
        tail_ref[g] = tail[:, mine]
        edge_ref[g] = edge[:, mine]


def prep(dt_raw, params, marks):
    tokens, heads = dt_raw.shape
    per = heads // GROUPS
    token_head = jax.ShapeDtypeStruct((GROUPS, tokens, per), F32)
    return pl.pallas_call(
        prep_kernel,
        out_shape=[
            token_head,
            token_head,
            token_head,
            jax.ShapeDtypeStruct((GROUPS, per, tokens), F32),
            token_head,
            token_head,
            jax.ShapeDtypeStruct((tokens, tokens), F32),
            jax.ShapeDtypeStruct((GROUPS, 8, per), F32),
        ],
        compiler_params=PARAMS,
        name="prep",
    )(dt_raw, params, marks)


def state_of(val_ref, proj_ref, scale_ref):
    high, low = split(val_ref[...].astype(F32) * widen(scale_ref[0]))
    proj = proj_ref[...]
    return dot(jnp.concatenate([proj, proj], axis=0), jnp.concatenate([high, low], axis=0), ((0,), (0,)))


def state_kernel(x_ref, w_ref, b_ref, c_ref, tail_ref, reach_ref, out_ref, power_ref):
    messages, rows, _ = out_ref.shape
    part = rows // 2
    fold = STATE // part
    row = iota((8, LANES), 0)
    powers = jnp.zeros((8, LANES), F32)
    for which, state in enumerate((state_of(x_ref, b_ref, tail_ref), state_of(w_ref, c_ref, reach_ref))):
        power = exponent_of(state)
        powers = jnp.where(row == which, jnp.broadcast_to(power, powers.shape), powers)
        state = state * jnp.exp2(TOP - power)
        for k in range(messages):
            lanes = slice(k // fold * LANES, (k // fold + 1) * LANES)
            here = slice(k % fold * part, (k % fold + 1) * part)
            out_ref[k, which * part : (which + 1) * part] = state[here, lanes]
    power_ref[0] = powers


def states(x, w, b, c, tail, reach, parts):
    tokens, channels = x.shape
    wide = channels // GROUPS
    per = tail.shape[2]
    rows = 2 * STATE * channels // (parts * LANES)
    values = pl.BlockSpec((tokens, wide), lambda g: (0, g))
    proj = pl.BlockSpec((tokens, STATE), lambda g: (0, g))
    small = pl.BlockSpec((1, tokens, per), lambda g: (g, 0, 0))
    return pl.pallas_call(
        state_kernel,
        grid=(GROUPS,),
        in_specs=[values, values, proj, proj, small, small],
        out_specs=[
            pl.BlockSpec((parts // GROUPS, rows, LANES), lambda g: (g, 0, 0)),
            pl.BlockSpec((1, 8, LANES), lambda g: (g, 0, 0)),
        ],
        out_shape=[
            jax.ShapeDtypeStruct((parts, rows, LANES), F32),
            jax.ShapeDtypeStruct((GROUPS, 8, LANES), F32),
        ],
        compiler_params=PARAMS,
        cost_estimate=pl.CostEstimate(flops=8 * tokens * STATE * channels, bytes_accessed=7000000, transcendentals=0),
        name="states",
    )(x, w, b, c, tail, reach)


def block_of(pay_ref, side_ref, i, which):
    part = pay_ref.shape[1] // 2
    return pay_ref[i, which * part : (which + 1) * part] * side_ref[1 + which, pl.ds(i, 1)]


def total_kernel(pay_ref, side_ref, most_ref, out_ref):
    blocks, rows, _ = pay_ref.shape
    part = rows // 2

    def step(k, carry):
        forth, back, through = carry
        late = blocks - 1 - k
        keep, keep_late = side_ref[0, pl.ds(k, 1)], side_ref[0, pl.ds(late, 1)]
        forth = keep * forth + block_of(pay_ref, side_ref, k, 0)
        back = keep_late * back + block_of(pay_ref, side_ref, late, 1)
        return forth, back, through * keep

    zero = jnp.zeros((part, LANES), F32)
    forth, back, through = lax.fori_loop(0, blocks, step, (zero, zero, jnp.ones((1, LANES), F32)), unroll=8)
    row = iota((8, LANES), 0)
    side = jnp.where(row == 0, through, most_ref[...])
    for which, state in enumerate((forth, back)):
        out_ref[which, 0:part] = state
        out_ref[which, part:] = side


def totals(pay, side, most):
    part = pay.shape[1] // 2
    return pl.pallas_call(
        total_kernel,
        out_shape=jax.ShapeDtypeStruct((2, part + 8, LANES), F32),
        compiler_params=PARAMS,
        cost_estimate=pl.CostEstimate(flops=2 * pay.size, bytes_accessed=4 * pay.size, transcendentals=0),
        name="totals",
    )(pay, side, most)


def enter_kernel(pay_ref, side_ref, own_ref, far_ref, mask_ref, out_ref, most_ref):
    blocks, rows, _ = pay_ref.shape
    part = rows // 2
    others = far_ref.shape[0]
    most = own_ref[0, part:]
    for k in range(others):
        most = jnp.maximum(most, far_ref[k, 0, part:])
    most_ref[...] = most
    starts = []
    for which in range(2):
        state = jnp.zeros((part, LANES), F32)
        for by in range(others, 0, -1):
            k = by - 1 if which == 0 else others - by
            far = far_ref[k, which]
            valid = mask_ref[which * others + by - 1 : which * others + by] > 0.0
            state = jnp.where(valid, far[0:part] + far[part : part + 1] * state, state)
        starts.append(state)
    scales = []
    for which in range(2):
        mine = mask_ref[2 * others + which : 2 * others + which + 1]
        power = jnp.sum(most[1:2] * mine, axis=1, keepdims=True)
        scales.append(jnp.exp2(TOP + 2.0 - BITS - power))

    def step(k, carry):
        forth, back = carry
        late = blocks - 1 - k
        out_ref[k, 0:part] = forth * scales[0]
        out_ref[late, part:] = back * scales[1]
        forth = side_ref[0, pl.ds(k, 1)] * forth + block_of(pay_ref, side_ref, k, 0)
        back = side_ref[0, pl.ds(late, 1)] * back + block_of(pay_ref, side_ref, late, 1)
        return forth, back

    lax.fori_loop(0, blocks, step, tuple(starts), unroll=8)


def entering(pay, side, own, far, mask):
    return pl.pallas_call(
        enter_kernel,
        out_shape=[jax.ShapeDtypeStruct(pay.shape, F32), jax.ShapeDtypeStruct((8, LANES), F32)],
        compiler_params=PARAMS,
        cost_estimate=pl.CostEstimate(flops=4 * pay.size, bytes_accessed=8 * pay.size, transcendentals=0),
        name="entering",
    )(pay, side, own, far, mask)


def inner_kernel(x_ref, w_ref, b_ref, c_ref, run_ref, runt_ref, bias_ref, skip_ref, y_ref, gx_ref, gb_ref, gc_ref, col_ref, diff_ref):
    tokens, wide = x_ref.shape
    heads = wide // HEADDIM
    pair = 2 * HEADDIM
    b_vals, c_vals = b_ref[...], c_ref[...]
    scores = dot(c_vals, b_vals, ((1,), (1,)))
    bias = bias_ref[...]
    run, runt = run_ref[0], runt_ref[0]
    first = iota((tokens, pair), 1) < HEADDIM
    grad_scores = jnp.zeros((tokens, tokens), F32)
    y_all, u_all = [], []
    for k in range(0, heads, 2):
        mine = slice(k * HEADDIM, (k + 2) * HEADDIM)
        x_pair, w_pair = x_ref[:, mine], w_ref[:, mine]
        x_two = jnp.concatenate([x_pair, x_pair], axis=0)
        w_two = jnp.concatenate([w_pair, w_pair], axis=0)
        ys, us = [], []
        for which in range(2):
            h = k + which
            keep = first if which == 0 else ~first
            weight = jnp.exp(run[:, h : h + 1] - runt[h : h + 1, :] + bias)
            cross = dot(jnp.where(keep, w_pair, jnp.zeros_like(w_pair)), x_pair, ((1,), (1,)))
            grad_scores = grad_scores + weight * cross
            high, low = split(weight * scores)
            ys.append(dot(jnp.concatenate([high, low], axis=1), x_two))
            us.append(dot(jnp.concatenate([high, low], axis=0), w_two, ((0,), (0,))))
        y_all.append(jnp.where(first, ys[0], ys[1]))
        u_all.append(jnp.where(first, us[0], us[1]))
    y_in = jnp.concatenate(y_all, axis=1)
    u_in = jnp.concatenate(u_all, axis=1)
    x_vals, w_vals = x_ref[...].astype(F32), w_ref[...].astype(F32)
    skip = skip_ref[0:1]
    y_ref[...] = y_in + skip * x_vals
    gx_ref[...] = u_in + skip * w_vals
    high, low = split(grad_scores)
    gc_ref[...] = dot(jnp.concatenate([high, low], axis=1), jnp.concatenate([b_vals, b_vals], axis=0))
    gb_ref[...] = dot(jnp.concatenate([high, low], axis=0), jnp.concatenate([c_vals, c_vals], axis=0), ((0,), (0,)))
    col = head_sums(x_vals * u_in)
    col_ref[0] = col
    diff_ref[0] = head_sums(w_vals * y_in) - col


def inner(x, w, b, c, run, runt, bias, skip):
    tokens, channels = x.shape
    wide = channels // GROUPS
    per = run.shape[2]
    values = pl.BlockSpec((tokens, wide), lambda g: (0, g))
    proj = pl.BlockSpec((tokens, STATE), lambda g: (0, g))
    small = pl.BlockSpec((1, tokens, per), lambda g: (g, 0, 0))
    return pl.pallas_call(
        inner_kernel,
        grid=(GROUPS,),
        in_specs=[
            values,
            values,
            proj,
            proj,
            small,
            pl.BlockSpec((1, per, tokens), lambda g: (g, 0, 0)),
            pl.BlockSpec((tokens, tokens), lambda g: (0, 0)),
            pl.BlockSpec((8, wide), lambda g: (0, g)),
        ],
        out_specs=[values, values, proj, proj, small, small],
        out_shape=[
            jax.ShapeDtypeStruct((tokens, channels), F32),
            jax.ShapeDtypeStruct((tokens, channels), F32),
            jax.ShapeDtypeStruct((tokens, GROUPS * STATE), F32),
            jax.ShapeDtypeStruct((tokens, GROUPS * STATE), F32),
            jax.ShapeDtypeStruct((GROUPS, tokens, per), F32),
            jax.ShapeDtypeStruct((GROUPS, tokens, per), F32),
        ],
        compiler_params=PARAMS,
        cost_estimate=pl.CostEstimate(flops=20_000_000_000, bytes_accessed=8_000_000, transcendentals=tokens * tokens * 64),
        name="inner",
    )(x, w, b, c, run, runt, bias, skip)


def state_from(pay_ref, most_ref, group, which):
    messages, rows, _ = pay_ref.shape
    part = rows // 2
    fold = STATE // part
    here = slice(which * part, (which + 1) * part)
    most = most_ref[1:2]
    mine = iota(most.shape, 1) == which * GROUPS + group
    power = jnp.sum(jnp.where(mine, most, 0.0), axis=1, keepdims=True)
    columns = []
    for first in range(0, messages, fold):
        columns.append(jnp.concatenate([pay_ref[first + k, here] for k in range(fold)], axis=0))
    return jnp.concatenate(columns, axis=1) * jnp.exp2(power - (TOP + 2.0 - BITS))


def carried_terms(state, values, scale_ref, proj_ref):
    wide = widen(scale_ref[0])
    proj = proj_ref[...]
    high, low = split(state)
    terms = dot(jnp.concatenate([proj, proj], axis=1), jnp.concatenate([high, low], axis=0)) * wide
    left_high, left_low = split(values * wide)
    last = ((1,), (1,))
    grad = dot(left_high, high, last) + (dot(left_high, low, last) + dot(left_low, high, last))
    return terms, grad, head_sums(terms * values)


def finish_kernel(
    pay_ref, most_ref, x_ref, w_ref, b_ref, c_ref, tail_ref, reach_ref, y_ref, gx_ref, gb_ref, gc_ref, col_ref, diff_ref, size_ref, sig_ref, edge_ref,
    mixed_ref, gradx_ref, dt_ref, gradb_ref, gradc_ref, all_ref,
):
    g = pl.program_id(0)
    tokens, _ = x_ref.shape
    per = tail_ref.shape[2]
    enter, leave = state_from(pay_ref, most_ref, g, 0), state_from(pay_ref, most_ref, g, 1)
    terms, grad, rows = carried_terms(enter, w_ref[...].astype(F32), reach_ref, c_ref)
    mixed_ref[...] = (y_ref[...] + terms).astype(BF16)
    gradc_ref[...] = (gc_ref[...] + grad).astype(BF16)
    terms, grad, cols = carried_terms(leave, x_ref[...].astype(F32), tail_ref, b_ref)
    gradx_ref[...] = (gx_ref[...] + terms).astype(BF16)
    gradb_ref[...] = (gb_ref[...] + grad).astype(BF16)
    met = jnp.sum(enter * leave, axis=0, keepdims=True)
    met = head_sums(jnp.broadcast_to(met, (8, met.shape[1])))[0:1]
    edge = edge_ref[0]
    keep, decay = edge[1:2], edge[2:3]
    shape = (tokens, tokens)
    from_here = (iota(shape, 0) <= iota(shape, 1)).astype(F32)
    before = (iota(shape, 0) > iota(shape, 1)).astype(F32)
    grad_rate = dot(from_here, diff_ref[0] + rows, precision=PRECISE) + dot(before, cols, precision=PRECISE) + keep * met
    grad_size = (col_ref[0] + cols) / size_ref[0] + decay * grad_rate
    place = (iota((per, GROUPS * per), 0) + g * per == iota((per, GROUPS * per), 1)).astype(F32)
    placed = dot(grad_size * sig_ref[0], place, precision=PRECISE)

    @pl.when(g == 0)
    def _():
        all_ref[...] = placed

    @pl.when(g > 0)
    def _():
        all_ref[...] += placed

    dt_ref[...] = all_ref[...].astype(BF16)


def finish(pay, most, x, w, b, c, tail, reach, y, gx, gb, gc, col, diff, size, sig, edge):
    tokens, channels = x.shape
    parts, rows, _ = pay.shape
    wide = channels // GROUPS
    per = tail.shape[2]
    values = pl.BlockSpec((tokens, wide), lambda g: (0, g))
    proj = pl.BlockSpec((tokens, STATE), lambda g: (0, g))
    small = pl.BlockSpec((1, tokens, per), lambda g: (g, 0, 0))
    return pl.pallas_call(
        finish_kernel,
        grid=(GROUPS,),
        in_specs=[
            pl.BlockSpec((parts // GROUPS, rows, LANES), lambda g: (g, 0, 0)),
            pl.BlockSpec((8, LANES), lambda g: (0, 0)),
            values, values, proj, proj, small, small, values, values, proj, proj, small, small, small, small,
            pl.BlockSpec((1, 8, per), lambda g: (g, 0, 0)),
        ],
        out_specs=[values, values, pl.BlockSpec((tokens, GROUPS * per), lambda g: (0, 0)), proj, proj],
        out_shape=[
            jax.ShapeDtypeStruct((tokens, channels), BF16),
            jax.ShapeDtypeStruct((tokens, channels), BF16),
            jax.ShapeDtypeStruct((tokens, GROUPS * per), BF16),
            jax.ShapeDtypeStruct((tokens, GROUPS * STATE), BF16),
            jax.ShapeDtypeStruct((tokens, GROUPS * STATE), BF16),
        ],
        scratch_shapes=[pltpu.VMEM((tokens, GROUPS * per), F32)],
        compiler_params=PARAMS,
        cost_estimate=pl.CostEstimate(flops=20 * tokens * STATE * channels, bytes_accessed=14_000_000, transcendentals=0),
        name="finish",
    )(pay, most, x, w, b, c, tail, reach, y, gx, gb, gc, col, diff, size, sig, edge)


GROUP = ("near", "head")


def exchanged(messages):
    sent = lax.all_to_all(messages.astype(jnp.float16), GROUP, split_axis=0, concat_axis=0, tiled=True)
    return sent.astype(F32)


def gathered(own, heads):
    parts = lax.axis_size("head")
    per_dev = own.shape[1]
    mine = lax.axis_index("head")
    whole = jnp.where(iota((8, 128), 1) // per_dev == mine, jnp.tile(own, (1, 128 // per_dev)), 0.0)
    whole = jnp.broadcast_to(whole[None], (parts, 8, 128))
    return lax.all_to_all(whole, "head", split_axis=0, concat_axis=0, tiled=True).sum(axis=0)[:, :heads]


def around(value, axis, stride, count):
    size = lax.axis_size(axis)
    digit = lax.axis_index(axis) // stride % count
    place = iota((count,) + (1,) * value.ndim, 0)
    whole = jnp.where(place == digit, value[None], 0.0)
    for k in range(1, count):
        pairs = [(p, p + ((p // stride + k) % count - p // stride % count) * stride) for p in range(size)]
        came = lax.ppermute(value, axis, pairs)
        whole = whole + jnp.where(place == (digit - k) % count, came[None], 0.0)
    return whole


def known_around(edge, powers, heads):
    own = jnp.concatenate([edge[:, 0].reshape(1, heads), powers[:, 0:2, 0].T.reshape(1, 2 * GROUPS)], axis=1)
    own = jnp.pad(own, ((0, 0), (0, LANES - own.shape[1])))
    table = around(own[0], "head", 1, 4)
    table = around(table, "head", 4, lax.axis_size("head") // 4).reshape(-1, LANES)
    return around(table, "near", 1, lax.axis_size("near")).reshape(-1, LANES)


def per_device(features, dt_raw, b_proj, c_proj, cotangent, starts, a_log, dt_bias, d_skip):
    parts = lax.axis_size(GROUP)
    tokens, heads = dt_raw.shape
    params = gathered(jnp.stack([a_log, dt_bias, d_skip] + [d_skip] * 5), heads)
    marks = lax.dynamic_slice(starts, (lax.axis_index("head") * tokens,), (tokens,)).astype(F32)
    marks = jnp.broadcast_to(marks[None], (8, tokens))
    skip = jnp.broadcast_to(jnp.repeat(params[2], HEADDIM)[None], (8, heads * HEADDIM))
    size, sig, run, runt, reach, tail, bias, edge = prep(dt_raw, params, marks)
    sent, powers = states(features, cotangent, b_proj, c_proj, tail, reach, parts)
    came = exchanged(sent)
    table = known_around(edge, powers, heads)
    y, gx, gb, gc, col, diff = inner(features, cotangent, b_proj, c_proj, run, runt, bias, skip)
    pair = lax.axis_index(GROUP) // (parts * 2 // heads)
    group = pair // (heads // 2 // GROUPS)
    decays = lax.dynamic_slice(table, (0, 2 * pair), (parts, 2))
    column = lambda at: lax.dynamic_slice(table, (0, at), (parts, 1))
    scales = [jnp.broadcast_to(jnp.exp2(column(heads + k * GROUPS + group) - TOP), (parts, LANES)) for k in range(2)]
    side = jnp.stack([jnp.repeat(jnp.exp(decays), HEADDIM, axis=1)] + scales)
    most = jnp.pad(jnp.max(table[:, heads : heads + 2 * GROUPS], axis=0), (0, LANES - 2 * GROUPS))
    total = totals(came, side, jnp.broadcast_to(most[None], (8, LANES)))
    count, here = lax.axis_size("far"), lax.axis_index("far")
    far = [lax.ppermute(total, "far", [(p, (p + by) % count) for p in range(count)]) for by in range(1, count)]
    lane = jnp.arange(LANES)
    mask = [jnp.full((LANES,), here - by >= 0) for by in range(1, count)]
    mask += [jnp.full((LANES,), here + by < count) for by in range(1, count)]
    mask += [lane == group, lane == GROUPS + group]
    left, most = entering(came, side, total, jnp.stack(far), jnp.stack(mask).astype(F32))
    return finish(
        exchanged(left), most, features, cotangent, b_proj, c_proj, tail, reach, y, gx, gb, gc, col, diff, size, sig, edge
    )


def solution(mesh):
    near = 8
    devices = mesh.devices
    seq, parts = devices.shape
    fine = jax.sharding.Mesh(devices.reshape(seq // near, near, parts), ("far",) + GROUP)
    token = P(("far",) + GROUP, None)
    return jax.shard_map(
        per_device,
        mesh=fine,
        in_specs=(token, token, token, token, token, P(("far", "near")), P("head"), P("head"), P("head")),
        out_specs=(token, token, token, token, token),
        check_vma=False,
    )
```

```python
import functools

import jax
import jax.numpy as jnp
from jax import lax
from jax.experimental import pallas as pl
from jax.experimental.pallas import tpu as pltpu
from jax.sharding import PartitionSpec as P

GROUPS = 4
HEADDIM = 64
STATE = 128
LANES = 128
BITS = 10.0
TOP = 13.0
CUT = -65000.0
F32 = jnp.float32
BF16 = jnp.bfloat16
PRECISE = lax.Precision.HIGHEST
PARAMS = pltpu.CompilerParams(vmem_limit_bytes=40 * 1024 * 1024)


def iota(shape, axis):
    return lax.broadcasted_iota(jnp.int32, shape, axis)


def split(value):
    high = value.astype(BF16)
    return high, (value - high.astype(F32)).astype(BF16)


def dot(a, b, dims=((1,), (0,)), precision=None):
    return lax.dot_general(a, b, (dims, ((), ())), precision=precision, preferred_element_type=F32)


def spread_map(heads, dtype):
    shape = (heads, heads * HEADDIM)
    return (iota(shape, 0) == iota(shape, 1) // HEADDIM).astype(dtype)


def widen(value):
    both = jnp.concatenate(split(value), axis=1)
    spread = spread_map(value.shape[1], BF16)
    return dot(both, jnp.concatenate([spread, spread], axis=0))


def head_sums(value):
    heads = value.shape[1] // HEADDIM
    shape = (heads * HEADDIM, heads)
    fold = (iota(shape, 0) // HEADDIM == iota(shape, 1)).astype(BF16)
    high, low = split(value)
    return dot(high, fold) + dot(low, fold)


def exponent_of(block):
    top = jnp.max(jnp.max(jnp.abs(block), axis=0, keepdims=True), axis=1, keepdims=True)
    return jnp.clip(jnp.floor(jnp.log(jnp.maximum(top, 1e-30)) * 1.4426950408889634), -90.0, 40.0)


def prep_kernel(dt_ref, par_ref, st_ref, size_ref, sig_ref, run_ref, runt_ref, reach_ref, tail_ref, bias_ref, edge_ref):
    tokens, heads = dt_ref.shape
    per = heads // GROUPS
    par = par_ref[...]
    a_log, dt_bias = par[0:1], par[1:2]
    decay = -jnp.exp(a_log)
    value = dt_ref[...].astype(F32) + dt_bias
    sizes = jnp.maximum(value, 0.0) + jnp.log1p(jnp.exp(-jnp.abs(value)))
    sigmoid = 1.0 / (1.0 + jnp.exp(-value))
    shape = (tokens, tokens)
    lower = (iota(shape, 0) >= iota(shape, 1)).astype(F32)
    upper = (iota(shape, 0) <= iota(shape, 1)).astype(F32)
    running = dot(lower, sizes * decay, precision=PRECISE)
    marks = st_ref[...]
    doc_row = dot(marks, upper)[0:1]
    doc_col = dot(lower, marks, ((1,), (1,)))[:, 0:1]
    doc_last = doc_row[:, tokens - 1 :]
    last = running[tokens - 1 :]
    reach = jnp.where(doc_col == 0.0, jnp.exp(running), 0.0)
    tail = jnp.where(doc_col == doc_last, jnp.exp(last - running), 0.0) * sizes
    linked = (doc_col == doc_row) & (iota(shape, 0) >= iota(shape, 1))
    bias_ref[...] = jnp.where(linked, 0.0, -1e30)
    turned = (running - jnp.log(sizes)).T
    through = jnp.where(doc_last == 0.0, last * 128.0, CUT)
    high = through.astype(BF16).astype(F32)
    mid = (through - high).astype(BF16).astype(F32)
    low = (through - high - mid).astype(BF16).astype(F32)
    keep = jnp.exp((high + mid + low) * (1.0 / 128.0))
    edge = jnp.concatenate([high, mid, low, keep, decay, decay, decay, decay], axis=0)
    for g in range(GROUPS):
        mine = slice(g * per, (g + 1) * per)
        size_ref[g] = sizes[:, mine]
        sig_ref[g] = sigmoid[:, mine]
        run_ref[g] = running[:, mine]
        runt_ref[g] = turned[mine]
        reach_ref[g] = reach[:, mine]
        tail_ref[g] = tail[:, mine]
        edge_ref[g] = edge[:, mine]


def prep(dt_raw, params, marks):
    tokens, heads = dt_raw.shape
    per = heads // GROUPS
    token_head = jax.ShapeDtypeStruct((GROUPS, tokens, per), F32)
    return pl.pallas_call(
        prep_kernel,
        out_shape=[
            token_head,
            token_head,
            token_head,
            jax.ShapeDtypeStruct((GROUPS, per, tokens), F32),
            token_head,
            token_head,
            jax.ShapeDtypeStruct((tokens, tokens), F32),
            jax.ShapeDtypeStruct((GROUPS, 8, per), F32),
        ],
        compiler_params=PARAMS,
        name="prep",
    )(dt_raw, params, marks)


def state_of(val_ref, proj_ref, scale_ref):
    high, low = split(val_ref[...].astype(F32) * widen(scale_ref[0]))
    proj = proj_ref[...]
    return dot(jnp.concatenate([proj, proj], axis=0), jnp.concatenate([high, low], axis=0), ((0,), (0,)))


def state_kernel(x_ref, w_ref, b_ref, c_ref, tail_ref, reach_ref, edge_ref, out_ref, piece_ref, power_ref):
    g = pl.program_id(0)
    messages, rows, _ = out_ref.shape
    part = (rows - 8) // 2
    fold = STATE // part
    per_group = messages // GROUPS
    row, lane = iota((8, LANES), 0), iota((8, LANES), 1)
    piece_ref[g] = dot(edge_ref[0].astype(BF16), spread_map(tail_ref.shape[2], BF16))
    powers = jnp.zeros((8, LANES), F32)
    for which, state in enumerate((state_of(x_ref, b_ref, tail_ref), state_of(w_ref, c_ref, reach_ref))):
        power = exponent_of(state)
        powers = jnp.where(lane == which * GROUPS + g, power, powers)
        state = state * jnp.exp2(TOP - power)
        for k in range(per_group):
            lanes = slice(k // fold * LANES, (k // fold + 1) * LANES)
            here = slice(k % fold * part, (k % fold + 1) * part)
            out_ref[g * per_group + k, which * part : (which + 1) * part] = state[here, lanes]

    @pl.when(g == 0)
    def _():
        power_ref[...] = powers

    @pl.when(g > 0)
    def _():
        power_ref[...] += powers

    @pl.when(g == GROUPS - 1)
    def _():
        side = jnp.where(row == 3, power_ref[...], 0.0)
        for k in range(messages):
            lanes = slice(k % per_group // fold * LANES, (k % per_group // fold + 1) * LANES)
            out_ref[k, 2 * part :] = jnp.where(row < 3, piece_ref[k // per_group, :, lanes], side)


def states(x, w, b, c, tail, reach, edge, parts):
    tokens, channels = x.shape
    wide = channels // GROUPS
    per = tail.shape[2]
    rows = 2 * STATE * channels // (parts * LANES) + 8
    values = pl.BlockSpec((tokens, wide), lambda g: (0, g))
    proj = pl.BlockSpec((tokens, STATE), lambda g: (0, g))
    small = pl.BlockSpec((1, tokens, per), lambda g: (g, 0, 0))
    return pl.pallas_call(
        state_kernel,
        grid=(GROUPS,),
        in_specs=[values, values, proj, proj, small, small, pl.BlockSpec((1, 8, per), lambda g: (g, 0, 0))],
        out_specs=pl.BlockSpec((parts, rows, LANES), lambda g: (0, 0, 0)),
        out_shape=jax.ShapeDtypeStruct((parts, rows, LANES), F32),
        scratch_shapes=[pltpu.VMEM((GROUPS, 8, wide), F32), pltpu.VMEM((8, LANES), F32)],
        compiler_params=PARAMS,
        cost_estimate=pl.CostEstimate(flops=8 * tokens * STATE * channels, bytes_accessed=7000000, transcendentals=0),
        name="states",
    )(x, w, b, c, tail, reach, edge)


def keep_of(pay_ref, i, part):
    side = pay_ref[i, 2 * part :]
    return jnp.exp((side[0:1] + side[1:2] + side[2:3]) * (1.0 / 128.0))


def lane_of(row, mask_ref, which):
    mine = mask_ref[mask_ref.shape[0] - 2 + which : mask_ref.shape[0] - 1 + which]
    return jnp.sum(row * mine, axis=1, keepdims=True)


def block_of(pay_ref, mask_ref, i, part, which):
    power = lane_of(pay_ref[i, 2 * part :][3:4], mask_ref, which)
    return pay_ref[i, which * part : (which + 1) * part] * jnp.exp2(power - TOP)


def total_kernel(pay_ref, mask_ref, out_ref):
    blocks, rows, _ = pay_ref.shape
    part = (rows - 8) // 2

    def step(k, carry):
        forth, back, through, most = carry
        late = blocks - 1 - k
        keep = keep_of(pay_ref, k, part)
        forth = keep * forth + block_of(pay_ref, mask_ref, k, part, 0)
        back = keep_of(pay_ref, late, part) * back + block_of(pay_ref, mask_ref, late, part, 1)
        return forth, back, through * keep, jnp.maximum(most, pay_ref[k, 2 * part :][3:4])

    zero = jnp.zeros((part, LANES), F32)
    one = jnp.ones((1, LANES), F32)
    forth, back, through, most = lax.fori_loop(0, blocks, step, (zero, zero, one, -1000.0 * one), unroll=8)
    row = iota((8, LANES), 0)
    side = jnp.where(row == 0, through, most)
    for which, state in enumerate((forth, back)):
        out_ref[which, 0:part] = state
        out_ref[which, part:] = side


def totals(pay, mask):
    part = (pay.shape[1] - 8) // 2
    return pl.pallas_call(
        total_kernel,
        out_shape=jax.ShapeDtypeStruct((2, part + 8, LANES), F32),
        compiler_params=PARAMS,
        cost_estimate=pl.CostEstimate(flops=2 * pay.size, bytes_accessed=4 * pay.size, transcendentals=0),
        name="totals",
    )(pay, mask)


def enter_kernel(pay_ref, own_ref, far_ref, mask_ref, out_ref, most_ref):
    blocks, rows, _ = pay_ref.shape
    part = (rows - 8) // 2
    others = far_ref.shape[0]
    most = own_ref[0, part:]
    for k in range(others):
        most = jnp.maximum(most, far_ref[k, 0, part:])
    most_ref[...] = most
    starts, scales = [], []
    for which in range(2):
        state = jnp.zeros((part, LANES), F32)
        for by in range(others, 0, -1):
            k = by - 1 if which == 0 else others - by
            far = far_ref[k, which]
            valid = mask_ref[which * others + by - 1 : which * others + by] > 0.0
            state = jnp.where(valid, far[0:part] + far[part : part + 1] * state, state)
        starts.append(state)
        scales.append(jnp.exp2(TOP + 2.0 - BITS - lane_of(most[1:2], mask_ref, which)))

    def step(k, carry):
        forth, back = carry
        late = blocks - 1 - k
        out_ref[k, 0:part] = forth * scales[0]
        out_ref[late, part:] = back * scales[1]
        forth = keep_of(pay_ref, k, part) * forth + block_of(pay_ref, mask_ref, k, part, 0)
        back = keep_of(pay_ref, late, part) * back + block_of(pay_ref, mask_ref, late, part, 1)
        return forth, back

    lax.fori_loop(0, blocks, step, tuple(starts), unroll=8)


def entering(pay, own, far, mask):
    blocks, rows, _ = pay.shape
    return pl.pallas_call(
        enter_kernel,
        out_shape=[jax.ShapeDtypeStruct((blocks, rows - 8, LANES), F32), jax.ShapeDtypeStruct((8, LANES), F32)],
        compiler_params=PARAMS,
        cost_estimate=pl.CostEstimate(flops=4 * pay.size, bytes_accessed=8 * pay.size, transcendentals=0),
        name="entering",
    )(pay, own, far, mask)


def inner_kernel(x_ref, w_ref, b_ref, c_ref, run_ref, runt_ref, bias_ref, skip_ref, y_ref, gx_ref, gb_ref, gc_ref, col_ref, diff_ref):
    tokens, wide = x_ref.shape
    heads = wide // HEADDIM
    pair = 2 * HEADDIM
    b_vals, c_vals = b_ref[...], c_ref[...]
    scores = dot(c_vals, b_vals, ((1,), (1,)))
    bias = bias_ref[...]
    run, runt = run_ref[0], runt_ref[0]
    first = iota((tokens, pair), 1) < HEADDIM
    grad_scores = jnp.zeros((tokens, tokens), F32)
    y_all, u_all = [], []
    for k in range(0, heads, 2):
        mine = slice(k * HEADDIM, (k + 2) * HEADDIM)
        x_pair, w_pair = x_ref[:, mine], w_ref[:, mine]
        x_two = jnp.concatenate([x_pair, x_pair], axis=0)
        w_two = jnp.concatenate([w_pair, w_pair], axis=0)
        ys, us = [], []
        for which in range(2):
            h = k + which
            keep = first if which == 0 else ~first
            weight = jnp.exp(run[:, h : h + 1] - runt[h : h + 1, :] + bias)
            cross = dot(jnp.where(keep, w_pair, jnp.zeros_like(w_pair)), x_pair, ((1,), (1,)))
            grad_scores = grad_scores + weight * cross
            high, low = split(weight * scores)
            ys.append(dot(jnp.concatenate([high, low], axis=1), x_two))
            us.append(dot(jnp.concatenate([high, low], axis=0), w_two, ((0,), (0,))))
        y_all.append(jnp.where(first, ys[0], ys[1]))
        u_all.append(jnp.where(first, us[0], us[1]))
    y_in = jnp.concatenate(y_all, axis=1)
    u_in = jnp.concatenate(u_all, axis=1)
    x_vals, w_vals = x_ref[...].astype(F32), w_ref[...].astype(F32)
    skip = skip_ref[0:1]
    y_ref[...] = y_in + skip * x_vals
    gx_ref[...] = u_in + skip * w_vals
    high, low = split(grad_scores)
    gc_ref[...] = dot(jnp.concatenate([high, low], axis=1), jnp.concatenate([b_vals, b_vals], axis=0))
    gb_ref[...] = dot(jnp.concatenate([high, low], axis=0), jnp.concatenate([c_vals, c_vals], axis=0), ((0,), (0,)))
    col = head_sums(x_vals * u_in)
    col_ref[0] = col
    diff_ref[0] = head_sums(w_vals * y_in) - col


def inner(x, w, b, c, run, runt, bias, skip):
    tokens, channels = x.shape
    wide = channels // GROUPS
    per = run.shape[2]
    values = pl.BlockSpec((tokens, wide), lambda g: (0, g))
    proj = pl.BlockSpec((tokens, STATE), lambda g: (0, g))
    small = pl.BlockSpec((1, tokens, per), lambda g: (g, 0, 0))
    return pl.pallas_call(
        inner_kernel,
        grid=(GROUPS,),
        in_specs=[
            values,
            values,
            proj,
            proj,
            small,
            pl.BlockSpec((1, per, tokens), lambda g: (g, 0, 0)),
            pl.BlockSpec((tokens, tokens), lambda g: (0, 0)),
            pl.BlockSpec((8, wide), lambda g: (0, g)),
        ],
        out_specs=[values, values, proj, proj, small, small],
        out_shape=[
            jax.ShapeDtypeStruct((tokens, channels), F32),
            jax.ShapeDtypeStruct((tokens, channels), F32),
            jax.ShapeDtypeStruct((tokens, GROUPS * STATE), F32),
            jax.ShapeDtypeStruct((tokens, GROUPS * STATE), F32),
            jax.ShapeDtypeStruct((GROUPS, tokens, per), F32),
            jax.ShapeDtypeStruct((GROUPS, tokens, per), F32),
        ],
        compiler_params=PARAMS,
        cost_estimate=pl.CostEstimate(flops=20_000_000_000, bytes_accessed=8_000_000, transcendentals=tokens * tokens * 64),
        name="inner",
    )(x, w, b, c, run, runt, bias, skip)


def state_from(pay_ref, most_ref, group, which):
    messages, rows, _ = pay_ref.shape
    part = rows // 2
    fold = STATE // part
    here = slice(which * part, (which + 1) * part)
    most = most_ref[1:2]
    mine = iota(most.shape, 1) == which * GROUPS + group
    power = jnp.sum(jnp.where(mine, most, 0.0), axis=1, keepdims=True)
    columns = []
    for first in range(0, messages, fold):
        columns.append(jnp.concatenate([pay_ref[first + k, here] for k in range(fold)], axis=0))
    return jnp.concatenate(columns, axis=1) * jnp.exp2(power - (TOP + 2.0 - BITS))


def carried_terms(state, values, scale_ref, proj_ref):
    wide = widen(scale_ref[0])
    proj = proj_ref[...]
    high, low = split(state)
    terms = dot(jnp.concatenate([proj, proj], axis=1), jnp.concatenate([high, low], axis=0)) * wide
    left_high, left_low = split(values * wide)
    last = ((1,), (1,))
    grad = dot(left_high, high, last) + (dot(left_high, low, last) + dot(left_low, high, last))
    return terms, grad, head_sums(terms * values)


def finish_kernel(
    pay_ref, most_ref, x_ref, w_ref, b_ref, c_ref, tail_ref, reach_ref, y_ref, gx_ref, gb_ref, gc_ref, col_ref, diff_ref, size_ref, sig_ref, edge_ref,
    mixed_ref, gradx_ref, dt_ref, gradb_ref, gradc_ref, rows_ref, cols_ref, met_ref,
):
    g = pl.program_id(0)
    tokens, _ = x_ref.shape
    enter, leave = state_from(pay_ref, most_ref, g, 0), state_from(pay_ref, most_ref, g, 1)
    terms, grad, rows = carried_terms(enter, w_ref[...].astype(F32), reach_ref, c_ref)
    mixed_ref[...] = (y_ref[...] + terms).astype(BF16)
    gradc_ref[...] = (gc_ref[...] + grad).astype(BF16)
    terms, grad, cols = carried_terms(leave, x_ref[...].astype(F32), tail_ref, b_ref)
    gradx_ref[...] = (gx_ref[...] + terms).astype(BF16)
    gradb_ref[...] = (gb_ref[...] + grad).astype(BF16)
    met = jnp.sum(enter * leave, axis=0, keepdims=True)
    rows_ref[g] = rows
    cols_ref[g] = cols
    met_ref[g] = head_sums(jnp.broadcast_to(met, (8, met.shape[1])))

    @pl.when(g == GROUPS - 1)
    def _():
        def whole(ref):
            return jnp.concatenate([ref[k] for k in range(GROUPS)], axis=1)

        edge = whole(edge_ref)
        keep, decay = edge[3:4], edge[4:5]
        shape = (tokens, tokens)
        from_here = (iota(shape, 0) <= iota(shape, 1)).astype(F32)
        before = (iota(shape, 0) > iota(shape, 1)).astype(F32)
        late = whole(cols_ref)
        grad_rate = (
            dot(from_here, whole(diff_ref) + whole(rows_ref), precision=PRECISE)
            + dot(before, late, precision=PRECISE)
            + keep * whole(met_ref)[0:1]
        )
        grad_size = (whole(col_ref) + late) / whole(size_ref) + decay * grad_rate
        dt_ref[...] = (grad_size * whole(sig_ref)).astype(BF16)


def finish(pay, most, x, w, b, c, tail, reach, y, gx, gb, gc, col, diff, size, sig, edge):
    tokens, channels = x.shape
    parts, rows, _ = pay.shape
    wide = channels // GROUPS
    per = tail.shape[2]
    values = pl.BlockSpec((tokens, wide), lambda g: (0, g))
    proj = pl.BlockSpec((tokens, STATE), lambda g: (0, g))
    small = pl.BlockSpec((1, tokens, per), lambda g: (g, 0, 0))
    every = pl.BlockSpec((GROUPS, tokens, per), lambda g: (0, 0, 0))
    return pl.pallas_call(
        finish_kernel,
        grid=(GROUPS,),
        in_specs=[
            pl.BlockSpec((parts // GROUPS, rows, LANES), lambda g: (g, 0, 0)),
            pl.BlockSpec((8, LANES), lambda g: (0, 0)),
            values, values, proj, proj, small, small, values, values, proj, proj, every, every, every, every,
            pl.BlockSpec((GROUPS, 8, per), lambda g: (0, 0, 0)),
        ],
        out_specs=[values, values, pl.BlockSpec((tokens, GROUPS * per), lambda g: (0, 0)), proj, proj],
        out_shape=[
            jax.ShapeDtypeStruct((tokens, channels), BF16),
            jax.ShapeDtypeStruct((tokens, channels), BF16),
            jax.ShapeDtypeStruct((tokens, GROUPS * per), BF16),
            jax.ShapeDtypeStruct((tokens, GROUPS * STATE), BF16),
            jax.ShapeDtypeStruct((tokens, GROUPS * STATE), BF16),
        ],
        scratch_shapes=[
            pltpu.VMEM((GROUPS, tokens, per), F32),
            pltpu.VMEM((GROUPS, tokens, per), F32),
            pltpu.VMEM((GROUPS, 8, per), F32),
        ],
        compiler_params=PARAMS,
        cost_estimate=pl.CostEstimate(flops=20 * tokens * STATE * channels, bytes_accessed=14_000_000, transcendentals=0),
        name="finish",
    )(pay, most, x, w, b, c, tail, reach, y, gx, gb, gc, col, diff, size, sig, edge)


GROUP = ("near", "head")


def exchanged(messages):
    sent = lax.all_to_all(messages.astype(jnp.float16), GROUP, split_axis=0, concat_axis=0, tiled=True)
    return sent.astype(F32)


def gathered(own, heads):
    parts = lax.axis_size("head")
    per_dev = own.shape[1]
    mine = lax.axis_index("head")
    whole = jnp.where(iota((8, 128), 1) // per_dev == mine, jnp.tile(own, (1, 128 // per_dev)), 0.0)
    whole = jnp.broadcast_to(whole[None], (parts, 8, 128))
    return lax.all_to_all(whole, "head", split_axis=0, concat_axis=0, tiled=True).sum(axis=0)[:, :heads]


def per_device(features, dt_raw, b_proj, c_proj, cotangent, starts, a_log, dt_bias, d_skip):
    parts = lax.axis_size(GROUP)
    tokens, heads = dt_raw.shape
    params = gathered(jnp.stack([a_log, dt_bias, d_skip] + [d_skip] * 5), heads)
    marks = lax.dynamic_slice(starts, (lax.axis_index("head") * tokens,), (tokens,)).astype(F32)
    marks = jnp.broadcast_to(marks[None], (8, tokens))
    skip = jnp.broadcast_to(jnp.repeat(params[2], HEADDIM)[None], (8, heads * HEADDIM))
    size, sig, run, runt, reach, tail, bias, edge = prep(dt_raw, params, marks)
    came = exchanged(states(features, cotangent, b_proj, c_proj, tail, reach, edge, parts))
    y, gx, gb, gc, col, diff = inner(features, cotangent, b_proj, c_proj, run, runt, bias, skip)
    count, here = lax.axis_size("far"), lax.axis_index("far")
    group = lax.axis_index(GROUP) * GROUPS // parts
    lane = jnp.arange(LANES)
    mask = [jnp.full((LANES,), here - by >= 0) for by in range(1, count)]
    mask += [jnp.full((LANES,), here + by < count) for by in range(1, count)]
    mask += [lane == group, lane == GROUPS + group]
    mask = jnp.stack(mask).astype(F32)
    total = totals(came, mask)
    far = [lax.ppermute(total, "far", [(p, (p + by) % count) for p in range(count)]) for by in range(1, count)]
    left, most = entering(came, total, jnp.stack(far), mask)
    return finish(
        exchanged(left), most, features, cotangent, b_proj, c_proj, tail, reach, y, gx, gb, gc, col, diff, size, sig, edge
    )


def solution(mesh):
    near = 8
    devices = mesh.devices
    seq, parts = devices.shape
    fine = jax.sharding.Mesh(devices.reshape(seq // near, near, parts), ("far",) + GROUP)
    token = P(("far",) + GROUP, None)
    return jax.shard_map(
        per_device,
        mesh=fine,
        in_specs=(token, token, token, token, token, P(("far", "near")), P("head"), P("head"), P("head")),
        out_specs=(token, token, token, token, token),
        check_vma=False,
    )
```

```python
import functools

import jax
import jax.numpy as jnp
from jax import lax
from jax.experimental import pallas as pl
from jax.experimental.pallas import tpu as pltpu
from jax.sharding import PartitionSpec as P

GROUPS = 4
HEADDIM = 64
STATE = 128
LANES = 128
BITS = 10.0
TOP = 13.0
CUT = -65000.0
F32 = jnp.float32
BF16 = jnp.bfloat16
PRECISE = lax.Precision.HIGHEST
PARAMS = pltpu.CompilerParams(vmem_limit_bytes=40 * 1024 * 1024)
STATES_VMEM = 62 * 1024 * 1024


def iota(shape, axis):
    return lax.broadcasted_iota(jnp.int32, shape, axis)


def split(value):
    high = value.astype(BF16)
    return high, (value - high.astype(F32)).astype(BF16)


def dot(a, b, dims=((1,), (0,)), precision=None):
    return lax.dot_general(a, b, (dims, ((), ())), precision=precision, preferred_element_type=F32)


def spread_map(heads, dtype):
    shape = (heads, heads * HEADDIM)
    return (iota(shape, 0) == iota(shape, 1) // HEADDIM).astype(dtype)


def widen(value):
    both = jnp.concatenate(split(value), axis=1)
    spread = spread_map(value.shape[1], BF16)
    return dot(both, jnp.concatenate([spread, spread], axis=0))


def head_sums(value):
    heads = value.shape[1] // HEADDIM
    shape = (heads * HEADDIM, heads)
    fold = (iota(shape, 0) // HEADDIM == iota(shape, 1)).astype(BF16)
    both = dot(jnp.concatenate(split(value), axis=0), fold)
    return both[: value.shape[0]] + both[value.shape[0] :]


def exponent_of(block):
    top = jnp.max(jnp.max(jnp.abs(block), axis=0, keepdims=True), axis=1, keepdims=True)
    return jnp.clip(jnp.floor(jnp.log(jnp.maximum(top, 1e-30)) * 1.4426950408889634), -90.0, 40.0)


def fill_tables(dt_ref, par_ref, st_ref, size_ref, sig_ref, run_ref, runt_ref, reach_ref, tail_ref, bias_ref, edge_ref):
    tokens, heads = dt_ref.shape
    per = heads // GROUPS
    par = par_ref[...]
    a_log, dt_bias = par[0:1], par[1:2]
    decay = -jnp.exp(a_log)
    value = dt_ref[...].astype(F32) + dt_bias
    sizes = jnp.maximum(value, 0.0) + jnp.log1p(jnp.exp(-jnp.abs(value)))
    sigmoid = 1.0 / (1.0 + jnp.exp(-value))
    shape = (tokens, tokens)
    lower = (iota(shape, 0) >= iota(shape, 1)).astype(F32)
    upper = (iota(shape, 0) <= iota(shape, 1)).astype(F32)
    running = dot(lower, sizes * decay, precision=PRECISE)
    marks = st_ref[...]
    doc_row = dot(marks, upper)[0:1]
    doc_col = dot(lower, marks, ((1,), (1,)))[:, 0:1]
    doc_last = doc_row[:, tokens - 1 :]
    last = running[tokens - 1 :]
    reach = jnp.where(doc_col == 0.0, jnp.exp(running), 0.0)
    tail = jnp.where(doc_col == doc_last, jnp.exp(last - running), 0.0) * sizes
    linked = (doc_col == doc_row) & (iota(shape, 0) >= iota(shape, 1))
    bias_ref[...] = jnp.where(linked, 0.0, -1e30)
    turned = (running - jnp.log(sizes)).T
    through = jnp.where(doc_last == 0.0, last * 128.0, CUT)
    high = through.astype(BF16).astype(F32)
    mid = (through - high).astype(BF16).astype(F32)
    low = (through - high - mid).astype(BF16).astype(F32)
    keep = jnp.exp((high + mid + low) * (1.0 / 128.0))
    edge = jnp.concatenate([high, mid, low, keep, decay, decay, decay, decay], axis=0)
    for g in range(GROUPS):
        mine = slice(g * per, (g + 1) * per)
        size_ref[g] = sizes[:, mine]
        sig_ref[g] = sigmoid[:, mine]
        run_ref[g] = running[:, mine]
        runt_ref[g] = turned[mine]
        reach_ref[g] = reach[:, mine]
        tail_ref[g] = tail[:, mine]
        edge_ref[g] = edge[:, mine]


def state_of(val_ref, proj_ref, scale):
    high, low = split(val_ref[...].astype(F32) * widen(scale))
    proj = proj_ref[...]
    return dot(jnp.concatenate([proj, proj], axis=0), jnp.concatenate([high, low], axis=0), ((0,), (0,)))


def state_kernel(
    x_ref, w_ref, b_ref, c_ref, dt_ref, par_ref, st_ref,
    out_ref, size_ref, sig_ref, run_ref, runt_ref, reach_ref, tail_ref, bias_ref, edge_ref,
    piece_ref, power_ref, spread_ref,
):
    g = pl.program_id(0)
    messages, rows, _ = out_ref.shape
    part = (rows - 8) // 2
    fold = STATE // part
    per_group = messages // GROUPS
    row, lane = iota((8, LANES), 0), iota((8, LANES), 1)

    @pl.when(g == 0)
    def _():
        fill_tables(
            dt_ref, par_ref, st_ref, size_ref, sig_ref, run_ref, runt_ref, reach_ref, tail_ref, bias_ref, edge_ref
        )
        power_ref[...] = jnp.zeros((8, LANES), F32)

    piece_ref[g] = dot(edge_ref[g].astype(BF16), spread_map(tail_ref.shape[2], BF16))
    spread = jnp.zeros((8, LANES), F32)
    for which, scale_ref in enumerate((tail_ref, reach_ref)):
        state = state_of((x_ref, w_ref)[which], (b_ref, c_ref)[which], scale_ref[g])
        power = exponent_of(state)
        spread = jnp.where(row == 4 + which, power, spread)
        power_ref[...] += jnp.where(lane == which * GROUPS + g, power, 0.0)
        state = state * jnp.exp2(TOP - power)
        for k in range(per_group):
            lanes = slice(k // fold * LANES, (k // fold + 1) * LANES)
            here = slice(k % fold * part, (k % fold + 1) * part)
            out_ref[g * per_group + k, which * part : (which + 1) * part] = state[here, lanes]
    spread_ref[g] = spread

    @pl.when(g == GROUPS - 1)
    def _():
        for k in range(messages):
            lanes = slice(k % per_group // fold * LANES, (k % per_group // fold + 1) * LANES)
            side = jnp.where(row == 3, power_ref[...], spread_ref[k // per_group])
            out_ref[k, 2 * part :] = jnp.where(row < 3, piece_ref[k // per_group, :, lanes], side)


def states(x, w, b, c, dt_raw, params, marks, parts):
    tokens, channels = x.shape
    wide = channels // GROUPS
    heads = dt_raw.shape[1]
    per = heads // GROUPS
    rows = 2 * STATE * channels // (parts * LANES) + 8
    values = pl.BlockSpec((tokens, wide), lambda g: (0, g))
    proj = pl.BlockSpec((tokens, STATE), lambda g: (0, g))

    def every(shape):
        return pl.BlockSpec(shape, lambda g: (0,) * len(shape))

    shapes = [(parts, rows, LANES)] + [(GROUPS, tokens, per)] * 3 + [(GROUPS, per, tokens)]
    shapes += [(GROUPS, tokens, per)] * 2 + [(tokens, tokens), (GROUPS, 8, per)]
    return pl.pallas_call(
        state_kernel,
        grid=(GROUPS,),
        in_specs=[values, values, proj, proj, every(dt_raw.shape), every(params.shape), every(marks.shape)],
        out_specs=[every(shape) for shape in shapes],
        out_shape=[jax.ShapeDtypeStruct(shape, F32) for shape in shapes],
        scratch_shapes=[
            pltpu.VMEM((GROUPS, 8, wide), F32),
            pltpu.VMEM((8, LANES), F32),
            pltpu.VMEM((GROUPS, 8, LANES), F32),
        ],
        compiler_params=pltpu.CompilerParams(vmem_limit_bytes=STATES_VMEM),
        cost_estimate=pl.CostEstimate(flops=8 * tokens * STATE * channels, bytes_accessed=7000000, transcendentals=0),
        name="states",
    )(x, w, b, c, dt_raw, params, marks)


def keep_of(pay_ref, i, part):
    side = pay_ref[i, 2 * part :]
    return jnp.exp((side[0:1] + side[1:2] + side[2:3]) * (1.0 / 128.0))


def lane_of(row, mask_ref, which):
    mine = mask_ref[mask_ref.shape[0] - 2 + which : mask_ref.shape[0] - 1 + which]
    return jnp.sum(row * mine, axis=1, keepdims=True)


def block_of(pay_ref, i, part, which):
    power = pay_ref[i, 2 * part :][4 + which : 5 + which]
    return pay_ref[i, which * part : (which + 1) * part] * jnp.exp2(power - TOP)


def total_kernel(pay_ref, out_ref):
    blocks, rows, _ = pay_ref.shape
    part = (rows - 8) // 2

    def step(k, carry):
        forth, back, through, most = carry
        late = blocks - 1 - k
        keep = keep_of(pay_ref, k, part)
        forth = keep * forth + block_of(pay_ref, k, part, 0)
        back = keep_of(pay_ref, late, part) * back + block_of(pay_ref, late, part, 1)
        return forth, back, through * keep, jnp.maximum(most, pay_ref[k, 2 * part :][3:4])

    zero = jnp.zeros((part, LANES), F32)
    one = jnp.ones((1, LANES), F32)
    forth, back, through, most = lax.fori_loop(0, blocks, step, (zero, zero, one, -1000.0 * one), unroll=8)
    row = iota((8, LANES), 0)
    side = jnp.where(row == 0, through, most)
    for which, state in enumerate((forth, back)):
        out_ref[which, 0:part] = state
        out_ref[which, part:] = side


def totals(pay):
    part = (pay.shape[1] - 8) // 2
    return pl.pallas_call(
        total_kernel,
        out_shape=jax.ShapeDtypeStruct((2, part + 8, LANES), F32),
        compiler_params=PARAMS,
        cost_estimate=pl.CostEstimate(flops=2 * pay.size, bytes_accessed=4 * pay.size, transcendentals=0),
        name="totals",
    )(pay)


def enter_kernel(pay_ref, own_ref, far_ref, mask_ref, out_ref, most_ref):
    blocks, rows, _ = pay_ref.shape
    part = (rows - 8) // 2
    others = far_ref.shape[0]
    most = own_ref[0, part:]
    for k in range(others):
        most = jnp.maximum(most, far_ref[k, 0, part:])
    most_ref[...] = most
    starts, scales = [], []
    for which in range(2):
        state = jnp.zeros((part, LANES), F32)
        for by in range(others, 0, -1):
            k = by - 1 if which == 0 else others - by
            far = far_ref[k, which]
            valid = mask_ref[which * others + by - 1 : which * others + by] > 0.0
            state = jnp.where(valid, far[0:part] + far[part : part + 1] * state, state)
        starts.append(state)
        scales.append(jnp.exp2(TOP + 2.0 - BITS - lane_of(most[1:2], mask_ref, which)))

    def step(k, carry):
        forth, back = carry
        late = blocks - 1 - k
        out_ref[k, 0:part] = forth * scales[0]
        out_ref[late, part:] = back * scales[1]
        forth = keep_of(pay_ref, k, part) * forth + block_of(pay_ref, k, part, 0)
        back = keep_of(pay_ref, late, part) * back + block_of(pay_ref, late, part, 1)
        return forth, back

    lax.fori_loop(0, blocks, step, tuple(starts), unroll=8)


def entering(pay, own, far, mask):
    blocks, rows, _ = pay.shape
    return pl.pallas_call(
        enter_kernel,
        out_shape=[jax.ShapeDtypeStruct((blocks, rows - 8, LANES), F32), jax.ShapeDtypeStruct((8, LANES), F32)],
        compiler_params=PARAMS,
        cost_estimate=pl.CostEstimate(flops=4 * pay.size, bytes_accessed=8 * pay.size, transcendentals=0),
        name="entering",
    )(pay, own, far, mask)


def inner_kernel(x_ref, w_ref, b_ref, c_ref, run_ref, runt_ref, bias_ref, skip_ref, y_ref, gx_ref, gb_ref, gc_ref, col_ref, diff_ref):
    tokens, wide = x_ref.shape
    heads = wide // HEADDIM
    pair = 2 * HEADDIM
    b_vals, c_vals = b_ref[...], c_ref[...]
    scores = dot(c_vals, b_vals, ((1,), (1,)))
    bias = bias_ref[...]
    run, runt = run_ref[0], runt_ref[0]
    first = iota((tokens, pair), 1) < HEADDIM
    grad_scores = jnp.zeros((tokens, tokens), F32)
    y_all, u_all = [], []
    for k in range(0, heads, 2):
        mine = slice(k * HEADDIM, (k + 2) * HEADDIM)
        x_pair, w_pair = x_ref[:, mine], w_ref[:, mine]
        x_two = jnp.concatenate([x_pair, x_pair], axis=0)
        w_two = jnp.concatenate([w_pair, w_pair], axis=0)
        ys, us = [], []
        for which in range(2):
            h = k + which
            keep = first if which == 0 else ~first
            weight = jnp.exp(run[:, h : h + 1] - runt[h : h + 1, :] + bias)
            cross = dot(jnp.where(keep, w_pair, jnp.zeros_like(w_pair)), x_pair, ((1,), (1,)))
            grad_scores = grad_scores + weight * cross
            high, low = split(weight * scores)
            ys.append(dot(jnp.concatenate([high, low], axis=1), x_two))
            us.append(dot(jnp.concatenate([high, low], axis=0), w_two, ((0,), (0,))))
        y_all.append(jnp.where(first, ys[0], ys[1]))
        u_all.append(jnp.where(first, us[0], us[1]))
    y_in = jnp.concatenate(y_all, axis=1)
    u_in = jnp.concatenate(u_all, axis=1)
    x_vals, w_vals = x_ref[...].astype(F32), w_ref[...].astype(F32)
    skip = skip_ref[0:1]
    y_ref[...] = y_in + skip * x_vals
    gx_ref[...] = u_in + skip * w_vals
    high, low = split(grad_scores)
    gc_ref[...] = dot(jnp.concatenate([high, low], axis=1), jnp.concatenate([b_vals, b_vals], axis=0))
    gb_ref[...] = dot(jnp.concatenate([high, low], axis=0), jnp.concatenate([c_vals, c_vals], axis=0), ((0,), (0,)))
    col = head_sums(x_vals * u_in)
    col_ref[0] = col
    diff_ref[0] = head_sums(w_vals * y_in) - col


def inner(x, w, b, c, run, runt, bias, skip):
    tokens, channels = x.shape
    wide = channels // GROUPS
    per = run.shape[2]
    values = pl.BlockSpec((tokens, wide), lambda g: (0, g))
    proj = pl.BlockSpec((tokens, STATE), lambda g: (0, g))
    small = pl.BlockSpec((1, tokens, per), lambda g: (g, 0, 0))
    return pl.pallas_call(
        inner_kernel,
        grid=(GROUPS,),
        in_specs=[
            values,
            values,
            proj,
            proj,
            small,
            pl.BlockSpec((1, per, tokens), lambda g: (g, 0, 0)),
            pl.BlockSpec((tokens, tokens), lambda g: (0, 0)),
            pl.BlockSpec((8, wide), lambda g: (0, g)),
        ],
        out_specs=[values, values, proj, proj, small, small],
        out_shape=[
            jax.ShapeDtypeStruct((tokens, channels), F32),
            jax.ShapeDtypeStruct((tokens, channels), F32),
            jax.ShapeDtypeStruct((tokens, GROUPS * STATE), F32),
            jax.ShapeDtypeStruct((tokens, GROUPS * STATE), F32),
            jax.ShapeDtypeStruct((GROUPS, tokens, per), F32),
            jax.ShapeDtypeStruct((GROUPS, tokens, per), F32),
        ],
        compiler_params=PARAMS,
        cost_estimate=pl.CostEstimate(flops=20_000_000_000, bytes_accessed=8_000_000, transcendentals=tokens * tokens * 64),
        name="inner",
    )(x, w, b, c, run, runt, bias, skip)


def state_from(pay_ref, most_ref, group, which):
    messages, rows, _ = pay_ref.shape
    part = rows // 2
    fold = STATE // part
    here = slice(which * part, (which + 1) * part)
    most = most_ref[1:2]
    mine = iota(most.shape, 1) == which * GROUPS + group
    power = jnp.sum(jnp.where(mine, most, 0.0), axis=1, keepdims=True)
    columns = []
    for first in range(0, messages, fold):
        columns.append(jnp.concatenate([pay_ref[first + k, here] for k in range(fold)], axis=0))
    return jnp.concatenate(columns, axis=1) * jnp.exp2(power - (TOP + 2.0 - BITS))


def carried_terms(state, values, scale_ref, proj_ref):
    wide = widen(scale_ref[0])
    proj = proj_ref[...]
    high, low = split(state)
    terms = dot(jnp.concatenate([proj, proj], axis=1), jnp.concatenate([high, low], axis=0)) * wide
    left_high, left_low = split(values * wide)
    last = ((1,), (1,))
    both = dot(jnp.concatenate([left_high, left_low], axis=0), high, last)
    tokens = values.shape[0]
    grad = both[:tokens] + (both[tokens:] + dot(left_high, low, last))
    return terms, grad, head_sums(terms * values)


def finish_kernel(
    pay_ref, most_ref, x_ref, w_ref, b_ref, c_ref, tail_ref, reach_ref, y_ref, gx_ref, gb_ref, gc_ref, col_ref, diff_ref, size_ref, sig_ref, edge_ref,
    mixed_ref, gradx_ref, dt_ref, gradb_ref, gradc_ref, rows_ref, cols_ref, met_ref,
):
    g = pl.program_id(0)
    tokens, _ = x_ref.shape
    enter, leave = state_from(pay_ref, most_ref, g, 0), state_from(pay_ref, most_ref, g, 1)
    terms, grad, rows = carried_terms(enter, w_ref[...].astype(F32), reach_ref, c_ref)
    mixed_ref[...] = (y_ref[...] + terms).astype(BF16)
    gradc_ref[...] = (gc_ref[...] + grad).astype(BF16)
    terms, grad, cols = carried_terms(leave, x_ref[...].astype(F32), tail_ref, b_ref)
    gradx_ref[...] = (gx_ref[...] + terms).astype(BF16)
    gradb_ref[...] = (gb_ref[...] + grad).astype(BF16)
    met = jnp.sum(enter * leave, axis=0, keepdims=True)
    rows_ref[g] = rows
    cols_ref[g] = cols
    met_ref[g] = head_sums(jnp.broadcast_to(met, (8, met.shape[1])))

    @pl.when(g == GROUPS - 1)
    def _():
        def whole(ref):
            return jnp.concatenate([ref[k] for k in range(GROUPS)], axis=1)

        edge = whole(edge_ref)
        keep, decay = edge[3:4], edge[4:5]
        shape = (tokens, tokens)
        from_here = (iota(shape, 0) <= iota(shape, 1)).astype(F32)
        before = (iota(shape, 0) > iota(shape, 1)).astype(F32)
        late = whole(cols_ref)
        grad_rate = (
            dot(from_here, whole(diff_ref) + whole(rows_ref), precision=PRECISE)
            + dot(before, late, precision=PRECISE)
            + keep * whole(met_ref)[0:1]
        )
        grad_size = (whole(col_ref) + late) / whole(size_ref) + decay * grad_rate
        dt_ref[...] = (grad_size * whole(sig_ref)).astype(BF16)


def finish(pay, most, x, w, b, c, tail, reach, y, gx, gb, gc, col, diff, size, sig, edge):
    tokens, channels = x.shape
    parts, rows, _ = pay.shape
    wide = channels // GROUPS
    per = tail.shape[2]
    values = pl.BlockSpec((tokens, wide), lambda g: (0, g))
    proj = pl.BlockSpec((tokens, STATE), lambda g: (0, g))
    small = pl.BlockSpec((1, tokens, per), lambda g: (g, 0, 0))
    every = pl.BlockSpec((GROUPS, tokens, per), lambda g: (0, 0, 0))
    return pl.pallas_call(
        finish_kernel,
        grid=(GROUPS,),
        in_specs=[
            pl.BlockSpec((parts // GROUPS, rows, LANES), lambda g: (g, 0, 0)),
            pl.BlockSpec((8, LANES), lambda g: (0, 0)),
            values, values, proj, proj, small, small, values, values, proj, proj, every, every, every, every,
            pl.BlockSpec((GROUPS, 8, per), lambda g: (0, 0, 0)),
        ],
        out_specs=[values, values, pl.BlockSpec((tokens, GROUPS * per), lambda g: (0, 0)), proj, proj],
        out_shape=[
            jax.ShapeDtypeStruct((tokens, channels), BF16),
            jax.ShapeDtypeStruct((tokens, channels), BF16),
            jax.ShapeDtypeStruct((tokens, GROUPS * per), BF16),
            jax.ShapeDtypeStruct((tokens, GROUPS * STATE), BF16),
            jax.ShapeDtypeStruct((tokens, GROUPS * STATE), BF16),
        ],
        scratch_shapes=[
            pltpu.VMEM((GROUPS, tokens, per), F32),
            pltpu.VMEM((GROUPS, tokens, per), F32),
            pltpu.VMEM((GROUPS, 8, per), F32),
        ],
        compiler_params=PARAMS,
        cost_estimate=pl.CostEstimate(flops=20 * tokens * STATE * channels, bytes_accessed=14_000_000, transcendentals=0),
        name="finish",
    )(pay, most, x, w, b, c, tail, reach, y, gx, gb, gc, col, diff, size, sig, edge)


GROUP = ("near", "head")


def exchanged(messages):
    sent = lax.all_to_all(messages.astype(jnp.float16), GROUP, split_axis=0, concat_axis=0, tiled=True)
    return sent.astype(F32)


def gathered(own, heads):
    parts = lax.axis_size("head")
    per_dev = own.shape[1]
    mine = lax.axis_index("head")
    whole = jnp.where(iota((8, 128), 1) // per_dev == mine, jnp.tile(own, (1, 128 // per_dev)), 0.0)
    whole = jnp.broadcast_to(whole[None], (parts, 8, 128))
    return lax.all_to_all(whole, "head", split_axis=0, concat_axis=0, tiled=True).sum(axis=0)[:, :heads]


def per_device(features, dt_raw, b_proj, c_proj, cotangent, starts, a_log, dt_bias, d_skip):
    parts = lax.axis_size(GROUP)
    tokens, heads = dt_raw.shape
    params = gathered(jnp.stack([a_log, dt_bias, d_skip] + [d_skip] * 5), heads)
    marks = lax.dynamic_slice(starts, (lax.axis_index("head") * tokens,), (tokens,)).astype(F32)
    marks = jnp.broadcast_to(marks[None], (8, tokens))
    skip = jnp.broadcast_to(jnp.repeat(params[2], HEADDIM)[None], (8, heads * HEADDIM))
    sent, size, sig, run, runt, reach, tail, bias, edge = states(
        features, cotangent, b_proj, c_proj, dt_raw, params, marks, parts
    )
    came = exchanged(sent)
    y, gx, gb, gc, col, diff = inner(features, cotangent, b_proj, c_proj, run, runt, bias, skip)
    count, here = lax.axis_size("far"), lax.axis_index("far")
    group = lax.axis_index(GROUP) * GROUPS // parts
    lane = jnp.arange(LANES)
    mask = [jnp.full((LANES,), here - by >= 0) for by in range(1, count)]
    mask += [jnp.full((LANES,), here + by < count) for by in range(1, count)]
    mask += [lane == group, lane == GROUPS + group]
    mask = jnp.stack(mask).astype(F32)
    total = totals(came)
    far = [lax.ppermute(total, "far", [(p, (p + by) % count) for p in range(count)]) for by in range(1, count)]
    left, most = entering(came, total, jnp.stack(far), mask)
    return finish(
        exchanged(left), most, features, cotangent, b_proj, c_proj, tail, reach, y, gx, gb, gc, col, diff, size, sig, edge
    )


def solution(mesh):
    near = 8
    devices = mesh.devices
    seq, parts = devices.shape
    fine = jax.sharding.Mesh(devices.reshape(seq // near, near, parts), ("far",) + GROUP)
    token = P(("far",) + GROUP, None)
    return jax.shard_map(
        per_device,
        mesh=fine,
        in_specs=(token, token, token, token, token, P(("far", "near")), P("head"), P("head"), P("head")),
        out_specs=(token, token, token, token, token),
        check_vma=False,
    )
```

```python
import functools

import jax
import jax.numpy as jnp
from jax import lax
from jax.experimental import pallas as pl
from jax.experimental.pallas import tpu as pltpu
from jax.sharding import PartitionSpec as P

GROUPS = 4
HEADDIM = 64
STATE = 128
LANES = 128
BITS = 10.0
TOP = 13.0
CUT = -65000.0
F32 = jnp.float32
BF16 = jnp.bfloat16
PRECISE = lax.Precision.HIGHEST
PARAMS = pltpu.CompilerParams(vmem_limit_bytes=24 * 1024 * 1024)


def iota(shape, axis):
    return lax.broadcasted_iota(jnp.int32, shape, axis)


def split(value):
    high = value.astype(BF16)
    return high, (value - high.astype(F32)).astype(BF16)


def dot(a, b, dims=((1,), (0,)), precision=None):
    return lax.dot_general(a, b, (dims, ((), ())), precision=precision, preferred_element_type=F32)


def spread_map(heads, dtype):
    shape = (heads, heads * HEADDIM)
    return (iota(shape, 0) == iota(shape, 1) // HEADDIM).astype(dtype)


def widen(value):
    both = jnp.concatenate(split(value), axis=1)
    spread = spread_map(value.shape[1], BF16)
    return dot(both, jnp.concatenate([spread, spread], axis=0))


def head_sums(value):
    heads = value.shape[1] // HEADDIM
    shape = (heads * HEADDIM, heads)
    fold = (iota(shape, 0) // HEADDIM == iota(shape, 1)).astype(BF16)
    high, low = split(value)
    return dot(high, fold) + dot(low, fold)


def exponent_of(block):
    top = jnp.max(jnp.max(jnp.abs(block), axis=0, keepdims=True), axis=1, keepdims=True)
    return jnp.clip(jnp.floor(jnp.log(jnp.maximum(top, 1e-30)) * 1.4426950408889634), -90.0, 40.0)


def prep_kernel(urgent, dt_ref, par_ref, st_ref, *outs):
    tokens, heads = dt_ref.shape
    per = heads // GROUPS
    par = par_ref[...]
    a_log, dt_bias = par[0:1], par[1:2]
    decay = -jnp.exp(a_log)
    value = dt_ref[...].astype(F32) + dt_bias
    sizes = jnp.maximum(value, 0.0) + jnp.log1p(jnp.exp(-jnp.abs(value)))
    shape = (tokens, tokens)
    lower = (iota(shape, 0) >= iota(shape, 1)).astype(F32)
    upper = (iota(shape, 0) <= iota(shape, 1)).astype(F32)
    running = dot(lower, sizes * decay, precision=PRECISE)
    marks = st_ref[...]
    doc_row = dot(marks, upper)[0:1]
    doc_col = dot(lower, marks, ((1,), (1,)))[:, 0:1]
    doc_last = doc_row[:, tokens - 1 :]
    groups = [slice(g * per, (g + 1) * per) for g in range(GROUPS)]
    if urgent:
        reach_ref, tail_ref, edge_ref = outs
        last = running[tokens - 1 :]
        reach = jnp.where(doc_col == 0.0, jnp.exp(running), 0.0)
        tail = jnp.where(doc_col == doc_last, jnp.exp(last - running), 0.0) * sizes
        through = jnp.where(doc_last == 0.0, last * 128.0, CUT)
        high = through.astype(BF16).astype(F32)
        mid = (through - high).astype(BF16).astype(F32)
        low = (through - high - mid).astype(BF16).astype(F32)
        keep = jnp.exp((high + mid + low) * (1.0 / 128.0))
        edge = jnp.concatenate([high, mid, low, keep, decay, decay, decay, decay], axis=0)
        for g, mine in enumerate(groups):
            reach_ref[g] = reach[:, mine]
            tail_ref[g] = tail[:, mine]
            edge_ref[g] = edge[:, mine]
    else:
        size_ref, sig_ref, run_ref, runt_ref, bias_ref = outs
        linked = (doc_col == doc_row) & (iota(shape, 0) >= iota(shape, 1))
        bias_ref[...] = jnp.where(linked, 0.0, -1e30)
        turned = (running - jnp.log(sizes)).T
        sigmoid = 1.0 / (1.0 + jnp.exp(-value))
        for g, mine in enumerate(groups):
            size_ref[g] = sizes[:, mine]
            sig_ref[g] = sigmoid[:, mine]
            run_ref[g] = running[:, mine]
            runt_ref[g] = turned[mine]


def prep(dt_raw, params, marks, urgent):
    tokens, heads = dt_raw.shape
    per = heads // GROUPS
    small = (GROUPS, tokens, per)
    if urgent:
        shapes = [small, small, (GROUPS, 8, per)]
    else:
        shapes = [small, small, small, (GROUPS, per, tokens), (tokens, tokens)]
    return pl.pallas_call(
        functools.partial(prep_kernel, urgent),
        out_shape=[jax.ShapeDtypeStruct(shape, F32) for shape in shapes],
        compiler_params=PARAMS,
        name="prep",
    )(dt_raw, params, marks)


def stage_kernel(*refs):
    half = len(refs) // 2
    for source, target in zip(refs[:half], refs[half:]):
        target[...] = source[...]


def staged(*arrays):
    return pl.pallas_call(
        stage_kernel,
        out_shape=[jax.ShapeDtypeStruct(array.shape, array.dtype) for array in arrays],
        compiler_params=PARAMS,
        cost_estimate=pl.CostEstimate(flops=0, bytes_accessed=2 * sum(2 * array.size for array in arrays), transcendentals=0),
        name="staged",
    )(*arrays)


def state_of(val_ref, proj_ref, scale_ref):
    high, low = split(val_ref[...].astype(F32) * widen(scale_ref[0]))
    proj = proj_ref[...]
    return dot(jnp.concatenate([proj, proj], axis=0), jnp.concatenate([high, low], axis=0), ((0,), (0,)))


def state_kernel(x_ref, w_ref, b_ref, c_ref, tail_ref, reach_ref, edge_ref, out_ref, piece_ref, power_ref, spread_ref):
    g = pl.program_id(0)
    messages, rows, _ = out_ref.shape
    part = (rows - 8) // 2
    fold = STATE // part
    per_group = messages // GROUPS
    row, lane = iota((8, LANES), 0), iota((8, LANES), 1)
    piece_ref[g] = dot(edge_ref[0].astype(BF16), spread_map(tail_ref.shape[2], BF16))
    powers = jnp.zeros((8, LANES), F32)
    spread = jnp.zeros((8, LANES), F32)
    for which, state in enumerate((state_of(x_ref, b_ref, tail_ref), state_of(w_ref, c_ref, reach_ref))):
        power = exponent_of(state)
        spread = jnp.where(row == 4 + which, power, spread)
        powers = jnp.where(lane == which * GROUPS + g, power, powers)
        state = state * jnp.exp2(TOP - power)
        for k in range(per_group):
            lanes = slice(k // fold * LANES, (k // fold + 1) * LANES)
            here = slice(k % fold * part, (k % fold + 1) * part)
            out_ref[g * per_group + k, which * part : (which + 1) * part] = state[here, lanes]
    spread_ref[g] = spread

    @pl.when(g == 0)
    def _():
        power_ref[...] = powers

    @pl.when(g > 0)
    def _():
        power_ref[...] += powers

    @pl.when(g == GROUPS - 1)
    def _():
        for k in range(messages):
            lanes = slice(k % per_group // fold * LANES, (k % per_group // fold + 1) * LANES)
            side = jnp.where(row == 3, power_ref[...], spread_ref[k // per_group])
            out_ref[k, 2 * part :] = jnp.where(row < 3, piece_ref[k // per_group, :, lanes], side)


def states(x, w, b, c, tail, reach, edge, parts):
    tokens, channels = x.shape
    wide = channels // GROUPS
    per = tail.shape[2]
    rows = 2 * STATE * channels // (parts * LANES) + 8
    values = pl.BlockSpec((tokens, wide), lambda g: (0, g))
    proj = pl.BlockSpec((tokens, STATE), lambda g: (0, g))
    small = pl.BlockSpec((1, tokens, per), lambda g: (g, 0, 0))
    return pl.pallas_call(
        state_kernel,
        grid=(GROUPS,),
        in_specs=[values, values, proj, proj, small, small, pl.BlockSpec((1, 8, per), lambda g: (g, 0, 0))],
        out_specs=pl.BlockSpec((parts, rows, LANES), lambda g: (0, 0, 0)),
        out_shape=jax.ShapeDtypeStruct((parts, rows, LANES), F32),
        scratch_shapes=[
            pltpu.VMEM((GROUPS, 8, wide), F32),
            pltpu.VMEM((8, LANES), F32),
            pltpu.VMEM((GROUPS, 8, LANES), F32),
        ],
        compiler_params=PARAMS,
        cost_estimate=pl.CostEstimate(flops=8 * tokens * STATE * channels, bytes_accessed=7000000, transcendentals=0),
        name="states",
    )(x, w, b, c, tail, reach, edge)


def keep_of(pay_ref, i, part):
    side = pay_ref[i, 2 * part :]
    return jnp.exp((side[0:1] + side[1:2] + side[2:3]) * (1.0 / 128.0))


def lane_of(row, mask_ref, which):
    mine = mask_ref[mask_ref.shape[0] - 2 + which : mask_ref.shape[0] - 1 + which]
    return jnp.sum(row * mine, axis=1, keepdims=True)


def block_of(pay_ref, i, part, which):
    power = pay_ref[i, 2 * part :][4 + which : 5 + which]
    return pay_ref[i, which * part : (which + 1) * part] * jnp.exp2(power - TOP)


def total_kernel(pay_ref, out_ref):
    blocks, rows, _ = pay_ref.shape
    part = (rows - 8) // 2

    def step(k, carry):
        forth, back, through, most = carry
        late = blocks - 1 - k
        keep = keep_of(pay_ref, k, part)
        forth = keep * forth + block_of(pay_ref, k, part, 0)
        back = keep_of(pay_ref, late, part) * back + block_of(pay_ref, late, part, 1)
        return forth, back, through * keep, jnp.maximum(most, pay_ref[k, 2 * part :][3:4])

    zero = jnp.zeros((part, LANES), F32)
    one = jnp.ones((1, LANES), F32)
    forth, back, through, most = lax.fori_loop(0, blocks, step, (zero, zero, one, -1000.0 * one), unroll=8)
    row = iota((8, LANES), 0)
    side = jnp.where(row == 0, through, most)
    for which, state in enumerate((forth, back)):
        out_ref[which, 0:part] = state
        out_ref[which, part:] = side


def totals(pay):
    part = (pay.shape[1] - 8) // 2
    return pl.pallas_call(
        total_kernel,
        out_shape=jax.ShapeDtypeStruct((2, part + 8, LANES), F32),
        compiler_params=PARAMS,
        cost_estimate=pl.CostEstimate(flops=2 * pay.size, bytes_accessed=4 * pay.size, transcendentals=0),
        name="totals",
    )(pay)


def enter_kernel(pay_ref, own_ref, far_ref, mask_ref, out_ref, most_ref):
    blocks, rows, _ = pay_ref.shape
    part = (rows - 8) // 2
    others = far_ref.shape[0]
    most = own_ref[0, part:]
    for k in range(others):
        most = jnp.maximum(most, far_ref[k, 0, part:])
    most_ref[...] = most
    starts, scales = [], []
    for which in range(2):
        state = jnp.zeros((part, LANES), F32)
        for by in range(others, 0, -1):
            k = by - 1 if which == 0 else others - by
            far = far_ref[k, which]
            valid = mask_ref[which * others + by - 1 : which * others + by] > 0.0
            state = jnp.where(valid, far[0:part] + far[part : part + 1] * state, state)
        starts.append(state)
        scales.append(jnp.exp2(TOP + 2.0 - BITS - lane_of(most[1:2], mask_ref, which)))

    def step(k, carry):
        forth, back = carry
        late = blocks - 1 - k
        out_ref[k, 0:part] = forth * scales[0]
        out_ref[late, part:] = back * scales[1]
        forth = keep_of(pay_ref, k, part) * forth + block_of(pay_ref, k, part, 0)
        back = keep_of(pay_ref, late, part) * back + block_of(pay_ref, late, part, 1)
        return forth, back

    lax.fori_loop(0, blocks, step, tuple(starts), unroll=8)


def entering(pay, own, far, mask):
    blocks, rows, _ = pay.shape
    return pl.pallas_call(
        enter_kernel,
        out_shape=[jax.ShapeDtypeStruct((blocks, rows - 8, LANES), F32), jax.ShapeDtypeStruct((8, LANES), F32)],
        compiler_params=PARAMS,
        cost_estimate=pl.CostEstimate(flops=4 * pay.size, bytes_accessed=8 * pay.size, transcendentals=0),
        name="entering",
    )(pay, own, far, mask)


def inner_kernel(x_ref, w_ref, b_ref, c_ref, run_ref, runt_ref, bias_ref, skip_ref, y_ref, gx_ref, gb_ref, gc_ref, col_ref, diff_ref):
    tokens, wide = x_ref.shape
    heads = wide // HEADDIM
    pair = 2 * HEADDIM
    b_vals, c_vals = b_ref[...], c_ref[...]
    scores = dot(c_vals, b_vals, ((1,), (1,)))
    bias = bias_ref[...]
    run, runt = run_ref[0], runt_ref[0]
    first = iota((tokens, pair), 1) < HEADDIM
    grad_scores = jnp.zeros((tokens, tokens), F32)
    y_all, u_all = [], []
    for k in range(0, heads, 2):
        mine = slice(k * HEADDIM, (k + 2) * HEADDIM)
        x_pair, w_pair = x_ref[:, mine], w_ref[:, mine]
        x_two = jnp.concatenate([x_pair, x_pair], axis=0)
        w_two = jnp.concatenate([w_pair, w_pair], axis=0)
        ys, us = [], []
        for which in range(2):
            h = k + which
            keep = first if which == 0 else ~first
            weight = jnp.exp(run[:, h : h + 1] - runt[h : h + 1, :] + bias)
            cross = dot(jnp.where(keep, w_pair, jnp.zeros_like(w_pair)), x_pair, ((1,), (1,)))
            grad_scores = grad_scores + weight * cross
            high, low = split(weight * scores)
            ys.append(dot(jnp.concatenate([high, low], axis=1), x_two))
            us.append(dot(jnp.concatenate([high, low], axis=0), w_two, ((0,), (0,))))
        y_all.append(jnp.where(first, ys[0], ys[1]))
        u_all.append(jnp.where(first, us[0], us[1]))
    y_in = jnp.concatenate(y_all, axis=1)
    u_in = jnp.concatenate(u_all, axis=1)
    x_vals, w_vals = x_ref[...].astype(F32), w_ref[...].astype(F32)
    skip = skip_ref[0:1]
    y_ref[...] = y_in + skip * x_vals
    gx_ref[...] = u_in + skip * w_vals
    high, low = split(grad_scores)
    gc_ref[...] = dot(jnp.concatenate([high, low], axis=1), jnp.concatenate([b_vals, b_vals], axis=0))
    gb_ref[...] = dot(jnp.concatenate([high, low], axis=0), jnp.concatenate([c_vals, c_vals], axis=0), ((0,), (0,)))
    col = head_sums(x_vals * u_in)
    col_ref[0] = col
    diff_ref[0] = head_sums(w_vals * y_in) - col


def inner(x, w, b, c, run, runt, bias, skip):
    tokens, channels = x.shape
    wide = channels // GROUPS
    per = run.shape[2]
    values = pl.BlockSpec((tokens, wide), lambda g: (0, g))
    proj = pl.BlockSpec((tokens, STATE), lambda g: (0, g))
    small = pl.BlockSpec((1, tokens, per), lambda g: (g, 0, 0))
    return pl.pallas_call(
        inner_kernel,
        grid=(GROUPS,),
        in_specs=[
            values,
            values,
            proj,
            proj,
            small,
            pl.BlockSpec((1, per, tokens), lambda g: (g, 0, 0)),
            pl.BlockSpec((tokens, tokens), lambda g: (0, 0)),
            pl.BlockSpec((8, wide), lambda g: (0, g)),
        ],
        out_specs=[values, values, proj, proj, small, small],
        out_shape=[
            jax.ShapeDtypeStruct((tokens, channels), F32),
            jax.ShapeDtypeStruct((tokens, channels), F32),
            jax.ShapeDtypeStruct((tokens, GROUPS * STATE), F32),
            jax.ShapeDtypeStruct((tokens, GROUPS * STATE), F32),
            jax.ShapeDtypeStruct((GROUPS, tokens, per), F32),
            jax.ShapeDtypeStruct((GROUPS, tokens, per), F32),
        ],
        compiler_params=PARAMS,
        cost_estimate=pl.CostEstimate(flops=20_000_000_000, bytes_accessed=8_000_000, transcendentals=tokens * tokens * 64),
        name="inner",
    )(x, w, b, c, run, runt, bias, skip)


def state_from(pay_ref, most_ref, group, which):
    messages, rows, _ = pay_ref.shape
    part = rows // 2
    fold = STATE // part
    here = slice(which * part, (which + 1) * part)
    most = most_ref[1:2]
    mine = iota(most.shape, 1) == which * GROUPS + group
    power = jnp.sum(jnp.where(mine, most, 0.0), axis=1, keepdims=True)
    columns = []
    for first in range(0, messages, fold):
        columns.append(jnp.concatenate([pay_ref[first + k, here] for k in range(fold)], axis=0))
    return jnp.concatenate(columns, axis=1) * jnp.exp2(power - (TOP + 2.0 - BITS))


def carried_terms(state, values, scale_ref, proj_ref):
    wide = widen(scale_ref[0])
    proj = proj_ref[...]
    high, low = split(state)
    terms = dot(jnp.concatenate([proj, proj], axis=1), jnp.concatenate([high, low], axis=0)) * wide
    left_high, left_low = split(values * wide)
    last = ((1,), (1,))
    grad = dot(left_high, high, last) + (dot(left_high, low, last) + dot(left_low, high, last))
    return terms, grad, head_sums(terms * values)


def finish_kernel(
    pay_ref, most_ref, x_ref, w_ref, b_ref, c_ref, tail_ref, reach_ref, y_ref, gx_ref, gb_ref, gc_ref, col_ref, diff_ref, size_ref, sig_ref, edge_ref,
    mixed_ref, gradx_ref, dt_ref, gradb_ref, gradc_ref, rows_ref, cols_ref, met_ref,
):
    g = pl.program_id(0)
    tokens, _ = x_ref.shape
    enter, leave = state_from(pay_ref, most_ref, g, 0), state_from(pay_ref, most_ref, g, 1)
    terms, grad, rows = carried_terms(enter, w_ref[...].astype(F32), reach_ref, c_ref)
    mixed_ref[...] = (y_ref[...] + terms).astype(BF16)
    gradc_ref[...] = (gc_ref[...] + grad).astype(BF16)
    terms, grad, cols = carried_terms(leave, x_ref[...].astype(F32), tail_ref, b_ref)
    gradx_ref[...] = (gx_ref[...] + terms).astype(BF16)
    gradb_ref[...] = (gb_ref[...] + grad).astype(BF16)
    met = jnp.sum(enter * leave, axis=0, keepdims=True)
    rows_ref[g] = rows
    cols_ref[g] = cols
    met_ref[g] = head_sums(jnp.broadcast_to(met, (8, met.shape[1])))

    @pl.when(g == GROUPS - 1)
    def _():
        def whole(ref):
            return jnp.concatenate([ref[k] for k in range(GROUPS)], axis=1)

        edge = whole(edge_ref)
        keep, decay = edge[3:4], edge[4:5]
        shape = (tokens, tokens)
        from_here = (iota(shape, 0) <= iota(shape, 1)).astype(F32)
        before = (iota(shape, 0) > iota(shape, 1)).astype(F32)
        late = whole(cols_ref)
        grad_rate = (
            dot(from_here, whole(diff_ref) + whole(rows_ref), precision=PRECISE)
            + dot(before, late, precision=PRECISE)
            + keep * whole(met_ref)[0:1]
        )
        grad_size = (whole(col_ref) + late) / whole(size_ref) + decay * grad_rate
        dt_ref[...] = (grad_size * whole(sig_ref)).astype(BF16)


def finish(pay, most, x, w, b, c, tail, reach, y, gx, gb, gc, col, diff, size, sig, edge):
    tokens, channels = x.shape
    parts, rows, _ = pay.shape
    wide = channels // GROUPS
    per = tail.shape[2]
    values = pl.BlockSpec((tokens, wide), lambda g: (0, g))
    proj = pl.BlockSpec((tokens, STATE), lambda g: (0, g))
    small = pl.BlockSpec((1, tokens, per), lambda g: (g, 0, 0))
    every = pl.BlockSpec((GROUPS, tokens, per), lambda g: (0, 0, 0))
    return pl.pallas_call(
        finish_kernel,
        grid=(GROUPS,),
        in_specs=[
            pl.BlockSpec((parts // GROUPS, rows, LANES), lambda g: (g, 0, 0)),
            pl.BlockSpec((8, LANES), lambda g: (0, 0)),
            values, values, proj, proj, small, small, values, values, proj, proj, every, every, every, every,
            pl.BlockSpec((GROUPS, 8, per), lambda g: (0, 0, 0)),
        ],
        out_specs=[values, values, pl.BlockSpec((tokens, GROUPS * per), lambda g: (0, 0)), proj, proj],
        out_shape=[
            jax.ShapeDtypeStruct((tokens, channels), BF16),
            jax.ShapeDtypeStruct((tokens, channels), BF16),
            jax.ShapeDtypeStruct((tokens, GROUPS * per), BF16),
            jax.ShapeDtypeStruct((tokens, GROUPS * STATE), BF16),
            jax.ShapeDtypeStruct((tokens, GROUPS * STATE), BF16),
        ],
        scratch_shapes=[
            pltpu.VMEM((GROUPS, tokens, per), F32),
            pltpu.VMEM((GROUPS, tokens, per), F32),
            pltpu.VMEM((GROUPS, 8, per), F32),
        ],
        compiler_params=PARAMS,
        cost_estimate=pl.CostEstimate(flops=20 * tokens * STATE * channels, bytes_accessed=14_000_000, transcendentals=0),
        name="finish",
    )(pay, most, x, w, b, c, tail, reach, y, gx, gb, gc, col, diff, size, sig, edge)


GROUP = ("near", "head")


def exchanged(messages):
    return lax.all_to_all(messages.astype(jnp.float16), GROUP, split_axis=0, concat_axis=0, tiled=True)


def message_kernel(mine_ref, a_ref, bias_ref, skip_ref, out_ref):
    row, lane = iota((8, LANES), 0), iota((8, LANES), 1)
    per_dev = a_ref.shape[0]
    value = jnp.zeros((8, LANES), F32)
    for k, ref in enumerate((a_ref, bias_ref, skip_ref)):
        for i in range(per_dev):
            value = jnp.where((row == k) & (lane == mine_ref[0] * per_dev + i), ref[i], value)
    out_ref[...] = jnp.broadcast_to(value[None], out_ref.shape)


def gathered(a_log, dt_bias, d_skip, heads):
    parts = lax.axis_size("head")
    message = pl.pallas_call(
        message_kernel,
        in_specs=[pl.BlockSpec(memory_space=pltpu.SMEM)] * 4,
        out_shape=jax.ShapeDtypeStruct((parts, 8, LANES), F32),
        compiler_params=PARAMS,
        name="message",
    )(lax.axis_index("head").reshape(1), a_log, dt_bias, d_skip)
    return lax.all_to_all(message, "head", split_axis=0, concat_axis=0, tiled=True).sum(axis=0)[:, :heads]


def per_device(features, dt_raw, b_proj, c_proj, cotangent, starts, a_log, dt_bias, d_skip):
    parts = lax.axis_size(GROUP)
    tokens, heads = dt_raw.shape
    params = gathered(a_log, dt_bias, d_skip, heads)
    marks = lax.dynamic_slice(starts, (lax.axis_index("head") * tokens,), (tokens,)).astype(F32)
    marks = jnp.broadcast_to(marks[None], (8, tokens))
    skip = jnp.broadcast_to(jnp.repeat(params[2], HEADDIM)[None], (8, heads * HEADDIM))
    reach, tail, edge = prep(dt_raw, params, marks, True)
    size, sig, run, runt, bias = prep(dt_raw, params, marks, False)
    near = staged(features, cotangent, b_proj, c_proj)
    came = exchanged(states(*near, tail, reach, edge, parts))
    y, gx, gb, gc, col, diff = inner(features, cotangent, b_proj, c_proj, run, runt, bias, skip)
    count, here = lax.axis_size("far"), lax.axis_index("far")
    group = lax.axis_index(GROUP) * GROUPS // parts
    lane = jnp.arange(LANES)
    mask = [jnp.full((LANES,), here - by >= 0) for by in range(1, count)]
    mask += [jnp.full((LANES,), here + by < count) for by in range(1, count)]
    mask += [lane == group, lane == GROUPS + group]
    mask = jnp.stack(mask).astype(F32)
    total = totals(came.astype(F32))
    came, total = lax.optimization_barrier((came, total))
    far = [lax.ppermute(total, "far", [(p, (p + by) % count) for p in range(count)]) for by in range(1, count)]
    left, most = entering(came.astype(F32), total, jnp.stack(far), mask)
    return finish(
        exchanged(left).astype(F32), most, features, cotangent, b_proj, c_proj, tail, reach, y, gx, gb, gc, col, diff, size, sig, edge
    )


def solution(mesh):
    near = 8
    devices = mesh.devices
    seq, parts = devices.shape
    fine = jax.sharding.Mesh(devices.reshape(seq // near, near, parts), ("far",) + GROUP)
    token = P(("far",) + GROUP, None)
    return jax.shard_map(
        per_device,
        mesh=fine,
        in_specs=(token, token, token, token, token, P(("far", "near")), P("head"), P("head"), P("head")),
        out_specs=(token, token, token, token, token),
        check_vma=False,
    )
```

```python
import functools

import jax
import jax.numpy as jnp
from jax import lax
from jax.experimental import pallas as pl
from jax.experimental.pallas import tpu as pltpu
from jax.sharding import PartitionSpec as P

GROUPS = 4
HEADDIM = 64
STATE = 128
LANES = 128
BITS = 10.0
TOP = 13.0
CUT = -65000.0
F32 = jnp.float32
BF16 = jnp.bfloat16
PRECISE = lax.Precision.HIGHEST
PARAMS = pltpu.CompilerParams(vmem_limit_bytes=24 * 1024 * 1024)


def iota(shape, axis):
    return lax.broadcasted_iota(jnp.int32, shape, axis)


def split(value):
    high = value.astype(BF16)
    return high, (value - high.astype(F32)).astype(BF16)


def dot(a, b, dims=((1,), (0,)), precision=None):
    return lax.dot_general(a, b, (dims, ((), ())), precision=precision, preferred_element_type=F32)


def spread_map(heads, dtype):
    shape = (heads, heads * HEADDIM)
    return (iota(shape, 0) == iota(shape, 1) // HEADDIM).astype(dtype)


def widen(value):
    both = jnp.concatenate(split(value), axis=1)
    spread = spread_map(value.shape[1], BF16)
    return dot(both, jnp.concatenate([spread, spread], axis=0))


def head_sums(value):
    heads = value.shape[1] // HEADDIM
    shape = (heads * HEADDIM, heads)
    fold = (iota(shape, 0) // HEADDIM == iota(shape, 1)).astype(BF16)
    high, low = split(value)
    return dot(high, fold) + dot(low, fold)


def exponent_of(block):
    top = jnp.max(jnp.max(jnp.abs(block), axis=0, keepdims=True), axis=1, keepdims=True)
    return jnp.clip(jnp.floor(jnp.log(jnp.maximum(top, 1e-30)) * 1.4426950408889634), -90.0, 40.0)


def prep_kernel(urgent, dt_ref, par_ref, st_ref, *outs):
    tokens, heads = dt_ref.shape
    per = heads // GROUPS
    par = par_ref[...]
    a_log, dt_bias = par[0:1], par[1:2]
    decay = -jnp.exp(a_log)
    value = dt_ref[...].astype(F32) + dt_bias
    sizes = jnp.maximum(value, 0.0) + jnp.log1p(jnp.exp(-jnp.abs(value)))
    shape = (tokens, tokens)
    lower = (iota(shape, 0) >= iota(shape, 1)).astype(F32)
    upper = (iota(shape, 0) <= iota(shape, 1)).astype(F32)
    running = dot(lower, sizes * decay, precision=PRECISE)
    marks = st_ref[...]
    doc_row = dot(marks, upper)[0:1]
    doc_col = dot(lower, marks, ((1,), (1,)))[:, 0:1]
    doc_last = doc_row[:, tokens - 1 :]
    groups = [slice(g * per, (g + 1) * per) for g in range(GROUPS)]
    if urgent:
        reach_ref, tail_ref, edge_ref = outs
        last = running[tokens - 1 :]
        reach = jnp.where(doc_col == 0.0, jnp.exp(running), 0.0)
        tail = jnp.where(doc_col == doc_last, jnp.exp(last - running), 0.0) * sizes
        through = jnp.where(doc_last == 0.0, last * 128.0, CUT)
        high = through.astype(BF16).astype(F32)
        mid = (through - high).astype(BF16).astype(F32)
        low = (through - high - mid).astype(BF16).astype(F32)
        keep = jnp.exp((high + mid + low) * (1.0 / 128.0))
        edge = jnp.concatenate([high, mid, low, keep, decay, decay, decay, decay], axis=0)
        for g, mine in enumerate(groups):
            reach_ref[g] = reach[:, mine]
            tail_ref[g] = tail[:, mine]
            edge_ref[g] = edge[:, mine]
    else:
        size_ref, sig_ref, run_ref, runt_ref, bias_ref = outs
        linked = (doc_col == doc_row) & (iota(shape, 0) >= iota(shape, 1))
        bias_ref[...] = jnp.where(linked, 0.0, -1e30)
        turned = (running - jnp.log(sizes)).T
        sigmoid = 1.0 / (1.0 + jnp.exp(-value))
        for g, mine in enumerate(groups):
            size_ref[g] = sizes[:, mine]
            sig_ref[g] = sigmoid[:, mine]
            run_ref[g] = running[:, mine]
            runt_ref[g] = turned[mine]


def prep(dt_raw, params, marks, urgent):
    tokens, heads = dt_raw.shape
    per = heads // GROUPS
    small = (GROUPS, tokens, per)
    if urgent:
        shapes = [small, small, (GROUPS, 8, per)]
    else:
        shapes = [small, small, small, (GROUPS, per, tokens), (tokens, tokens)]
    return pl.pallas_call(
        functools.partial(prep_kernel, urgent),
        out_shape=[jax.ShapeDtypeStruct(shape, F32) for shape in shapes],
        compiler_params=PARAMS,
        name="prep",
    )(dt_raw, params, marks)


def stage_kernel(*refs):
    half = len(refs) // 2
    for source, target in zip(refs[:half], refs[half:]):
        target[...] = source[...]


def staged(*arrays):
    return pl.pallas_call(
        stage_kernel,
        out_shape=[jax.ShapeDtypeStruct(array.shape, array.dtype) for array in arrays],
        compiler_params=PARAMS,
        cost_estimate=pl.CostEstimate(flops=0, bytes_accessed=2 * sum(2 * array.size for array in arrays), transcendentals=0),
        name="staged",
    )(*arrays)


def state_of(values, proj, scale):
    high, low = split(values.astype(F32) * widen(scale))
    return dot(jnp.concatenate([proj, proj], axis=0), jnp.concatenate([high, low], axis=0), ((0,), (0,)))


def state_kernel(x_ref, w_ref, b_ref, c_ref, tail_ref, reach_ref, edge_ref, out_ref):
    messages, rows, _ = out_ref.shape
    wide = x_ref.shape[1] // GROUPS
    part = (rows - 8) // 2
    fold = STATE // part
    per_group = messages // GROUPS
    row, lane = iota((8, LANES), 0), iota((8, LANES), 1)
    all_powers = jnp.zeros((8, LANES), F32)
    sides = []
    for g in range(GROUPS):
        mine, own = slice(g * wide, (g + 1) * wide), slice(g * STATE, (g + 1) * STATE)
        pieces = dot(edge_ref[g].astype(BF16), spread_map(tail_ref.shape[2], BF16))
        spread = jnp.zeros((8, LANES), F32)
        for which, (val_ref, proj_ref, scale_ref) in enumerate(
            ((x_ref, b_ref, tail_ref), (w_ref, c_ref, reach_ref))
        ):
            state = state_of(val_ref[:, mine], proj_ref[:, own], scale_ref[g])
            power = exponent_of(state)
            spread = jnp.where(row == 4 + which, power, spread)
            all_powers = jnp.where(lane == which * GROUPS + g, power, all_powers)
            state = state * jnp.exp2(TOP - power)
            for k in range(per_group):
                lanes = slice(k // fold * LANES, (k // fold + 1) * LANES)
                here = slice(k % fold * part, (k % fold + 1) * part)
                out_ref[g * per_group + k, which * part : (which + 1) * part] = state[here, lanes]
        sides.append((pieces, spread))
    for g, (pieces, spread) in enumerate(sides):
        side = jnp.where(row == 3, all_powers, spread)
        for k in range(per_group):
            lanes = slice(k // fold * LANES, (k // fold + 1) * LANES)
            out_ref[g * per_group + k, 2 * part :] = jnp.where(row < 3, pieces[:, lanes], side)


def states(x, w, b, c, tail, reach, edge, parts):
    tokens, channels = x.shape
    rows = 2 * STATE * channels // (parts * LANES) + 8
    return pl.pallas_call(
        state_kernel,
        out_shape=jax.ShapeDtypeStruct((parts, rows, LANES), F32),
        compiler_params=PARAMS,
        cost_estimate=pl.CostEstimate(flops=8 * tokens * STATE * channels, bytes_accessed=7000000, transcendentals=0),
        name="states",
    )(x, w, b, c, tail, reach, edge)


def keep_of(pay_ref, i, part):
    side = pay_ref[i, 2 * part :]
    return jnp.exp((side[0:1] + side[1:2] + side[2:3]) * (1.0 / 128.0))


def lane_of(row, mask_ref, which):
    mine = mask_ref[mask_ref.shape[0] - 2 + which : mask_ref.shape[0] - 1 + which]
    return jnp.sum(row * mine, axis=1, keepdims=True)


def block_of(pay_ref, i, part, which):
    power = pay_ref[i, 2 * part :][4 + which : 5 + which]
    return pay_ref[i, which * part : (which + 1) * part] * jnp.exp2(power - TOP)


def total_kernel(pay_ref, out_ref):
    blocks, rows, _ = pay_ref.shape
    part = (rows - 8) // 2

    def step(k, carry):
        forth, back, through, most = carry
        late = blocks - 1 - k
        keep = keep_of(pay_ref, k, part)
        forth = keep * forth + block_of(pay_ref, k, part, 0)
        back = keep_of(pay_ref, late, part) * back + block_of(pay_ref, late, part, 1)
        return forth, back, through * keep, jnp.maximum(most, pay_ref[k, 2 * part :][3:4])

    zero = jnp.zeros((part, LANES), F32)
    one = jnp.ones((1, LANES), F32)
    forth, back, through, most = lax.fori_loop(0, blocks, step, (zero, zero, one, -1000.0 * one), unroll=8)
    row = iota((8, LANES), 0)
    side = jnp.where(row == 0, through, most)
    for which, state in enumerate((forth, back)):
        out_ref[which, 0:part] = state
        out_ref[which, part:] = side


def totals(pay):
    part = (pay.shape[1] - 8) // 2
    return pl.pallas_call(
        total_kernel,
        out_shape=jax.ShapeDtypeStruct((2, part + 8, LANES), F32),
        compiler_params=PARAMS,
        cost_estimate=pl.CostEstimate(flops=2 * pay.size, bytes_accessed=4 * pay.size, transcendentals=0),
        name="totals",
    )(pay)


def enter_kernel(pay_ref, own_ref, far_ref, mask_ref, out_ref, most_ref):
    blocks, rows, _ = pay_ref.shape
    part = (rows - 8) // 2
    others = far_ref.shape[0]
    most = own_ref[0, part:]
    for k in range(others):
        most = jnp.maximum(most, far_ref[k, 0, part:])
    most_ref[...] = most
    starts, scales = [], []
    for which in range(2):
        state = jnp.zeros((part, LANES), F32)
        for by in range(others, 0, -1):
            k = by - 1 if which == 0 else others - by
            far = far_ref[k, which]
            valid = mask_ref[which * others + by - 1 : which * others + by] > 0.0
            state = jnp.where(valid, far[0:part] + far[part : part + 1] * state, state)
        starts.append(state)
        scales.append(jnp.exp2(TOP + 2.0 - BITS - lane_of(most[1:2], mask_ref, which)))

    def step(k, carry):
        forth, back = carry
        late = blocks - 1 - k
        out_ref[k, 0:part] = forth * scales[0]
        out_ref[late, part:] = back * scales[1]
        forth = keep_of(pay_ref, k, part) * forth + block_of(pay_ref, k, part, 0)
        back = keep_of(pay_ref, late, part) * back + block_of(pay_ref, late, part, 1)
        return forth, back

    lax.fori_loop(0, blocks, step, tuple(starts), unroll=8)


def entering(pay, own, far, mask):
    blocks, rows, _ = pay.shape
    return pl.pallas_call(
        enter_kernel,
        out_shape=[jax.ShapeDtypeStruct((blocks, rows - 8, LANES), F32), jax.ShapeDtypeStruct((8, LANES), F32)],
        compiler_params=PARAMS,
        cost_estimate=pl.CostEstimate(flops=4 * pay.size, bytes_accessed=8 * pay.size, transcendentals=0),
        name="entering",
    )(pay, own, far, mask)


def inner_kernel(x_ref, w_ref, b_ref, c_ref, run_ref, runt_ref, bias_ref, skip_ref, y_ref, gx_ref, gb_ref, gc_ref, col_ref, diff_ref):
    tokens, wide = x_ref.shape
    heads = wide // HEADDIM
    pair = 2 * HEADDIM
    b_vals, c_vals = b_ref[...], c_ref[...]
    scores = dot(c_vals, b_vals, ((1,), (1,)))
    bias = bias_ref[...]
    run, runt = run_ref[0], runt_ref[0]
    first = iota((tokens, pair), 1) < HEADDIM
    grad_scores = jnp.zeros((tokens, tokens), F32)
    y_all, u_all = [], []
    for k in range(0, heads, 2):
        mine = slice(k * HEADDIM, (k + 2) * HEADDIM)
        x_pair, w_pair = x_ref[:, mine], w_ref[:, mine]
        x_two = jnp.concatenate([x_pair, x_pair], axis=0)
        w_two = jnp.concatenate([w_pair, w_pair], axis=0)
        ys, us = [], []
        for which in range(2):
            h = k + which
            keep = first if which == 0 else ~first
            weight = jnp.exp(run[:, h : h + 1] - runt[h : h + 1, :] + bias)
            cross = dot(jnp.where(keep, w_pair, jnp.zeros_like(w_pair)), x_pair, ((1,), (1,)))
            grad_scores = grad_scores + weight * cross
            high, low = split(weight * scores)
            ys.append(dot(jnp.concatenate([high, low], axis=1), x_two))
            us.append(dot(jnp.concatenate([high, low], axis=0), w_two, ((0,), (0,))))
        y_all.append(jnp.where(first, ys[0], ys[1]))
        u_all.append(jnp.where(first, us[0], us[1]))
    y_in = jnp.concatenate(y_all, axis=1)
    u_in = jnp.concatenate(u_all, axis=1)
    x_vals, w_vals = x_ref[...].astype(F32), w_ref[...].astype(F32)
    skip = skip_ref[0:1]
    y_ref[...] = y_in + skip * x_vals
    gx_ref[...] = u_in + skip * w_vals
    high, low = split(grad_scores)
    gc_ref[...] = dot(jnp.concatenate([high, low], axis=1), jnp.concatenate([b_vals, b_vals], axis=0))
    gb_ref[...] = dot(jnp.concatenate([high, low], axis=0), jnp.concatenate([c_vals, c_vals], axis=0), ((0,), (0,)))
    col = head_sums(x_vals * u_in)
    col_ref[0] = col
    diff_ref[0] = head_sums(w_vals * y_in) - col


def inner(x, w, b, c, run, runt, bias, skip):
    tokens, channels = x.shape
    wide = channels // GROUPS
    per = run.shape[2]
    values = pl.BlockSpec((tokens, wide), lambda g: (0, g))
    proj = pl.BlockSpec((tokens, STATE), lambda g: (0, g))
    small = pl.BlockSpec((1, tokens, per), lambda g: (g, 0, 0))
    return pl.pallas_call(
        inner_kernel,
        grid=(GROUPS,),
        in_specs=[
            values,
            values,
            proj,
            proj,
            small,
            pl.BlockSpec((1, per, tokens), lambda g: (g, 0, 0)),
            pl.BlockSpec((tokens, tokens), lambda g: (0, 0)),
            pl.BlockSpec((8, wide), lambda g: (0, g)),
        ],
        out_specs=[values, values, proj, proj, small, small],
        out_shape=[
            jax.ShapeDtypeStruct((tokens, channels), F32),
            jax.ShapeDtypeStruct((tokens, channels), F32),
            jax.ShapeDtypeStruct((tokens, GROUPS * STATE), F32),
            jax.ShapeDtypeStruct((tokens, GROUPS * STATE), F32),
            jax.ShapeDtypeStruct((GROUPS, tokens, per), F32),
            jax.ShapeDtypeStruct((GROUPS, tokens, per), F32),
        ],
        compiler_params=PARAMS,
        cost_estimate=pl.CostEstimate(flops=20_000_000_000, bytes_accessed=8_000_000, transcendentals=tokens * tokens * 64),
        name="inner",
    )(x, w, b, c, run, runt, bias, skip)


def state_from(pay_ref, most_ref, group, which):
    messages, rows, _ = pay_ref.shape
    per_group = messages // GROUPS
    part = rows // 2
    fold = STATE // part
    here = slice(which * part, (which + 1) * part)
    lane = which * GROUPS + group
    power = most_ref[1:2, lane : lane + 1]
    columns = []
    for first in range(group * per_group, (group + 1) * per_group, fold):
        columns.append(jnp.concatenate([pay_ref[first + k, here] for k in range(fold)], axis=0))
    return jnp.concatenate(columns, axis=1) * jnp.exp2(power - (TOP + 2.0 - BITS))


def carried_terms(state, values, scale, proj):
    wide = widen(scale)
    high, low = split(state)
    terms = dot(jnp.concatenate([proj, proj], axis=1), jnp.concatenate([high, low], axis=0)) * wide
    left_high, left_low = split(values * wide)
    last = ((1,), (1,))
    both = dot(jnp.concatenate([left_high, left_low], axis=0), high, last)
    tokens = values.shape[0]
    grad = both[:tokens] + (both[tokens:] + dot(left_high, low, last))
    return terms, grad, head_sums(terms * values)


def finish_kernel(
    pay_ref, most_ref, x_ref, w_ref, b_ref, c_ref, tail_ref, reach_ref, y_ref, gx_ref, gb_ref, gc_ref, col_ref, diff_ref, size_ref, sig_ref, edge_ref,
    mixed_out, gradx_out, dt_ref, gradb_out, gradc_out, mixed_ref, gradx_ref, gradb_ref, gradc_ref, sems,
):
    tokens, channels = x_ref.shape
    wide = channels // GROUPS
    rows, cols, met, copies = [], [], [], []
    for g in range(GROUPS):
        mine, own = slice(g * wide, (g + 1) * wide), slice(g * STATE, (g + 1) * STATE)
        enter, leave = state_from(pay_ref, most_ref, g, 0), state_from(pay_ref, most_ref, g, 1)
        terms, grad, sums = carried_terms(enter, w_ref[:, mine].astype(F32), reach_ref[g], c_ref[:, own])
        mixed_ref[:, mine] = (y_ref[:, mine] + terms).astype(BF16)
        gradc_ref[:, own] = (gc_ref[:, own] + grad).astype(BF16)
        rows.append(sums)
        terms, grad, sums = carried_terms(leave, x_ref[:, mine].astype(F32), tail_ref[g], b_ref[:, own])
        gradx_ref[:, mine] = (gx_ref[:, mine] + terms).astype(BF16)
        gradb_ref[:, own] = (gb_ref[:, own] + grad).astype(BF16)
        cols.append(sums)
        for k, (source, target, here) in enumerate(
            (
                (mixed_ref, mixed_out, mine),
                (gradx_ref, gradx_out, mine),
                (gradb_ref, gradb_out, own),
                (gradc_ref, gradc_out, own),
            )
        ):
            copy = pltpu.make_async_copy(source.at[:, here], target.at[:, here], sems.at[g, k])
            copy.start()
            copies.append(copy)
        both = jnp.sum(enter * leave, axis=0, keepdims=True)
        met.append(head_sums(jnp.broadcast_to(both, (8, wide))))

    def whole(parts):
        return jnp.concatenate([parts[k] for k in range(GROUPS)], axis=1)

    edge = whole(edge_ref)
    keep, decay = edge[3:4], edge[4:5]
    shape = (tokens, tokens)
    from_here = (iota(shape, 0) <= iota(shape, 1)).astype(F32)
    before = (iota(shape, 0) > iota(shape, 1)).astype(F32)
    late = whole(cols)
    grad_rate = (
        dot(from_here, whole(diff_ref) + whole(rows), precision=PRECISE)
        + dot(before, late, precision=PRECISE)
        + keep * whole(met)[0:1]
    )
    grad_size = (whole(col_ref) + late) / whole(size_ref) + decay * grad_rate
    dt_ref[...] = (grad_size * whole(sig_ref)).astype(BF16)
    for copy in copies:
        copy.wait()


def finish(pay, most, x, w, b, c, tail, reach, y, gx, gb, gc, col, diff, size, sig, edge):
    tokens, channels = x.shape
    heads = channels // HEADDIM
    shapes = [(tokens, channels), (tokens, channels), (tokens, heads), b.shape, b.shape]
    close = pl.BlockSpec(memory_space=pltpu.VMEM)
    far = pl.BlockSpec(memory_space=pl.ANY)
    return pl.pallas_call(
        finish_kernel,
        in_specs=[close] * 17,
        out_specs=[far, far, close, far, far],
        out_shape=[jax.ShapeDtypeStruct(shape, BF16) for shape in shapes],
        scratch_shapes=[pltpu.VMEM(shape, BF16) for shape in (shapes[0], shapes[1], shapes[3], shapes[4])]
        + [pltpu.SemaphoreType.DMA((GROUPS, 4))],
        compiler_params=PARAMS,
        cost_estimate=pl.CostEstimate(flops=20 * tokens * STATE * channels, bytes_accessed=14_000_000, transcendentals=0),
        name="finish",
    )(pay, most, x, w, b, c, tail, reach, y, gx, gb, gc, col, diff, size, sig, edge)


GROUP = ("near", "head")


def exchanged(messages):
    return lax.all_to_all(messages.astype(jnp.float16), GROUP, split_axis=0, concat_axis=0, tiled=True)


def gathered(own, heads):
    parts = lax.axis_size("head")
    per_dev = own.shape[1]
    mine = lax.axis_index("head")
    whole = jnp.where(iota((8, LANES), 1) // per_dev == mine, jnp.tile(own, (1, LANES // per_dev)), 0.0)
    whole = jnp.broadcast_to(whole[None], (parts, 8, LANES))
    return lax.all_to_all(whole, "head", split_axis=0, concat_axis=0, tiled=True).sum(axis=0)[:, :heads]


def per_device(features, dt_raw, b_proj, c_proj, cotangent, starts, a_log, dt_bias, d_skip):
    parts = lax.axis_size(GROUP)
    tokens, heads = dt_raw.shape
    params = gathered(jnp.stack([a_log, dt_bias, d_skip] + [d_skip] * 5), heads)
    marks = lax.dynamic_slice(starts, (lax.axis_index("head") * tokens,), (tokens,)).astype(F32)
    marks = jnp.broadcast_to(marks[None], (8, tokens))
    skip = jnp.broadcast_to(jnp.repeat(params[2], HEADDIM)[None], (8, heads * HEADDIM))
    reach, tail, edge = prep(dt_raw, params, marks, True)
    size, sig, run, runt, bias = prep(dt_raw, params, marks, False)
    near = staged(features, cotangent, b_proj, c_proj)
    came = exchanged(states(*near, tail, reach, edge, parts))
    y, gx, gb, gc, col, diff = inner(features, cotangent, b_proj, c_proj, run, runt, bias, skip)
    count, here = lax.axis_size("far"), lax.axis_index("far")
    group = lax.axis_index(GROUP) * GROUPS // parts
    lane = jnp.arange(LANES)
    mask = [jnp.full((LANES,), here - by >= 0) for by in range(1, count)]
    mask += [jnp.full((LANES,), here + by < count) for by in range(1, count)]
    mask += [lane == group, lane == GROUPS + group]
    mask = jnp.stack(mask).astype(F32)
    total = totals(came.astype(F32))
    came, total = lax.optimization_barrier((came, total))
    far = [lax.ppermute(total, "far", [(p, (p + by) % count) for p in range(count)]) for by in range(1, count)]
    left, most = entering(came.astype(F32), total, jnp.stack(far), mask)
    return finish(
        exchanged(left).astype(F32), most, features, cotangent, b_proj, c_proj, tail, reach, y, gx, gb, gc, col, diff, size, sig, edge
    )


def solution(mesh):
    near = 8
    devices = mesh.devices
    seq, parts = devices.shape
    fine = jax.sharding.Mesh(devices.reshape(seq // near, near, parts), ("far",) + GROUP)
    token = P(("far",) + GROUP, None)
    return jax.shard_map(
        per_device,
        mesh=fine,
        in_specs=(token, token, token, token, token, P(("far", "near")), P("head"), P("head"), P("head")),
        out_specs=(token, token, token, token, token),
        check_vma=False,
    )
```

```python
import functools

import jax
import jax.numpy as jnp
from jax import lax
from jax.experimental import pallas as pl
from jax.experimental.pallas import tpu as pltpu
from jax.sharding import PartitionSpec as P

GROUPS = 4
HEADDIM = 64
STATE = 128
LANES = 128
BITS = 10.0
TOP = 13.0
CUT = -65000.0
F32 = jnp.float32
BF16 = jnp.bfloat16
PRECISE = lax.Precision.HIGHEST
PARAMS = pltpu.CompilerParams(vmem_limit_bytes=24 * 1024 * 1024)


def iota(shape, axis):
    return lax.broadcasted_iota(jnp.int32, shape, axis)


def split(value):
    high = value.astype(BF16)
    return high, (value - high.astype(F32)).astype(BF16)


def dot(a, b, dims=((1,), (0,)), precision=None):
    return lax.dot_general(a, b, (dims, ((), ())), precision=precision, preferred_element_type=F32)


def spread_map(heads, dtype):
    shape = (heads, heads * HEADDIM)
    return (iota(shape, 0) == iota(shape, 1) // HEADDIM).astype(dtype)


def widen(value):
    both = jnp.concatenate(split(value), axis=1)
    spread = spread_map(value.shape[1], BF16)
    return dot(both, jnp.concatenate([spread, spread], axis=0))


def head_sums(value):
    heads = value.shape[1] // HEADDIM
    shape = (heads * HEADDIM, heads)
    fold = (iota(shape, 0) // HEADDIM == iota(shape, 1)).astype(BF16)
    high, low = split(value)
    return dot(high, fold) + dot(low, fold)


def exponent_of(block):
    top = jnp.max(jnp.max(jnp.abs(block), axis=0, keepdims=True), axis=1, keepdims=True)
    return jnp.clip(jnp.floor(jnp.log(jnp.maximum(top, 1e-30)) * 1.4426950408889634), -90.0, 40.0)


def prep_kernel(urgent, dt_ref, par_ref, st_ref, *outs):
    tokens, heads = dt_ref.shape
    per = heads // GROUPS
    par = par_ref[...]
    a_log, dt_bias = par[0:1], par[1:2]
    decay = -jnp.exp(a_log)
    value = dt_ref[...].astype(F32) + dt_bias
    sizes = jnp.maximum(value, 0.0) + jnp.log1p(jnp.exp(-jnp.abs(value)))
    shape = (tokens, tokens)
    lower = (iota(shape, 0) >= iota(shape, 1)).astype(F32)
    upper = (iota(shape, 0) <= iota(shape, 1)).astype(F32)
    running = dot(lower, sizes * decay, precision=PRECISE)
    marks = st_ref[...]
    doc_row = dot(marks, upper)[0:1]
    doc_col = dot(lower, marks, ((1,), (1,)))[:, 0:1]
    doc_last = doc_row[:, tokens - 1 :]
    groups = [slice(g * per, (g + 1) * per) for g in range(GROUPS)]
    if urgent:
        reach_ref, tail_ref, edge_ref = outs
        last = running[tokens - 1 :]
        reach = jnp.where(doc_col == 0.0, jnp.exp(running), 0.0)
        tail = jnp.where(doc_col == doc_last, jnp.exp(last - running), 0.0) * sizes
        through = jnp.where(doc_last == 0.0, last * 128.0, CUT)
        high = through.astype(BF16).astype(F32)
        mid = (through - high).astype(BF16).astype(F32)
        low = (through - high - mid).astype(BF16).astype(F32)
        keep = jnp.exp((high + mid + low) * (1.0 / 128.0))
        edge = jnp.concatenate([high, mid, low, keep, decay, decay, decay, decay], axis=0)
        for g, mine in enumerate(groups):
            reach_ref[g] = reach[:, mine]
            tail_ref[g] = tail[:, mine]
            edge_ref[g] = edge[:, mine]
    else:
        size_ref, sig_ref, run_ref, runt_ref, bias_ref = outs
        linked = (doc_col == doc_row) & (iota(shape, 0) >= iota(shape, 1))
        bias_ref[...] = jnp.where(linked, 0.0, -1e30)
        turned = (running - jnp.log(sizes)).T
        sigmoid = 1.0 / (1.0 + jnp.exp(-value))
        for g, mine in enumerate(groups):
            size_ref[g] = sizes[:, mine]
            sig_ref[g] = sigmoid[:, mine]
            run_ref[g] = running[:, mine]
            runt_ref[g] = turned[mine]


def prep(dt_raw, params, marks, urgent):
    tokens, heads = dt_raw.shape
    per = heads // GROUPS
    small = (GROUPS, tokens, per)
    if urgent:
        shapes = [small, small, (GROUPS, 8, per)]
    else:
        shapes = [small, small, small, (GROUPS, per, tokens), (tokens, tokens)]
    return pl.pallas_call(
        functools.partial(prep_kernel, urgent),
        out_shape=[jax.ShapeDtypeStruct(shape, F32) for shape in shapes],
        compiler_params=PARAMS,
        name="prep",
    )(dt_raw, params, marks)


def stage_kernel(*refs):
    half = len(refs) // 2
    for source, target in zip(refs[:half], refs[half:]):
        target[...] = source[...]


def staged(*arrays):
    return pl.pallas_call(
        stage_kernel,
        out_shape=[jax.ShapeDtypeStruct(array.shape, array.dtype) for array in arrays],
        compiler_params=PARAMS,
        cost_estimate=pl.CostEstimate(flops=0, bytes_accessed=2 * sum(2 * array.size for array in arrays), transcendentals=0),
        name="staged",
    )(*arrays)


def state_of(values, proj, scale):
    high, low = split(values.astype(F32) * widen(scale))
    return dot(jnp.concatenate([proj, proj], axis=0), jnp.concatenate([high, low], axis=0), ((0,), (0,)))


def state_kernel(x_ref, w_ref, b_ref, c_ref, tail_ref, reach_ref, edge_ref, out_ref):
    messages, rows, _ = out_ref.shape
    wide = x_ref.shape[1] // GROUPS
    part = (rows - 8) // 2
    fold = STATE // part
    per_group = messages // GROUPS
    row, lane = iota((8, LANES), 0), iota((8, LANES), 1)
    all_powers = jnp.zeros((8, LANES), F32)
    sides = []
    for g in range(GROUPS):
        mine, own = slice(g * wide, (g + 1) * wide), slice(g * STATE, (g + 1) * STATE)
        pieces = dot(edge_ref[g].astype(BF16), spread_map(tail_ref.shape[2], BF16))
        spread = jnp.zeros((8, LANES), F32)
        for which, (val_ref, proj_ref, scale_ref) in enumerate(
            ((x_ref, b_ref, tail_ref), (w_ref, c_ref, reach_ref))
        ):
            state = state_of(val_ref[:, mine], proj_ref[:, own], scale_ref[g])
            power = exponent_of(state)
            spread = jnp.where(row == 4 + which, power, spread)
            all_powers = jnp.where(lane == which * GROUPS + g, power, all_powers)
            state = state * jnp.exp2(TOP - power)
            for k in range(per_group):
                lanes = slice(k // fold * LANES, (k // fold + 1) * LANES)
                here = slice(k % fold * part, (k % fold + 1) * part)
                out_ref[g * per_group + k, which * part : (which + 1) * part] = state[here, lanes]
        sides.append((pieces, spread))
    for g, (pieces, spread) in enumerate(sides):
        side = jnp.where(row == 3, all_powers, spread)
        for k in range(per_group):
            lanes = slice(k // fold * LANES, (k // fold + 1) * LANES)
            out_ref[g * per_group + k, 2 * part :] = jnp.where(row < 3, pieces[:, lanes], side)


def states(x, w, b, c, tail, reach, edge, parts):
    tokens, channels = x.shape
    rows = 2 * STATE * channels // (parts * LANES) + 8
    return pl.pallas_call(
        state_kernel,
        out_shape=jax.ShapeDtypeStruct((parts, rows, LANES), F32),
        compiler_params=PARAMS,
        cost_estimate=pl.CostEstimate(flops=8 * tokens * STATE * channels, bytes_accessed=7000000, transcendentals=0),
        name="states",
    )(x, w, b, c, tail, reach, edge)


def keep_of(pay_ref, i, part):
    side = pay_ref[i, 2 * part :]
    return jnp.exp((side[0:1] + side[1:2] + side[2:3]) * (1.0 / 128.0))


def lane_of(row, mask_ref, which):
    mine = mask_ref[mask_ref.shape[0] - 2 + which : mask_ref.shape[0] - 1 + which]
    return jnp.sum(row * mine, axis=1, keepdims=True)


def block_of(pay_ref, i, part, which):
    power = pay_ref[i, 2 * part :][4 + which : 5 + which]
    return pay_ref[i, which * part : (which + 1) * part] * jnp.exp2(power - TOP)


def total_kernel(pay_ref, out_ref):
    blocks, rows, _ = pay_ref.shape
    part = (rows - 8) // 2

    def step(k, carry):
        forth, back, through, most = carry
        late = blocks - 1 - k
        keep = keep_of(pay_ref, k, part)
        forth = keep * forth + block_of(pay_ref, k, part, 0)
        back = keep_of(pay_ref, late, part) * back + block_of(pay_ref, late, part, 1)
        return forth, back, through * keep, jnp.maximum(most, pay_ref[k, 2 * part :][3:4])

    zero = jnp.zeros((part, LANES), F32)
    one = jnp.ones((1, LANES), F32)
    forth, back, through, most = lax.fori_loop(0, blocks, step, (zero, zero, one, -1000.0 * one), unroll=8)
    row = iota((8, LANES), 0)
    side = jnp.where(row == 0, through, most)
    for which, state in enumerate((forth, back)):
        out_ref[which, 0:part] = state
        out_ref[which, part:] = side


def totals(pay):
    part = (pay.shape[1] - 8) // 2
    return pl.pallas_call(
        total_kernel,
        out_shape=jax.ShapeDtypeStruct((2, part + 8, LANES), F32),
        compiler_params=PARAMS,
        cost_estimate=pl.CostEstimate(flops=2 * pay.size, bytes_accessed=4 * pay.size, transcendentals=0),
        name="totals",
    )(pay)


def enter_kernel(pay_ref, own_ref, far_ref, mask_ref, out_ref, most_ref):
    blocks, rows, _ = pay_ref.shape
    part = (rows - 8) // 2
    others = far_ref.shape[0]
    most = own_ref[0, part:]
    for k in range(others):
        most = jnp.maximum(most, far_ref[k, 0, part:])
    most_ref[...] = most
    starts, scales = [], []
    for which in range(2):
        state = jnp.zeros((part, LANES), F32)
        for by in range(others, 0, -1):
            k = by - 1 if which == 0 else others - by
            far = far_ref[k, which]
            valid = mask_ref[which * others + by - 1 : which * others + by] > 0.0
            state = jnp.where(valid, far[0:part] + far[part : part + 1] * state, state)
        starts.append(state)
        scales.append(jnp.exp2(TOP + 2.0 - BITS - lane_of(most[1:2], mask_ref, which)))

    def step(k, carry):
        forth, back = carry
        late = blocks - 1 - k
        out_ref[k, 0:part] = forth * scales[0]
        out_ref[late, part:] = back * scales[1]
        forth = keep_of(pay_ref, k, part) * forth + block_of(pay_ref, k, part, 0)
        back = keep_of(pay_ref, late, part) * back + block_of(pay_ref, late, part, 1)
        return forth, back

    lax.fori_loop(0, blocks, step, tuple(starts), unroll=8)


def entering(pay, own, far, mask):
    blocks, rows, _ = pay.shape
    return pl.pallas_call(
        enter_kernel,
        out_shape=[jax.ShapeDtypeStruct((blocks, rows - 8, LANES), F32), jax.ShapeDtypeStruct((8, LANES), F32)],
        compiler_params=PARAMS,
        cost_estimate=pl.CostEstimate(flops=4 * pay.size, bytes_accessed=8 * pay.size, transcendentals=0),
        name="entering",
    )(pay, own, far, mask)


def inner_kernel(x_ref, w_ref, b_ref, c_ref, run_ref, runt_ref, bias_ref, skip_ref, y_ref, gx_ref, gb_ref, gc_ref, col_ref, diff_ref):
    tokens, wide = x_ref.shape
    heads = wide // HEADDIM
    pair = 2 * HEADDIM
    b_vals, c_vals = b_ref[...], c_ref[...]
    scores = dot(c_vals, b_vals, ((1,), (1,)))
    bias = bias_ref[...]
    run, runt = run_ref[0], runt_ref[0]
    first = iota((tokens, pair), 1) < HEADDIM
    grad_scores = jnp.zeros((tokens, tokens), F32)
    y_all, u_all = [], []
    for k in range(0, heads, 2):
        mine = slice(k * HEADDIM, (k + 2) * HEADDIM)
        x_pair, w_pair = x_ref[:, mine], w_ref[:, mine]
        x_two = jnp.concatenate([x_pair, x_pair], axis=0)
        w_two = jnp.concatenate([w_pair, w_pair], axis=0)
        ys, us = [], []
        for which in range(2):
            h = k + which
            keep = first if which == 0 else ~first
            weight = jnp.exp(run[:, h : h + 1] - runt[h : h + 1, :] + bias)
            cross = dot(jnp.where(keep, w_pair, jnp.zeros_like(w_pair)), x_pair, ((1,), (1,)))
            grad_scores = grad_scores + weight * cross
            high, low = split(weight * scores)
            ys.append(dot(jnp.concatenate([high, low], axis=1), x_two))
            us.append(dot(jnp.concatenate([high, low], axis=0), w_two, ((0,), (0,))))
        y_all.append(jnp.where(first, ys[0], ys[1]))
        u_all.append(jnp.where(first, us[0], us[1]))
    y_in = jnp.concatenate(y_all, axis=1)
    u_in = jnp.concatenate(u_all, axis=1)
    x_vals, w_vals = x_ref[...].astype(F32), w_ref[...].astype(F32)
    skip = skip_ref[0:1]
    y_ref[...] = y_in + skip * x_vals
    gx_ref[...] = u_in + skip * w_vals
    high, low = split(grad_scores)
    gc_ref[...] = dot(jnp.concatenate([high, low], axis=1), jnp.concatenate([b_vals, b_vals], axis=0))
    gb_ref[...] = dot(jnp.concatenate([high, low], axis=0), jnp.concatenate([c_vals, c_vals], axis=0), ((0,), (0,)))
    col = head_sums(x_vals * u_in)
    col_ref[0] = col
    diff_ref[0] = head_sums(w_vals * y_in) - col


def inner(x, w, b, c, run, runt, bias, skip):
    tokens, channels = x.shape
    wide = channels // GROUPS
    per = run.shape[2]
    values = pl.BlockSpec((tokens, wide), lambda g: (0, g))
    proj = pl.BlockSpec((tokens, STATE), lambda g: (0, g))
    small = pl.BlockSpec((1, tokens, per), lambda g: (g, 0, 0))
    return pl.pallas_call(
        inner_kernel,
        grid=(GROUPS,),
        in_specs=[
            values,
            values,
            proj,
            proj,
            small,
            pl.BlockSpec((1, per, tokens), lambda g: (g, 0, 0)),
            pl.BlockSpec((tokens, tokens), lambda g: (0, 0)),
            pl.BlockSpec((8, wide), lambda g: (0, g)),
        ],
        out_specs=[values, values, proj, proj, small, small],
        out_shape=[
            jax.ShapeDtypeStruct((tokens, channels), F32),
            jax.ShapeDtypeStruct((tokens, channels), F32),
            jax.ShapeDtypeStruct((tokens, GROUPS * STATE), F32),
            jax.ShapeDtypeStruct((tokens, GROUPS * STATE), F32),
            jax.ShapeDtypeStruct((GROUPS, tokens, per), F32),
            jax.ShapeDtypeStruct((GROUPS, tokens, per), F32),
        ],
        compiler_params=PARAMS,
        cost_estimate=pl.CostEstimate(flops=20_000_000_000, bytes_accessed=8_000_000, transcendentals=tokens * tokens * 64),
        name="inner",
    )(x, w, b, c, run, runt, bias, skip)


def state_from(pay_ref, most_ref, group, which):
    messages, rows, _ = pay_ref.shape
    per_group = messages // GROUPS
    part = rows // 2
    fold = STATE // part
    here = slice(which * part, (which + 1) * part)
    lane = which * GROUPS + group
    power = most_ref[1:2, lane : lane + 1]
    columns = []
    for first in range(group * per_group, (group + 1) * per_group, fold):
        columns.append(jnp.concatenate([pay_ref[first + k, here] for k in range(fold)], axis=0))
    return jnp.concatenate(columns, axis=1), jnp.exp2(power - (TOP + 2.0 - BITS))


def carried_terms(state, values, scale, proj):
    wide = widen(scale)
    high, low = split(state)
    terms = dot(jnp.concatenate([proj, proj], axis=1), jnp.concatenate([high, low], axis=0)) * wide
    left_high, left_low = split(values * wide)
    last = ((1,), (1,))
    both = dot(jnp.concatenate([left_high, left_low], axis=0), high, last)
    tokens = values.shape[0]
    grad = both[:tokens] + (both[tokens:] + dot(left_high, low, last))
    return terms, grad, head_sums(terms * values)


def finish_kernel(
    pay_ref, most_ref, x_ref, w_ref, b_ref, c_ref, tail_ref, reach_ref, y_ref, gx_ref, gb_ref, gc_ref, col_ref, diff_ref, size_ref, sig_ref, edge_ref,
    mixed_out, gradx_out, dt_ref, gradb_out, gradc_out, mixed_ref, gradx_ref, gradb_ref, gradc_ref, sems,
):
    tokens, channels = x_ref.shape
    wide = channels // GROUPS
    rows, cols, met, copies = [], [], [], []
    for g in range(GROUPS):
        mine, own = slice(g * wide, (g + 1) * wide), slice(g * STATE, (g + 1) * STATE)
        enter, enter_scale = state_from(pay_ref, most_ref, g, 0)
        leave, leave_scale = state_from(pay_ref, most_ref, g, 1)
        terms, grad, sums = carried_terms(enter, w_ref[:, mine].astype(F32), reach_ref[g] * enter_scale, c_ref[:, own])
        mixed_ref[:, mine] = (y_ref[:, mine] + terms).astype(BF16)
        gradc_ref[:, own] = (gc_ref[:, own] + grad).astype(BF16)
        rows.append(sums)
        terms, grad, sums = carried_terms(leave, x_ref[:, mine].astype(F32), tail_ref[g] * leave_scale, b_ref[:, own])
        gradx_ref[:, mine] = (gx_ref[:, mine] + terms).astype(BF16)
        gradb_ref[:, own] = (gb_ref[:, own] + grad).astype(BF16)
        cols.append(sums)
        for k, (source, target, here) in enumerate(
            (
                (mixed_ref, mixed_out, mine),
                (gradx_ref, gradx_out, mine),
                (gradb_ref, gradb_out, own),
                (gradc_ref, gradc_out, own),
            )
        ):
            copy = pltpu.make_async_copy(source.at[:, here], target.at[:, here], sems.at[g, k])
            copy.start()
            copies.append(copy)
        both = jnp.sum(enter * leave, axis=0, keepdims=True) * (enter_scale * leave_scale)
        met.append(head_sums(jnp.broadcast_to(both, (8, wide))))

    def whole(parts):
        return jnp.concatenate([parts[k] for k in range(GROUPS)], axis=1)

    edge = whole(edge_ref)
    keep, decay = edge[3:4], edge[4:5]
    shape = (tokens, tokens)
    from_here = (iota(shape, 0) <= iota(shape, 1)).astype(F32)
    before = (iota(shape, 0) > iota(shape, 1)).astype(F32)
    late = whole(cols)
    grad_rate = (
        dot(from_here, whole(diff_ref) + whole(rows), precision=PRECISE)
        + dot(before, late, precision=PRECISE)
        + keep * whole(met)[0:1]
    )
    grad_size = (whole(col_ref) + late) / whole(size_ref) + decay * grad_rate
    dt_ref[...] = (grad_size * whole(sig_ref)).T.astype(BF16)
    for copy in copies:
        copy.wait()


def finish(pay, most, x, w, b, c, tail, reach, y, gx, gb, gc, col, diff, size, sig, edge):
    tokens, channels = x.shape
    heads = channels // HEADDIM
    shapes = [(tokens, channels), (tokens, channels), (heads, tokens), b.shape, b.shape]
    close = pl.BlockSpec(memory_space=pltpu.VMEM)
    far = pl.BlockSpec(memory_space=pl.ANY)
    return pl.pallas_call(
        finish_kernel,
        in_specs=[close] * 17,
        out_specs=[far, far, close, far, far],
        out_shape=[jax.ShapeDtypeStruct(shape, BF16) for shape in shapes],
        scratch_shapes=[pltpu.VMEM(shape, BF16) for shape in (shapes[0], shapes[1], shapes[3], shapes[4])]
        + [pltpu.SemaphoreType.DMA((GROUPS, 4))],
        compiler_params=PARAMS,
        cost_estimate=pl.CostEstimate(flops=20 * tokens * STATE * channels, bytes_accessed=14_000_000, transcendentals=0),
        name="finish",
    )(pay, most, x, w, b, c, tail, reach, y, gx, gb, gc, col, diff, size, sig, edge)


GROUP = ("near", "head")


def exchanged(messages):
    return lax.all_to_all(messages.astype(jnp.float16), GROUP, split_axis=0, concat_axis=0, tiled=True)


def gathered(own, heads):
    parts = lax.axis_size("head")
    per_dev = own.shape[1]
    mine = lax.axis_index("head")
    whole = jnp.where(iota((8, LANES), 1) // per_dev == mine, jnp.tile(own, (1, LANES // per_dev)), 0.0)
    whole = jnp.broadcast_to(whole[None], (parts, 8, LANES))
    return lax.all_to_all(whole, "head", split_axis=0, concat_axis=0, tiled=True).sum(axis=0)[:, :heads]


def per_device(features, dt_raw, b_proj, c_proj, cotangent, starts, a_log, dt_bias, d_skip):
    parts = lax.axis_size(GROUP)
    tokens, heads = dt_raw.shape
    params = gathered(jnp.stack([a_log, dt_bias, d_skip] + [d_skip] * 5), heads)
    marks = lax.dynamic_slice(starts, (lax.axis_index("head") * tokens,), (tokens,)).astype(F32)
    marks = jnp.broadcast_to(marks[None], (8, tokens))
    skip = jnp.broadcast_to(jnp.repeat(params[2], HEADDIM)[None], (8, heads * HEADDIM))
    reach, tail, edge = prep(dt_raw, params, marks, True)
    size, sig, run, runt, bias = prep(dt_raw, params, marks, False)
    near = staged(features, cotangent, b_proj, c_proj)
    came = exchanged(states(*near, tail, reach, edge, parts))
    y, gx, gb, gc, col, diff = inner(features, cotangent, b_proj, c_proj, run, runt, bias, skip)
    count, here = lax.axis_size("far"), lax.axis_index("far")
    group = lax.axis_index(GROUP) * GROUPS // parts
    lane = jnp.arange(LANES)
    mask = [jnp.full((LANES,), here - by >= 0) for by in range(1, count)]
    mask += [jnp.full((LANES,), here + by < count) for by in range(1, count)]
    mask += [lane == group, lane == GROUPS + group]
    mask = jnp.stack(mask).astype(F32)
    total = totals(came.astype(F32))
    came, total = lax.optimization_barrier((came, total))
    far = [lax.ppermute(total, "far", [(p, (p + by) % count) for p in range(count)]) for by in range(1, count)]
    left, most = entering(came.astype(F32), total, jnp.stack(far), mask)
    mixed, grad_x, grad_dt, grad_b, grad_c = finish(
        exchanged(left).astype(F32), most, features, cotangent, b_proj, c_proj, tail, reach, y, gx, gb, gc, col, diff, size, sig, edge
    )
    return mixed, grad_x, grad_dt.T, grad_b, grad_c


def solution(mesh):
    near = 8
    devices = mesh.devices
    seq, parts = devices.shape
    fine = jax.sharding.Mesh(devices.reshape(seq // near, near, parts), ("far",) + GROUP)
    token = P(("far",) + GROUP, None)
    return jax.shard_map(
        per_device,
        mesh=fine,
        in_specs=(token, token, token, token, token, P(("far", "near")), P("head"), P("head"), P("head")),
        out_specs=(token, token, token, token, token),
        check_vma=False,
    )
```

```python
import functools

import jax
import jax.numpy as jnp
from jax import lax
from jax.experimental import pallas as pl
from jax.experimental.pallas import tpu as pltpu
from jax.sharding import PartitionSpec as P

GROUPS = 4
HEADDIM = 64
STATE = 128
LANES = 128
BITS = 10.0
TOP = 13.0
CUT = -65000.0
F32 = jnp.float32
BF16 = jnp.bfloat16
PRECISE = lax.Precision.HIGHEST
PARAMS = pltpu.CompilerParams(vmem_limit_bytes=24 * 1024 * 1024)


def iota(shape, axis):
    return lax.broadcasted_iota(jnp.int32, shape, axis)


def split(value):
    high = value.astype(BF16)
    return high, (value - high.astype(F32)).astype(BF16)


def dot(a, b, dims=((1,), (0,)), precision=None):
    return lax.dot_general(a, b, (dims, ((), ())), precision=precision, preferred_element_type=F32)


def spread_map(heads, dtype):
    shape = (heads, heads * HEADDIM)
    return (iota(shape, 0) == iota(shape, 1) // HEADDIM).astype(dtype)


def widen(value):
    both = jnp.concatenate(split(value), axis=1)
    spread = spread_map(value.shape[1], BF16)
    return dot(both, jnp.concatenate([spread, spread], axis=0))


def head_sums(value):
    heads = value.shape[1] // HEADDIM
    shape = (heads * HEADDIM, heads)
    fold = (iota(shape, 0) // HEADDIM == iota(shape, 1)).astype(BF16)
    high, low = split(value)
    return dot(high, fold) + dot(low, fold)


def exponent_of(block):
    top = jnp.max(jnp.max(jnp.abs(block), axis=0, keepdims=True), axis=1, keepdims=True)
    return jnp.clip(jnp.floor(jnp.log(jnp.maximum(top, 1e-30)) * 1.4426950408889634), -90.0, 40.0)


def prep_kernel(urgent, dt_ref, par_ref, st_ref, *outs):
    tokens, heads = dt_ref.shape
    per = heads // GROUPS
    par = par_ref[...]
    a_log, dt_bias = par[0:1], par[1:2]
    decay = -jnp.exp(a_log)
    value = dt_ref[...].astype(F32) + dt_bias
    sizes = jnp.maximum(value, 0.0) + jnp.log1p(jnp.exp(-jnp.abs(value)))
    shape = (tokens, tokens)
    lower = (iota(shape, 0) >= iota(shape, 1)).astype(F32)
    upper = (iota(shape, 0) <= iota(shape, 1)).astype(F32)
    running = dot(lower, sizes * decay, precision=PRECISE)
    marks = st_ref[...]
    doc_row = dot(marks, upper)[0:1]
    doc_col = dot(lower, marks, ((1,), (1,)))[:, 0:1]
    doc_last = doc_row[:, tokens - 1 :]
    groups = [slice(g * per, (g + 1) * per) for g in range(GROUPS)]
    if urgent:
        reach_ref, tail_ref, edge_ref = outs
        last = running[tokens - 1 :]
        reach = jnp.where(doc_col == 0.0, jnp.exp(running), 0.0)
        tail = jnp.where(doc_col == doc_last, jnp.exp(last - running), 0.0) * sizes
        through = jnp.where(doc_last == 0.0, last * 128.0, CUT)
        high = through.astype(BF16).astype(F32)
        mid = (through - high).astype(BF16).astype(F32)
        low = (through - high - mid).astype(BF16).astype(F32)
        keep = jnp.exp((high + mid + low) * (1.0 / 128.0))
        edge = jnp.concatenate([high, mid, low, keep, decay, decay, decay, decay], axis=0)
        for g, mine in enumerate(groups):
            reach_ref[g] = reach[:, mine]
            tail_ref[g] = tail[:, mine]
            edge_ref[g] = edge[:, mine]
    else:
        size_ref, sig_ref, run_ref, runt_ref, bias_ref = outs
        linked = (doc_col == doc_row) & (iota(shape, 0) >= iota(shape, 1))
        bias_ref[...] = jnp.where(linked, 0.0, -1e30)
        turned = (running - jnp.log(sizes)).T
        sigmoid = 1.0 / (1.0 + jnp.exp(-value))
        for g, mine in enumerate(groups):
            size_ref[g] = sizes[:, mine]
            sig_ref[g] = sigmoid[:, mine]
            run_ref[g] = running[:, mine]
            runt_ref[g] = turned[mine]


def prep(dt_raw, params, marks, urgent):
    tokens, heads = dt_raw.shape
    per = heads // GROUPS
    small = (GROUPS, tokens, per)
    if urgent:
        shapes = [small, small, (GROUPS, 8, per)]
    else:
        shapes = [small, small, small, (GROUPS, per, tokens), (tokens, tokens)]
    return pl.pallas_call(
        functools.partial(prep_kernel, urgent),
        out_shape=[jax.ShapeDtypeStruct(shape, F32) for shape in shapes],
        compiler_params=PARAMS,
        name="prep",
    )(dt_raw, params, marks)


def stage_kernel(*refs):
    half = len(refs) // 2
    for source, target in zip(refs[:half], refs[half:]):
        target[...] = source[...]


def staged(*arrays):
    return pl.pallas_call(
        stage_kernel,
        out_shape=[jax.ShapeDtypeStruct(array.shape, array.dtype) for array in arrays],
        compiler_params=PARAMS,
        cost_estimate=pl.CostEstimate(flops=0, bytes_accessed=2 * sum(2 * array.size for array in arrays), transcendentals=0),
        name="staged",
    )(*arrays)


def state_of(values, proj, scale):
    high, low = split(values.astype(F32) * widen(scale))
    return dot(jnp.concatenate([proj, proj], axis=0), jnp.concatenate([high, low], axis=0), ((0,), (0,)))


def state_kernel(x_ref, w_ref, b_ref, c_ref, tail_ref, reach_ref, edge_ref, out_ref):
    messages, rows, _ = out_ref.shape
    wide = x_ref.shape[1] // GROUPS
    part = (rows - 8) // 2
    fold = STATE // part
    per_group = messages // GROUPS
    row, lane = iota((8, LANES), 0), iota((8, LANES), 1)
    all_powers = jnp.zeros((8, LANES), F32)
    sides = []
    for g in range(GROUPS):
        mine, own = slice(g * wide, (g + 1) * wide), slice(g * STATE, (g + 1) * STATE)
        pieces = dot(edge_ref[g].astype(BF16), spread_map(tail_ref.shape[2], BF16))
        spread = jnp.zeros((8, LANES), F32)
        for which, (val_ref, proj_ref, scale_ref) in enumerate(
            ((x_ref, b_ref, tail_ref), (w_ref, c_ref, reach_ref))
        ):
            state = state_of(val_ref[:, mine], proj_ref[:, own], scale_ref[g])
            power = exponent_of(state)
            spread = jnp.where(row == 4 + which, power, spread)
            spread = jnp.where((row == 6 + which) & (lane == which * GROUPS + g), 1.0, spread)
            all_powers = jnp.where(lane == which * GROUPS + g, power, all_powers)
            state = state * jnp.exp2(TOP - power)
            for k in range(per_group):
                lanes = slice(k // fold * LANES, (k // fold + 1) * LANES)
                here = slice(k % fold * part, (k % fold + 1) * part)
                out_ref[g * per_group + k, which * part : (which + 1) * part] = state[here, lanes]
        sides.append((pieces, spread))
    for g, (pieces, spread) in enumerate(sides):
        side = jnp.where(row == 3, all_powers, spread)
        for k in range(per_group):
            lanes = slice(k // fold * LANES, (k // fold + 1) * LANES)
            out_ref[g * per_group + k, 2 * part :] = jnp.where(row < 3, pieces[:, lanes], side)


def states(x, w, b, c, tail, reach, edge, parts):
    tokens, channels = x.shape
    rows = 2 * STATE * channels // (parts * LANES) + 8
    return pl.pallas_call(
        state_kernel,
        out_shape=jax.ShapeDtypeStruct((parts, rows, LANES), F32),
        compiler_params=PARAMS,
        cost_estimate=pl.CostEstimate(flops=8 * tokens * STATE * channels, bytes_accessed=7000000, transcendentals=0),
        name="states",
    )(x, w, b, c, tail, reach, edge)


def keep_of(pay_ref, i, part):
    side = pay_ref[i, 2 * part :]
    return jnp.exp((side[0:1] + side[1:2] + side[2:3]) * (1.0 / 128.0))


def lane_of(row, pay_ref, part, which):
    return jnp.sum(row * pay_ref[0, 2 * part :][6 + which : 7 + which], axis=1, keepdims=True)


def block_of(pay_ref, i, part, which):
    power = pay_ref[i, 2 * part :][4 + which : 5 + which]
    return pay_ref[i, which * part : (which + 1) * part] * jnp.exp2(power - TOP)


def total_kernel(pay_ref, out_ref):
    blocks, rows, _ = pay_ref.shape
    part = (rows - 8) // 2

    def step(k, carry):
        forth, back, through, most = carry
        late = blocks - 1 - k
        keep = keep_of(pay_ref, k, part)
        forth = keep * forth + block_of(pay_ref, k, part, 0)
        back = keep_of(pay_ref, late, part) * back + block_of(pay_ref, late, part, 1)
        return forth, back, through * keep, jnp.maximum(most, pay_ref[k, 2 * part :][3:4])

    zero = jnp.zeros((part, LANES), F32)
    one = jnp.ones((1, LANES), F32)
    forth, back, through, most = lax.fori_loop(0, blocks, step, (zero, zero, one, -1000.0 * one), unroll=8)
    row = iota((8, LANES), 0)
    side = jnp.where(row == 0, through, most)
    for which, state in enumerate((forth, back)):
        out_ref[which, 0:part] = state
        out_ref[which, part:] = side


def totals(pay):
    part = (pay.shape[1] - 8) // 2
    return pl.pallas_call(
        total_kernel,
        out_shape=jax.ShapeDtypeStruct((2, part + 8, LANES), F32),
        compiler_params=PARAMS,
        cost_estimate=pl.CostEstimate(flops=2 * pay.size, bytes_accessed=4 * pay.size, transcendentals=0),
        name="totals",
    )(pay)


def enter_kernel(pay_ref, own_ref, far_ref, mask_ref, out_ref, most_ref):
    blocks, rows, _ = pay_ref.shape
    part = (rows - 8) // 2
    others = far_ref.shape[0]
    most = own_ref[0, part:]
    for k in range(others):
        most = jnp.maximum(most, far_ref[k, 0, part:])
    most_ref[...] = most
    starts, scales = [], []
    for which in range(2):
        state = jnp.zeros((part, LANES), F32)
        for by in range(others, 0, -1):
            k = by - 1 if which == 0 else others - by
            far = far_ref[k, which]
            valid = mask_ref[which * others + by - 1 : which * others + by] > 0.0
            state = jnp.where(valid, far[0:part] + far[part : part + 1] * state, state)
        starts.append(state)
        scales.append(jnp.exp2(TOP + 2.0 - BITS - lane_of(most[1:2], pay_ref, part, which)))

    def step(k, carry):
        forth, back = carry
        late = blocks - 1 - k
        out_ref[k, 0:part] = forth * scales[0]
        out_ref[late, part:] = back * scales[1]
        forth = keep_of(pay_ref, k, part) * forth + block_of(pay_ref, k, part, 0)
        back = keep_of(pay_ref, late, part) * back + block_of(pay_ref, late, part, 1)
        return forth, back

    lax.fori_loop(0, blocks, step, tuple(starts), unroll=8)


def entering(pay, own, far, mask):
    blocks, rows, _ = pay.shape
    return pl.pallas_call(
        enter_kernel,
        out_shape=[jax.ShapeDtypeStruct((blocks, rows - 8, LANES), F32), jax.ShapeDtypeStruct((8, LANES), F32)],
        compiler_params=PARAMS,
        cost_estimate=pl.CostEstimate(flops=4 * pay.size, bytes_accessed=8 * pay.size, transcendentals=0),
        name="entering",
    )(pay, own, far, mask)


def inner_kernel(x_ref, w_ref, b_ref, c_ref, run_ref, runt_ref, bias_ref, skip_ref, y_ref, gx_ref, gb_ref, gc_ref, col_ref, diff_ref):
    tokens, wide = x_ref.shape
    heads = wide // HEADDIM
    pair = 2 * HEADDIM
    b_vals, c_vals = b_ref[...], c_ref[...]
    scores = dot(c_vals, b_vals, ((1,), (1,)))
    bias = bias_ref[...]
    run, runt = run_ref[0], runt_ref[0]
    first = iota((tokens, pair), 1) < HEADDIM
    grad_scores = jnp.zeros((tokens, tokens), F32)
    y_all, u_all = [], []
    for k in range(0, heads, 2):
        mine = slice(k * HEADDIM, (k + 2) * HEADDIM)
        x_pair, w_pair = x_ref[:, mine], w_ref[:, mine]
        x_two = jnp.concatenate([x_pair, x_pair], axis=0)
        w_two = jnp.concatenate([w_pair, w_pair], axis=0)
        ys, us = [], []
        for which in range(2):
            h = k + which
            keep = first if which == 0 else ~first
            weight = jnp.exp(run[:, h : h + 1] - runt[h : h + 1, :] + bias)
            cross = dot(jnp.where(keep, w_pair, jnp.zeros_like(w_pair)), x_pair, ((1,), (1,)))
            grad_scores = grad_scores + weight * cross
            high, low = split(weight * scores)
            ys.append(dot(jnp.concatenate([high, low], axis=1), x_two))
            us.append(dot(jnp.concatenate([high, low], axis=0), w_two, ((0,), (0,))))
        y_all.append(jnp.where(first, ys[0], ys[1]))
        u_all.append(jnp.where(first, us[0], us[1]))
    y_in = jnp.concatenate(y_all, axis=1)
    u_in = jnp.concatenate(u_all, axis=1)
    x_vals, w_vals = x_ref[...].astype(F32), w_ref[...].astype(F32)
    skip = skip_ref[0:1]
    y_ref[...] = y_in + skip * x_vals
    gx_ref[...] = u_in + skip * w_vals
    high, low = split(grad_scores)
    gc_ref[...] = dot(jnp.concatenate([high, low], axis=1), jnp.concatenate([b_vals, b_vals], axis=0))
    gb_ref[...] = dot(jnp.concatenate([high, low], axis=0), jnp.concatenate([c_vals, c_vals], axis=0), ((0,), (0,)))
    col = head_sums(x_vals * u_in)
    col_ref[0] = col
    diff_ref[0] = head_sums(w_vals * y_in) - col


def inner(x, w, b, c, run, runt, bias, skip):
    tokens, channels = x.shape
    wide = channels // GROUPS
    per = run.shape[2]
    values = pl.BlockSpec((tokens, wide), lambda g: (0, g))
    proj = pl.BlockSpec((tokens, STATE), lambda g: (0, g))
    small = pl.BlockSpec((1, tokens, per), lambda g: (g, 0, 0))
    return pl.pallas_call(
        inner_kernel,
        grid=(GROUPS,),
        in_specs=[
            values,
            values,
            proj,
            proj,
            small,
            pl.BlockSpec((1, per, tokens), lambda g: (g, 0, 0)),
            pl.BlockSpec((tokens, tokens), lambda g: (0, 0)),
            pl.BlockSpec((8, wide), lambda g: (0, g)),
        ],
        out_specs=[values, values, proj, proj, small, small],
        out_shape=[
            jax.ShapeDtypeStruct((tokens, channels), F32),
            jax.ShapeDtypeStruct((tokens, channels), F32),
            jax.ShapeDtypeStruct((tokens, GROUPS * STATE), F32),
            jax.ShapeDtypeStruct((tokens, GROUPS * STATE), F32),
            jax.ShapeDtypeStruct((GROUPS, tokens, per), F32),
            jax.ShapeDtypeStruct((GROUPS, tokens, per), F32),
        ],
        compiler_params=PARAMS,
        cost_estimate=pl.CostEstimate(flops=20_000_000_000, bytes_accessed=8_000_000, transcendentals=tokens * tokens * 64),
        name="inner",
    )(x, w, b, c, run, runt, bias, skip)


def state_from(pay_ref, most_ref, group, which):
    messages, rows, _ = pay_ref.shape
    per_group = messages // GROUPS
    part = rows // 2
    fold = STATE // part
    here = slice(which * part, (which + 1) * part)
    lane = which * GROUPS + group
    power = most_ref[1:2, lane : lane + 1]
    columns = []
    for first in range(group * per_group, (group + 1) * per_group, fold):
        columns.append(jnp.concatenate([pay_ref[first + k, here] for k in range(fold)], axis=0))
    return jnp.concatenate(columns, axis=1), jnp.exp2(power - (TOP + 2.0 - BITS))


def carried_terms(state, values, scale, proj):
    wide = widen(scale)
    high, low = split(state)
    terms = dot(jnp.concatenate([proj, proj], axis=1), jnp.concatenate([high, low], axis=0)) * wide
    left_high, left_low = split(values * wide)
    last = ((1,), (1,))
    both = dot(jnp.concatenate([left_high, left_low], axis=0), high, last)
    tokens = values.shape[0]
    grad = both[:tokens] + (both[tokens:] + dot(left_high, low, last))
    return terms, grad, head_sums(terms * values)


def finish_kernel(
    pay_ref, most_ref, x_ref, w_ref, b_ref, c_ref, tail_ref, reach_ref, y_ref, gx_ref, gb_ref, gc_ref, col_ref, diff_ref, size_ref, sig_ref, edge_ref,
    mixed_out, gradx_out, dt_ref, gradb_out, gradc_out, mixed_ref, gradx_ref, gradb_ref, gradc_ref, sems,
):
    tokens, channels = x_ref.shape
    wide = channels // GROUPS
    rows, cols, met, copies = [], [], [], []
    for g in range(GROUPS):
        mine, own = slice(g * wide, (g + 1) * wide), slice(g * STATE, (g + 1) * STATE)
        enter, enter_scale = state_from(pay_ref, most_ref, g, 0)
        leave, leave_scale = state_from(pay_ref, most_ref, g, 1)
        terms, grad, sums = carried_terms(enter, w_ref[:, mine].astype(F32), reach_ref[g] * enter_scale, c_ref[:, own])
        mixed_ref[:, mine] = (y_ref[:, mine] + terms).astype(BF16)
        gradc_ref[:, own] = (gc_ref[:, own] + grad).astype(BF16)
        rows.append(sums)
        terms, grad, sums = carried_terms(leave, x_ref[:, mine].astype(F32), tail_ref[g] * leave_scale, b_ref[:, own])
        gradx_ref[:, mine] = (gx_ref[:, mine] + terms).astype(BF16)
        gradb_ref[:, own] = (gb_ref[:, own] + grad).astype(BF16)
        cols.append(sums)
        for k, (source, target, here) in enumerate(
            (
                (mixed_ref, mixed_out, mine),
                (gradx_ref, gradx_out, mine),
                (gradb_ref, gradb_out, own),
                (gradc_ref, gradc_out, own),
            )
        ):
            copy = pltpu.make_async_copy(source.at[:, here], target.at[:, here], sems.at[g, k])
            copy.start()
            copies.append(copy)
        both = jnp.sum(enter * leave, axis=0, keepdims=True) * (enter_scale * leave_scale)
        met.append(head_sums(jnp.broadcast_to(both, (8, wide))))

    def whole(parts):
        return jnp.concatenate([parts[k] for k in range(GROUPS)], axis=1)

    edge = whole(edge_ref)
    keep, decay = edge[3:4], edge[4:5]
    shape = (tokens, tokens)
    from_here = (iota(shape, 0) <= iota(shape, 1)).astype(F32)
    before = (iota(shape, 0) > iota(shape, 1)).astype(F32)
    late = whole(cols)
    grad_rate = (
        dot(from_here, whole(diff_ref) + whole(rows), precision=PRECISE)
        + dot(before, late, precision=PRECISE)
        + keep * whole(met)[0:1]
    )
    grad_size = (whole(col_ref) + late) / whole(size_ref) + decay * grad_rate
    dt_ref[...] = (grad_size * whole(sig_ref)).T.astype(BF16)
    for copy in copies:
        copy.wait()


def finish(pay, most, x, w, b, c, tail, reach, y, gx, gb, gc, col, diff, size, sig, edge):
    tokens, channels = x.shape
    heads = channels // HEADDIM
    shapes = [(tokens, channels), (tokens, channels), (heads, tokens), b.shape, b.shape]
    close = pl.BlockSpec(memory_space=pltpu.VMEM)
    far = pl.BlockSpec(memory_space=pl.ANY)
    return pl.pallas_call(
        finish_kernel,
        in_specs=[close] * 17,
        out_specs=[far, far, close, far, far],
        out_shape=[jax.ShapeDtypeStruct(shape, BF16) for shape in shapes],
        scratch_shapes=[pltpu.VMEM(shape, BF16) for shape in (shapes[0], shapes[1], shapes[3], shapes[4])]
        + [pltpu.SemaphoreType.DMA((GROUPS, 4))],
        compiler_params=PARAMS,
        cost_estimate=pl.CostEstimate(flops=20 * tokens * STATE * channels, bytes_accessed=14_000_000, transcendentals=0),
        name="finish",
    )(pay, most, x, w, b, c, tail, reach, y, gx, gb, gc, col, diff, size, sig, edge)


GROUP = ("near", "head")


def exchanged(messages):
    return lax.all_to_all(messages.astype(jnp.float16), GROUP, split_axis=0, concat_axis=0, tiled=True)


def gathered(own, heads):
    parts = lax.axis_size("head")
    per_dev = own.shape[1]
    mine = lax.axis_index("head")
    whole = jnp.where(iota((8, LANES), 1) // per_dev == mine, jnp.tile(own, (1, LANES // per_dev)), 0.0)
    whole = jnp.broadcast_to(whole[None], (parts, 8, LANES))
    return lax.all_to_all(whole, "head", split_axis=0, concat_axis=0, tiled=True).sum(axis=0)[:, :heads]


def per_device(features, dt_raw, b_proj, c_proj, cotangent, starts, a_log, dt_bias, d_skip):
    parts = lax.axis_size(GROUP)
    tokens, heads = dt_raw.shape
    params = gathered(jnp.stack([a_log, dt_bias, d_skip] + [d_skip] * 5), heads)
    marks = lax.dynamic_slice(starts, (lax.axis_index("head") * tokens,), (tokens,)).astype(F32)
    marks = jnp.broadcast_to(marks[None], (8, tokens))
    skip = jnp.broadcast_to(jnp.repeat(params[2], HEADDIM)[None], (8, heads * HEADDIM))
    reach, tail, edge = prep(dt_raw, params, marks, True)
    size, sig, run, runt, bias = prep(dt_raw, params, marks, False)
    near = staged(features, cotangent, b_proj, c_proj)
    came = exchanged(states(*near, tail, reach, edge, parts))
    y, gx, gb, gc, col, diff = inner(features, cotangent, b_proj, c_proj, run, runt, bias, skip)
    count, here = lax.axis_size("far"), lax.axis_index("far")
    mask = [jnp.full((LANES,), here - by >= 0) for by in range(1, count)]
    mask += [jnp.full((LANES,), here + by < count) for by in range(1, count)]
    mask = jnp.stack(mask).astype(F32)
    total = totals(came.astype(F32))
    came, total = lax.optimization_barrier((came, total))
    far = [lax.ppermute(total, "far", [(p, (p + by) % count) for p in range(count)]) for by in range(1, count)]
    left, most = entering(came.astype(F32), total, jnp.stack(far), mask)
    mixed, grad_x, grad_dt, grad_b, grad_c = finish(
        exchanged(left).astype(F32), most, features, cotangent, b_proj, c_proj, tail, reach, y, gx, gb, gc, col, diff, size, sig, edge
    )
    return mixed, grad_x, grad_dt.T, grad_b, grad_c


def solution(mesh):
    near = 8
    devices = mesh.devices
    seq, parts = devices.shape
    fine = jax.sharding.Mesh(devices.reshape(seq // near, near, parts), ("far",) + GROUP)
    token = P(("far",) + GROUP, None)
    return jax.shard_map(
        per_device,
        mesh=fine,
        in_specs=(token, token, token, token, token, P(("far", "near")), P("head"), P("head"), P("head")),
        out_specs=(token, token, token, token, token),
        check_vma=False,
    )
```
